32 devices in a mesh: sector: 8 (over y, x, core), block: 4 (over z).
Axes of the slice: x: 2, y: 2, z: 4, core: 2. Of those that a mesh axis runs over, the one named last changes fastest.
Arguments:
- flow: float32 [5, 4, 64, 1024], P(None, None, 'block', 'sector'), may hold values from -1 to 5, as said below
- adjoint: float32 [5, 4, 64, 1024], P(None, None, 'block', 'sector'), may hold values from -6 to 6
- adjoint_later: float32 [2, 5, 4, 64, 1024], P(None, None, None, 'block', 'sector'), may hold values from -6 to 6
- objective_grad: float32 [5, 4, 64, 1024], P(None, None, 'block', 'sector'), may hold values from -12 to 12
- volume: float32 [4, 64, 1024], P(None, 'block', 'sector'), may hold values from 0.5 to 2
- panel_maps: float32 [4, 4, 128, 128], replicated, may hold values from 0 to 1, as said below
- rotor_step: int32 [1], replicated, may hold values from 0 to 31
Outputs:
- updated_adjoint: float32 [5, 4, 64, 1024], P(None, None, 'block', 'sector')
The draws below stay inside these ranges and needn't reach their ends.
Inputs may be any that keep to these rules, and one draw needn't show every extreme that they name: `flow`: density and pressure are positive in every cell. `panel_maps`: entries are non-negative.
All inputs are finite; a program needn't handle non-finite values.
Results may differ from the reference program's by a relative error of at most 0.000057.
Values sent between devices are 32-bit elements; how exact they have to be, the bound alone decides.
No kernel may reach another device: no remote copies, remote signals or barrier semaphores. Data moves between devices by JAX's collectives and lax.ppermute only.
A program may use at most 64 MiB of HBM per device.

```python
import math
import jax
import jax.numpy as jnp
from jax import lax

LAYERS = 4
CIRC_DEV = 128
PHASES = 4
ITERS = 4
SECTORS = 8
NX = 64
NT = 1024


def draw_flow(key, part):
    keys = jax.random.split(jax.random.fold_in(key, 11), 5)
    shape = (LAYERS, NX, NT)
    density = jax.random.uniform(keys[0], shape, jnp.float32, 0.6, 1.6)
    pressure_field = jax.random.uniform(keys[4], shape, jnp.float32, 0.5, 1.5)
    axial_speed = jax.random.uniform(keys[1], shape, jnp.float32, 0.2, 0.8)
    swirl_speed = jax.random.uniform(keys[2], shape, jnp.float32, -0.5, 0.5)
    radial_speed = jax.random.uniform(keys[3], shape, jnp.float32, -0.2, 0.2)
    energy = pressure_field / 0.4 + 0.5 * density * (axial_speed * axial_speed + swirl_speed * swirl_speed + radial_speed * radial_speed)
    return jnp.stack([density, density * axial_speed, density * swirl_speed, density * radial_speed, energy])


def draw_panel_maps(key, part):
    keys = jax.random.split(jax.random.fold_in(key, 23), 3)
    weight_share = jax.random.uniform(keys[0], (PHASES, 2), jnp.float32, 0.2, 0.8)
    shares = jnp.stack([1.0 - weight_share[:, 0], weight_share[:, 0], 1.0 - weight_share[:, 1], weight_share[:, 1]], axis=1)
    diagonal_part = jax.random.uniform(keys[1], (PHASES, 4, 1, 1), jnp.float32, 0.5, 0.8)
    spread = jax.random.uniform(keys[2], (PHASES, 4, CIRC_DEV, CIRC_DEV), jnp.float32, 0.0, 2.0)
    identity_part = jnp.eye(CIRC_DEV, dtype=jnp.float32)
    return shares[:, :, None, None] * (diagonal_part * identity_part + (1.0 - diagonal_part) * spread / CIRC_DEV)


def block_levels(own_key, dims, pieces, low, top_value):
    factor_of, own = 1.0, jax.random.fold_in(own_key, 6)
    for axis_at, parts in pieces:
        steps = jnp.exp(jax.random.uniform(jax.random.fold_in(own, axis_at), (parts,), jnp.float32, low / len(pieces), top_value / len(pieces)))
        factor_of = factor_of * jnp.repeat(steps, dims[axis_at] // parts).reshape([-1 if axis == axis_at else 1 for axis in range(len(dims))])
    return factor_of


def bell_draw(key, shape, width, reach, cuts=(), held_as=jnp.bfloat16):
    entries = width * jax.random.normal(key, shape, jnp.float32)
    if cuts:
        entries = entries * block_levels(key, shape, cuts, -0.22, 0.18)
    return jnp.clip(entries, -reach, reach).astype(held_as)


def setup_inputs(seed: int = 0) -> dict:
    key_of = jax.random.split(jax.random.key(seed), 8)
    flow = draw_flow(jax.random.fold_in(key_of[7], 71), 0)
    adjoint = bell_draw(key_of[1], (5, LAYERS, NX, NT), 1.0, 6.0, ((2, 4), (3, 8)), jnp.float32)
    adjoint_later = bell_draw(key_of[2], (2, 5, LAYERS, NX, NT), 1.0, 6.0, ((3, 4), (4, 8)), jnp.float32)
    objective_grad = bell_draw(key_of[3], (5, LAYERS, NX, NT), 2.0, 12.0, ((2, 4), (3, 8)), jnp.float32)
    volume = jnp.clip(jnp.exp(math.log(2.0) - 1.3862944 * jax.random.uniform(key_of[4], (LAYERS, NX, NT), jnp.float32) ** block_levels(key_of[4], (LAYERS, NX, NT), ((1, 4), (2, 8)), -0.2, 0.2)), 0.5, 2.0)
    panel_maps = draw_panel_maps(jax.random.fold_in(key_of[7], 71), 0)
    rotor_step = jax.random.randint(key_of[6], (1,), 0, SECTORS * PHASES).astype(jnp.int32)
    return dict(flow=flow, adjoint=adjoint, adjoint_later=adjoint_later, objective_grad=objective_grad, volume=volume, panel_maps=panel_maps, rotor_step=rotor_step)


gamma_gas = 1.4
second_coef = 0.5
fourth_coef = 1.0 / 32.0
courant = 0.6
physical_step = 2.0
sensor_floor = 0.0001
highest = lax.Precision.HIGHEST

def pressure(state):
    density = state[0]
    kinetic = 0.5 * (state[1] * state[1] + state[2] * state[2] + state[3] * state[3]) / density
    return (gamma_gas - 1.0) * (state[4] - kinetic)

def slab(array, start, stop, axis):
    return lax.slice_in_dim(array, start, stop, axis=axis)

def direction_terms(wide, axis, momentum_row):
    density = wide[0]
    pressure_now = pressure(wide)
    speed = wide[momentum_row] / density
    sound_speed = jnp.sqrt(gamma_gas * pressure_now / density)
    radius = jnp.sqrt(speed * speed + 0.01) + sound_speed
    fluxes = [wide[momentum_row], wide[1] * speed, wide[2] * speed, wide[3] * speed, (wide[4] + pressure_now) * speed]
    fluxes[momentum_row] = fluxes[momentum_row] + pressure_now
    flux = jnp.stack(fluxes)
    scalar_axis = axis - 1
    length = pressure_now.shape[scalar_axis]
    upper_p = slab(pressure_now, 2, length, scalar_axis)
    middle_p = slab(pressure_now, 1, length - 1, scalar_axis)
    lower_p = slab(pressure_now, 0, length - 2, scalar_axis)
    bend = upper_p - 2.0 * middle_p + lower_p
    total = upper_p + 2.0 * middle_p + lower_p
    sensor = jnp.sqrt(bend * bend + sensor_floor) / total
    second_damp = second_coef * 0.5 * (slab(sensor, 0, length - 3, scalar_axis) + slab(sensor, 1, length - 2, scalar_axis))
    fourth_damp = fourth_coef * fourth_coef / (fourth_coef + second_damp)
    spectral = 0.5 * (slab(radius, 1, length - 2, scalar_axis) + slab(radius, 2, length - 1, scalar_axis))
    behind = slab(wide, 0, length - 3, axis)
    left_cell = slab(wide, 1, length - 2, axis)
    right_cell = slab(wide, 2, length - 1, axis)
    ahead = slab(wide, 3, length, axis)
    damping = spectral * (second_damp * (right_cell - left_cell) - fourth_damp * (ahead - 3.0 * right_cell + 3.0 * left_cell - behind))
    face = 0.5 * (slab(flux, 1, length - 2, axis) + slab(flux, 2, length - 1, axis)) - damping
    faces = length - 3
    change = slab(face, 1, faces, axis) - slab(face, 0, faces - 1, axis)
    return (change, slab(radius, 2, length - 2, scalar_axis))

def residual_and_radius(padded):
    full = jnp.pad(padded, ((0, 0), (2, 2), (0, 0), (0, 0)), mode='edge')
    axial_change, axial_radius = direction_terms(full[:, 2:-2, :, 2:-2], 2, 1)
    turning_change, turning_radius = direction_terms(full[:, 2:-2, 2:-2, :], 3, 2)
    radial_change, radial_radius = direction_terms(full[:, :, 2:-2, 2:-2], 1, 3)
    return (axial_change + turning_change + radial_change, axial_radius + turning_radius + radial_radius)

def apply_pair(nearer, farther, first_map, second_map):
    return jnp.einsum('...i,ti->...t', nearer, first_map, precision=highest) + jnp.einsum('...i,ti->...t', farther, second_map, precision=highest)

def interpolate(panel, first_map, second_map, near_shift, far_shift):
    sectors = panel.reshape(panel.shape[:-1] + (SECTORS, CIRC_DEV))
    order = jnp.arange(SECTORS, dtype=jnp.int32)
    nearer = jnp.take(sectors, ((order - near_shift) % SECTORS).astype(jnp.int32), axis=-2)
    farther = jnp.take(sectors, ((order - far_shift) % SECTORS).astype(jnp.int32), axis=-2)
    return apply_pair(nearer, farther, first_map, second_map).reshape(panel.shape)

def wrap_sides(column):
    return jnp.concatenate([column[..., -2:], column, column[..., :2]], axis=-1)

def reference(flow, adjoint, adjoint_later, objective_grad, volume, panel_maps, rotor_step):
    turn = rotor_step[0]
    offset = turn // PHASES
    maps = lax.dynamic_index_in_dim(panel_maps, turn % PHASES, 0, keepdims=False)
    half = NX // 2

    def whole_residual(state):
        rotor = state[:, :, :half]
        stator = state[:, :, half:]
        stator_ghost = interpolate(rotor[:, :, -2:], maps[0], maps[1], offset, offset + 1)
        rotor_ghost = interpolate(stator[:, :, :2], maps[2], maps[3], -offset, -offset - 1)
        inlet = jnp.repeat(rotor[:, :, :1], 2, axis=2)
        outlet = jnp.repeat(stator[:, :, -1:], 2, axis=2)
        rotor_change, rotor_radius = residual_and_radius(wrap_sides(jnp.concatenate([inlet, rotor, rotor_ghost], axis=2)))
        stator_change, stator_radius = residual_and_radius(wrap_sides(jnp.concatenate([stator_ghost, stator, outlet], axis=2)))
        return (jnp.concatenate([rotor_change, stator_change], axis=2), jnp.concatenate([rotor_radius, stator_radius], axis=1))
    change, pullback, radius_sum = jax.vjp(whole_residual, flow, has_aux=True)
    factor = courant / (radius_sum + 1.5 * courant * volume / physical_step)
    source = objective_grad + volume * (2.0 * adjoint_later[0] - 0.5 * adjoint_later[1]) / physical_step
    current = adjoint
    for sweep in range(ITERS):
        transposed, = pullback(current)
        current = current - factor * (1.5 * volume * current / physical_step + transposed - source)
    return current
```

```python
from functools import partial

import jax
import jax.numpy as jnp
from jax import lax
from jax.experimental import pallas as pl
from jax.experimental.pallas import tpu as pltpu
from jax.sharding import PartitionSpec as P

PHASES = 4
ITERS = 4
LANES = 128
ROWS = 16
LAYERS = 4
FIELDS = 5
SEG = LANES // LAYERS

gamma_gas = 1.4
second_coef = 0.5
fourth_coef = 1.0 / 32.0
courant = 0.6
physical_step = 2.0
sensor_floor = 0.0001
highest = lax.Precision.HIGHEST

S_EVEN, B_EVEN, INLET, OUTLET, LOWER_PLANE, UPPER_PLANE = range(6)
U1, U2, U3, HT, BX, BT, BL, CR, CP, EK = range(10)
CELLS = 10
A2, A4, DL, ES, N0, N1 = 0, 1, 2, 7, 12, 13
FACES = 14


def up_by(x, axis, k):
    n = x.shape[axis]
    return pltpu.roll(x, (-k) % n, axis=axis)


def iota(shape, axis):
    return lax.broadcasted_iota(jnp.int32, shape, axis)


def flagged(flags, which, shape):
    return jnp.broadcast_to(flags[which], shape) == 1


def primitives(u):
    inverse = 1.0 / u[0]
    vel = [u[1] * inverse, u[2] * inverse, u[3] * inverse]
    square = vel[0] * vel[0] + vel[1] * vel[1] + vel[2] * vel[2]
    p = (gamma_gas - 1.0) * (u[4] - 0.5 * u[0] * square)
    sound = jnp.sqrt(gamma_gas * p * inverse)
    roots = [jnp.sqrt(q * q + 0.01) for q in vel]
    return inverse, vel, square, p, sound, roots


def cell_coefficients(u, prim):
    inverse, vel, square, p, sound, roots = prim
    return (
        vel
        + [(u[4] + p) * inverse]
        + [q / r * inverse for q, r in zip(vel, roots)]
        + [0.5 * sound * inverse, 0.5 * sound / p, (0.5 * (gamma_gas - 1.0)) * square]
    )


def sensor_terms(below, here, above):
    bend = above - 2.0 * here + below
    total = above + 2.0 * here + below
    root = jnp.sqrt(bend * bend + sensor_floor)
    over = 1.0 / total
    nu = root * over
    a = bend / root * over
    b = nu * over
    return nu, -2.0 * a - 2.0 * b, a - b


def face_terms(nu_left, nu_right, rad_left, rad_right, behind, left, right, ahead):
    e2 = (0.5 * second_coef) * (nu_left + nu_right)
    ratio = fourth_coef / (fourth_coef + e2)
    e4 = fourth_coef * ratio
    slope = ratio * ratio
    lam = 0.5 * (rad_left + rad_right)
    radial, sensed = [], []
    for b, l, r, a in zip(behind, left, right, ahead):
        first = r - l
        third = a - 3.0 * first - b
        radial.append(-0.5 * (e2 * first - e4 * third))
        sensed.append((-0.25) * lam * (first + slope * third))
    return [lam * e2, lam * e4] + radial + sensed


def rolled_faces(u, prim, direction, axis):
    _, _, _, p, sound, roots = prim
    nu, n0, n1 = sensor_terms(up_by(p, axis, -1), p, up_by(p, axis, 1))
    radius = roots[direction] + sound
    right = [up_by(x, axis, 1) for x in u]
    behind = [up_by(x, axis, -1) for x in u]
    ahead = [up_by(x, axis, 2) for x in u]
    return face_terms(
        nu, up_by(nu, axis, 1), radius, up_by(radius, axis, 1), behind, u, right, ahead
    ) + [n0, n1]


def dot5(a, b):
    return (a[0] * b[0] + a[1] * b[1]) + (a[2] * b[2] + a[3] * b[3]) + a[4] * b[4]


def to_state(lin, s, rbar, nbar, cells, direction):
    q = cells[direction]
    kappa = s[1] * cells[U1] + s[2] * cells[U2] + s[3] * cells[U3] + s[4] * cells[HT]
    kappa = kappa + cells[BX + direction] * rbar
    sq = s[4] * q
    pbar = nbar + sq + s[direction + 1] + cells[CP] * rbar
    scaled = (gamma_gas - 1.0) * pbar
    g = [None] * FIELDS
    g[0] = lin[0] - q * kappa - cells[CR] * rbar + cells[EK] * pbar
    for k in range(3):
        g[k + 1] = lin[k + 1] + q * s[k + 1] - cells[k] * scaled
    g[direction + 1] = g[direction + 1] + (s[0] + kappa)
    g[4] = lin[4] + sq + scaled
    return g


def rolled_transpose(psi, faces, cells, direction, axis, mask=None):
    w = [x - up_by(x, axis, 1) for x in psi]
    if mask is not None:
        w = [jnp.where(mask, x, 0.0) for x in w]
    gl = dot5(w, [faces(DL + k) for k in range(FIELDS)])
    ge = dot5(w, [faces(ES + k) for k in range(FIELDS)])
    a2, a4 = faces(A2), faces(A4)
    lin, s = [], []
    for x in w:
        c = a4 * x
        z = a2 * x + 2.0 * c - up_by(c, axis, 1) - up_by(c, axis, -1)
        lin.append(z - up_by(z, axis, -1))
        s.append(0.5 * (x + up_by(x, axis, -1)))
    rbar = gl + up_by(gl, axis, -1)
    nu_bar = ge + up_by(ge, axis, -1)
    v = faces(N1) * nu_bar
    nbar = faces(N0) * nu_bar + up_by(v, axis, 1) + up_by(v, axis, -1)
    return to_state(lin, s, rbar, nbar, cells, direction)


def packed_rows(tiles):
    row = iota((8, LANES), 0)
    out = tiles[0]
    for l in range(1, LAYERS):
        out = jnp.where(row >= 2 * l, pltpu.roll(tiles[l], 2 * l, axis=0), out)
    return out


def packed_strip(layers):
    lane = iota((ROWS, LANES), 1)
    out = jnp.zeros((ROWS, LANES), jnp.float32)
    for l, x in enumerate(layers):
        base = SEG * l
        out = jnp.where((lane >= base) & (lane < base + 8), pltpu.roll(x, (base + 8) % LANES, axis=1), out)
        out = jnp.where(
            (lane >= base + 24) & (lane < base + 32), pltpu.roll(x, (base + 24) % LANES, axis=1), out
        )
    return out


def from_strip(strip, l):
    lane = iota((ROWS, LANES), 1)
    base = SEG * l
    low = pltpu.roll(strip, (-(base + 24)) % LANES, axis=1)
    high = pltpu.roll(strip, (-(base + 8)) % LANES, axis=1)
    return jnp.where(lane < 8, low, jnp.where(lane >= LANES - 8, high, 0.0))


def place_in_segment():
    return jnp.bitwise_and(iota((ROWS, LANES), 1), SEG - 1)


def pack_kernel(flags, flow, strip, to_a, to_b):
    even = flagged(flags, B_EVEN, (8, LANES))
    for k in range(FIELDS):
        strip[k] = packed_strip([flow[k, l] for l in range(LAYERS)])
        lower = [flow[k, l, 0:8] for l in range(LAYERS)]
        upper = [pltpu.roll(flow[k, l, 8:16], 2, axis=0) for l in range(LAYERS)]
        low, high = packed_rows(lower), packed_rows(upper)
        to_a[k] = jnp.where(even, high, low)
        to_b[k] = jnp.where(even, low, high)


def mapped(near, far, maps, transposed):
    dims = (((1,), (0,)), ((), ())) if transposed else (((1,), (1,)), ((), ()))
    near = near[...].reshape(FIELDS * 8, LANES)
    far = far[...].reshape(FIELDS * 8, LANES)
    out = lax.dot_general(near, maps[0], dims, precision=highest, preferred_element_type=jnp.float32)
    out = out + lax.dot_general(far, maps[1], dims, precision=highest, preferred_element_type=jnp.float32)
    return out.reshape(FIELDS, 8, LANES)


def lower_and_upper(flags, from_a, near, through):
    even = flagged(flags, B_EVEN, (8, LANES))
    plane = flagged(flags, LOWER_PLANE, (8, LANES)) | flagged(flags, UPPER_PLANE, (8, LANES))
    lower, upper = [], []
    for k in range(FIELDS):
        b = jnp.where(plane, through[k], near[k])
        a = from_a[k]
        lower.append(jnp.where(even, b, a))
        upper.append(jnp.where(even, a, b))
    return lower, upper


def left_and_right(flags, from_a, from_b, k):
    even = flagged(flags, S_EVEN, (ROWS, LANES))
    a, b = from_a[k], from_b[k]
    return jnp.where(even, b, a), jnp.where(even, a, b)


def coefficients(flags, flow, own, from_a, from_b, zone_a, near, far, maps, cm, ch, cs, xf, tf, lf, ln):
    through = mapped(near, far, maps, False)
    lower, upper = lower_and_upper(flags, zone_a, near, through)
    row = iota((8, LANES), 0)
    inlet = flagged(flags, INLET, (8, LANES))
    outlet = flagged(flags, OUTLET, (8, LANES))
    for l in range(LAYERS):
        u = []
        for k in range(FIELDS):
            main = flow[k, l]
            up = pltpu.roll(upper[k], (-2 * l) % 8, axis=0)
            low = pltpu.roll(lower[k], (6 - 2 * l) % 8, axis=0)
            up = jnp.where(outlet, jnp.broadcast_to(main[15:16], (8, LANES)), up)
            low = jnp.where(inlet, jnp.broadcast_to(main[0:1], (8, LANES)), low)
            halo = jnp.where(
                row < 2,
                up,
                jnp.where(
                    row < 4,
                    pltpu.roll(up, 2, axis=0),
                    jnp.where(row < 6, pltpu.roll(low, 6, axis=0), low),
                ),
            )
            u.append(jnp.concatenate([main, halo], axis=0))
        prim = primitives(u)
        for i, x in enumerate(cell_coefficients(u, prim)):
            cm[i, l] = x[:16]
            ch[i, l] = x[16:]
        for i, x in enumerate(rolled_faces(u, prim, 0, 0)):
            xf[i, l] = x
    sub = place_in_segment()
    for slot in range(LAYERS + 1):
        if slot < LAYERS:
            u = [flow[k, slot] for k in range(FIELDS)]
        else:
            u = []
            for k in range(FIELDS):
                left, right = left_and_right(flags, from_a, from_b, k)
                x = jnp.where((sub >= 8) & (sub < 16), pltpu.roll(right, LANES - 16, axis=1), own[k])
                u.append(jnp.where((sub >= 16) & (sub < 24), pltpu.roll(left, 16, axis=1), x))
        prim = primitives(u)
        if slot == LAYERS:
            for i, x in enumerate(cell_coefficients(u, prim)):
                cs[i] = x
        for i, x in enumerate(rolled_faces(u, prim, 1, 1)):
            tf[i, slot] = x
    for half in range(2):
        rows = slice(8 * half, 8 * half + 8)
        cell = [[flow[k, l, rows] for k in range(FIELDS)] for l in range(LAYERS)]
        prims = [primitives(u) for u in cell]
        clamp = lambda j: min(max(j, 0), LAYERS - 1)
        nus = {}
        for j in range(-1, LAYERS + 1):
            nu, n0, n1 = sensor_terms(*[prims[clamp(j + d)][3] for d in (-1, 0, 1)])
            nus[j] = nu
            ln[0, j + 1, rows] = n0
            ln[1, j + 1, rows] = n1
        radius = [pr[5][2] + pr[4] for pr in prims]
        for f in range(-1, LAYERS):
            terms = face_terms(
                nus[f],
                nus[f + 1],
                radius[clamp(f)],
                radius[clamp(f + 1)],
                *[cell[clamp(f + d)] for d in (-1, 0, 1, 2)],
            )
            for i, x in enumerate(terms):
                lf[i, f + 1, rows] = x


def transposed_terms(flags, psi, coefs, acc, strip, to_a, to_b, ghost):
    cm, ch, cs, xf, tf, lf, ln = coefs
    row = iota((8, LANES), 0)
    inlet = flagged(flags, INLET, (8, LANES))
    outlet = flagged(flags, OUTLET, (8, LANES))
    even = flagged(flags, B_EVEN, (8, LANES))
    empty = jnp.zeros((8, LANES), jnp.float32)
    for l in range(LAYERS):
        wide = [jnp.concatenate([psi[k, l], empty], axis=0) for k in range(FIELDS)]
        cells = [jnp.concatenate([cm[i, l], ch[i, l]], axis=0) for i in range(CELLS)]
        g = rolled_transpose(wide, lambda i: xf[i, l], cells, 0, 0)
        for k in range(FIELDS):
            out = g[k][16:]
            ghost[k, l] = out
            first = pltpu.roll(out, 2, axis=0) + pltpu.roll(out, 1, axis=0)
            last = pltpu.roll(out, 7, axis=0) + pltpu.roll(out, 6, axis=0)
            acc[k, l, 0:8] = g[k][0:8] + jnp.where(inlet & (row == 0), first, 0.0)
            acc[k, l, 8:16] = g[k][8:16] + jnp.where(outlet & (row == 7), last, 0.0)
    for k in range(FIELDS):
        high = packed_rows([ghost[k, l] for l in range(LAYERS)])
        low = packed_rows([pltpu.roll(ghost[k, l], 2, axis=0) for l in range(LAYERS)])
        to_a[k] = jnp.where(even, high, low)
        to_b[k] = jnp.where(even, low, high)
    lane = iota((ROWS, LANES), 1)
    sub = place_in_segment()
    inner = (lane >= 1) & (lane < LANES - 2)
    edges = ((sub >= 6) & (sub < 8)) | ((sub >= 23) & (sub < 25))
    for slot in range(LAYERS + 1):
        if slot < LAYERS:
            values = [psi[k, slot] for k in range(FIELDS)]
            cells = [cm[i, slot] for i in range(CELLS)]
            mask = inner
        else:
            values = [packed_strip([psi[k, l] for l in range(LAYERS)]) for k in range(FIELDS)]
            cells = [cs[i] for i in range(CELLS)]
            mask = edges
        g = rolled_transpose(values, lambda i: tf[i, slot], cells, 1, 1, mask)
        for k in range(FIELDS):
            if slot < LAYERS:
                acc[k, slot] = acc[k, slot] + g[k]
            else:
                strip[k] = g[k]
    last = LAYERS - 1
    for half in range(2):
        rows = slice(8 * half, 8 * half + 8)
        value = [[psi[k, l, rows] for k in range(FIELDS)] for l in range(LAYERS)]
        w, c, gl, ge = {}, {}, {}, {}
        for f in range(-1, LAYERS):
            if f < 0:
                w[f] = [-x for x in value[0]]
            elif f == last:
                w[f] = value[last]
            else:
                w[f] = [x - y for x, y in zip(value[f], value[f + 1])]
            face = lambda i: lf[i, f + 1, rows]
            gl[f] = dot5(w[f], [face(DL + k) for k in range(FIELDS)])
            ge[f] = dot5(w[f], [face(ES + k) for k in range(FIELDS)])
            c[f] = [face(A4) * x for x in w[f]]
        z = {}
        for f in range(last):
            a2 = lf[A2, f + 1, rows]
            z[f] = [a2 * w[f][k] + 2.0 * c[f][k] - c[f + 1][k] - c[f - 1][k] for k in range(FIELDS)]
        nbar = [None] * LAYERS
        for j in range(-1, LAYERS + 1):
            nu_bar = ge.get(j, 0.0) + ge.get(j - 1, 0.0)
            here = ln[0, j + 1, rows] * nu_bar
            side = ln[1, j + 1, rows] * nu_bar
            for to, x in ((j, here), (j - 1, side), (j + 1, side)):
                to = min(max(to, 0), last)
                nbar[to] = x if nbar[to] is None else nbar[to] + x
        for j in range(LAYERS):
            if j == 0:
                s = [0.5 * w[0][k] + w[-1][k] for k in range(FIELDS)]
                lin = z[0]
                rbar = gl[0] + 2.0 * gl[-1]
            elif j == last:
                s = [0.5 * w[last - 1][k] + w[last][k] for k in range(FIELDS)]
                lin = [-x for x in z[last - 1]]
                rbar = gl[last - 1] + 2.0 * gl[last]
            else:
                s = [0.5 * (w[j][k] + w[j - 1][k]) for k in range(FIELDS)]
                lin = [z[j][k] - z[j - 1][k] for k in range(FIELDS)]
                rbar = gl[j] + gl[j - 1]
            g = to_state(lin, s, rbar, nbar[j], [cm[i, j, rows] for i in range(CELLS)], 2)
            for k in range(FIELDS):
                acc[k, j, rows] = acc[k, j, rows] + g[k]


def start_kernel(
    flags, flow, own, from_a, from_b, zone_a, near, far, maps, adjoint, later, gradient, volume,
    keep, factor, pushed, acc, strip, to_a, to_b, cm, ch, cs, xf, tf, lf, ln, ghost,
):
    coefficients(
        flags, flow, own, from_a, from_b, zone_a, near, far, maps, cm, ch, cs, xf, tf, lf, ln
    )
    for l in range(LAYERS):
        u = [flow[k, l] for k in range(FIELDS)]
        _, _, _, _, sound, roots = primitives(u)
        vol = volume[l]
        radius_sum = roots[0] + roots[1] + roots[2] + 3.0 * sound
        f = courant / (radius_sum + (1.5 * courant / physical_step) * vol)
        factor[l] = f
        keep[l] = 1.0 - f * ((1.5 / physical_step) * vol)
        for k in range(FIELDS):
            source = gradient[k, l] + vol * (2.0 * later[0, k, l] - 0.5 * later[1, k, l]) / physical_step
            pushed[k, l] = f * source
    transposed_terms(flags, adjoint, (cm, ch, cs, xf, tf, lf, ln), acc, strip, to_a, to_b, ghost)


def advance(flags, psi, acc, strip, from_a, from_b, zone_a, near, far, maps, keep, factor, pushed, out):
    through = mapped(near, far, maps, True)
    lower, upper = lower_and_upper(flags, zone_a, near, through)
    row = iota((8, LANES), 0)
    lane = iota((ROWS, LANES), 1)
    sub = place_in_segment()
    for k in range(FIELDS):
        left, right = left_and_right(flags, from_a, from_b, k)
        whole = strip[k]
        whole = whole + jnp.where(sub >= 24, pltpu.roll(left, 16, axis=1), 0.0)
        whole = whole + jnp.where(sub < 8, pltpu.roll(right, LANES - 16, axis=1), 0.0)
        for l in range(LAYERS):
            low = jnp.where(row < 2, pltpu.roll(lower[k], (-2 * l) % 8, axis=0), 0.0)
            high = jnp.where(row >= 6, pltpu.roll(upper[k], (6 - 2 * l) % 8, axis=0), 0.0)
            total = acc[k, l] + from_strip(whole, l) + jnp.concatenate([low, high], axis=0)
            out[k, l] = psi[k, l] * keep[l] - factor[l] * total + pushed[k, l]


def step_kernel(
    flags, psi, acc, strip, from_a, from_b, zone_a, near, far, maps, keep, factor, pushed,
    cm, ch, cs, xf, tf, lf, ln, out, acc_out, strip_out, to_a, to_b, ghost,
):
    advance(flags, psi, acc, strip, from_a, from_b, zone_a, near, far, maps, keep, factor, pushed, out)
    transposed_terms(flags, out, (cm, ch, cs, xf, tf, lf, ln), acc_out, strip_out, to_a, to_b, ghost)


def last_kernel(flags, psi, acc, strip, from_a, from_b, zone_a, near, far, maps, keep, factor, pushed, out):
    advance(flags, psi, acc, strip, from_a, from_b, zone_a, near, far, maps, keep, factor, pushed, out)


def f32(*shape):
    return jax.ShapeDtypeStruct(shape, jnp.float32)


STATE = (FIELDS, LAYERS, ROWS, LANES)
STRIP = (FIELDS, ROWS, LANES)
PANEL = (FIELDS, 8, LANES)
SCALAR = (LAYERS, ROWS, LANES)
TERMS = (f32(*STATE), f32(*STRIP), f32(*PANEL), f32(*PANEL))
COEFS = (
    f32(CELLS, *SCALAR),
    f32(CELLS, LAYERS, 8, LANES),
    f32(CELLS, ROWS, LANES),
    f32(FACES, LAYERS, ROWS + 8, LANES),
    f32(FACES, LAYERS + 1, ROWS, LANES),
    f32(12, LAYERS + 1, ROWS, LANES),
    f32(2, LAYERS + 2, ROWS, LANES),
)


def call(kernel, outs, args, ghost=False, name=None):
    vmem = pl.BlockSpec(memory_space=pltpu.VMEM)
    smem = pl.BlockSpec(memory_space=pltpu.SMEM)
    return pl.pallas_call(
        kernel,
        out_shape=outs,
        in_specs=[smem] + [vmem] * (len(args) - 1),
        out_specs=[vmem] * len(outs) if isinstance(outs, tuple) else vmem,
        scratch_shapes=[pltpu.VMEM((FIELDS, LAYERS, 8, LANES), jnp.float32)] if ghost else [],
        compiler_params=pltpu.CompilerParams(vmem_limit_bytes=32 * 1024 * 1024),
        name=name,
    )(*args)


def swaps(names, sectors, blocks, turn):
    half = blocks // 2
    assert half % 2 == 0
    where = {"sector": sectors, "block": blocks}
    minor = where[names[1]]

    def flat(b, s):
        first, second = (s, b) if names[0] == "sector" else (b, s)
        return first * minor + second

    sector_a, sector_b, block_a, near, far = [], [], [], [], []
    for b in range(blocks):
        for s in range(sectors):
            me = flat(b, s)
            sector_a.append((me, flat(b, s ^ 1)))
            sector_b.append((me, flat(b, (s + (1 if s % 2 else -1)) % sectors)))
            block_a.append((me, flat(b ^ 1, s)))
            if b == half - 1:
                near.append((me, flat(half, (s + turn) % sectors)))
                far.append((me, flat(half, (s + turn + 1) % sectors)))
            elif b == half:
                near.append((me, flat(half - 1, (s - turn) % sectors)))
                far.append((me, flat(half - 1, (s - turn - 1) % sectors)))
            elif b % 2 and b + 1 < blocks:
                near.append((me, flat(b + 1, s)))
            elif b % 2 == 0 and b > 0:
                near.append((me, flat(b - 1, s)))
    return sector_a, sector_b, block_a, near, far


def exchange(names, partners, strip, to_a, to_b):
    sector_a, sector_b, block_a, near, far = partners
    move = lambda x, pairs: lax.ppermute(x, names, pairs)
    return (
        move(strip, sector_a),
        move(strip, sector_b),
        move(to_a, block_a),
        move(to_b, near),
        move(to_b, far),
    )


def shards(flow, adjoint, adjoint_later, objective_grad, volume, panel_maps, rotor_step, names):
    blocks = lax.axis_size("block")
    sectors = lax.axis_size("sector")
    place = lax.axis_index("block")
    half = blocks // 2
    stator = place >= half
    turn = rotor_step[0]
    offset = (turn // PHASES) % sectors
    maps = lax.dynamic_index_in_dim(panel_maps, turn % PHASES, 0, keepdims=False)
    state_maps = jnp.where(stator, maps[:2], maps[2:])
    grad_maps = jnp.where(stator, maps[2:], maps[:2])
    flags = jnp.stack(
        [
            lax.axis_index("sector") % 2 == 0,
            place % 2 == 0,
            place == 0,
            place == blocks - 1,
            place == half,
            place == half - 1,
            place < 0,
            place < 0,
        ]
    ).astype(jnp.int32)
    packed = call(pack_kernel, (f32(*STRIP), f32(*PANEL), f32(*PANEL)), (flags, flow), name="pack")

    def branch(shift):
        partners = swaps(names, sectors, blocks, shift)

        def run(packed):
            arrived = exchange(names, partners, *packed)
            out = call(
                start_kernel,
                (f32(*SCALAR), f32(*SCALAR), f32(*STATE)) + TERMS + COEFS,
                (flags, flow, packed[0])
                + arrived
                + (state_maps, adjoint, adjoint_later, objective_grad, volume),
                ghost=True,
                name="start",
            )
            update, terms, coefs = tuple(out[:3]), tuple(out[3:7]), tuple(out[7:])
            current = adjoint
            for sweep in range(ITERS):
                arrived = exchange(names, partners, *terms[1:])
                args = (flags, current) + terms[:2] + arrived + (grad_maps,) + update
                if sweep == ITERS - 1:
                    return call(last_kernel, f32(*STATE), args, name="last")
                out = call(
                    step_kernel, (f32(*STATE),) + TERMS, args + coefs, ghost=True, name="step"
                )
                current, terms = out[0], tuple(out[1:])

        return run

    return lax.switch(offset, [branch(shift) for shift in range(sectors)], tuple(packed))


def solution(mesh):
    placed = (
        P(None, None, "block", "sector"),
        P(None, None, "block", "sector"),
        P(None, None, None, "block", "sector"),
        P(None, None, "block", "sector"),
        P(None, "block", "sector"),
        P(),
        P(),
    )
    return jax.shard_map(
        partial(shards, names=tuple(mesh.axis_names)),
        mesh=mesh,
        in_specs=placed,
        out_specs=P(None, None, "block", "sector"),
        check_vma=False,
    )
```

```python
from functools import partial

import jax
import jax.numpy as jnp
from jax import lax
from jax.experimental import pallas as pl
from jax.experimental.pallas import tpu as pltpu
from jax.sharding import PartitionSpec as P

PHASES = 4
ITERS = 4
LANES = 128
ROWS = 16
LAYERS = 4
FIELDS = 5
SEG = LANES // LAYERS

gamma_gas = 1.4
second_coef = 0.5
fourth_coef = 1.0 / 32.0
courant = 0.6
physical_step = 2.0
sensor_floor = 0.0001
highest = lax.Precision.HIGHEST

S_EVEN, B_EVEN, INLET, OUTLET, LOWER_PLANE, UPPER_PLANE = range(6)
U1, U2, U3, HT, BX, BT, BL, CR, CP, EK = range(10)
CELLS = 10
A2, A4, DL, ES, N0, N1 = 0, 1, 2, 7, 12, 13
FACES = 14


def up_by(x, axis, k):
    n = x.shape[axis]
    return pltpu.roll(x, (-k) % n, axis=axis)


def iota(shape, axis):
    return lax.broadcasted_iota(jnp.int32, shape, axis)


def flagged(flags, which, shape):
    return jnp.broadcast_to(flags[which], shape) == 1


def primitives(u):
    inverse = 1.0 / u[0]
    vel = [u[1] * inverse, u[2] * inverse, u[3] * inverse]
    square = vel[0] * vel[0] + vel[1] * vel[1] + vel[2] * vel[2]
    p = (gamma_gas - 1.0) * (u[4] - 0.5 * u[0] * square)
    sound = jnp.sqrt(gamma_gas * p * inverse)
    roots = [jnp.sqrt(q * q + 0.01) for q in vel]
    return inverse, vel, square, p, sound, roots


def cell_coefficients(u, prim):
    inverse, vel, square, p, sound, roots = prim
    return (
        vel
        + [(u[4] + p) * inverse]
        + [q / r * inverse for q, r in zip(vel, roots)]
        + [0.5 * sound * inverse, 0.5 * sound / p, (0.5 * (gamma_gas - 1.0)) * square]
    )


def sensor_terms(below, here, above):
    bend = above - 2.0 * here + below
    total = above + 2.0 * here + below
    root = jnp.sqrt(bend * bend + sensor_floor)
    over = 1.0 / total
    nu = root * over
    a = bend / root * over
    b = nu * over
    return nu, -2.0 * a - 2.0 * b, a - b


def face_terms(nu_left, nu_right, rad_left, rad_right, behind, left, right, ahead):
    e2 = (0.5 * second_coef) * (nu_left + nu_right)
    ratio = fourth_coef / (fourth_coef + e2)
    e4 = fourth_coef * ratio
    slope = ratio * ratio
    lam = 0.5 * (rad_left + rad_right)
    radial, sensed = [], []
    for b, l, r, a in zip(behind, left, right, ahead):
        first = r - l
        third = a - 3.0 * first - b
        radial.append(-0.5 * (e2 * first - e4 * third))
        sensed.append((-0.25) * lam * (first + slope * third))
    return [lam * e2, lam * e4] + radial + sensed


def rolled_faces(u, prim, direction, axis):
    _, _, _, p, sound, roots = prim
    nu, n0, n1 = sensor_terms(up_by(p, axis, -1), p, up_by(p, axis, 1))
    radius = roots[direction] + sound
    right = [up_by(x, axis, 1) for x in u]
    behind = [up_by(x, axis, -1) for x in u]
    ahead = [up_by(x, axis, 2) for x in u]
    return face_terms(
        nu, up_by(nu, axis, 1), radius, up_by(radius, axis, 1), behind, u, right, ahead
    ) + [n0, n1]


def dot5(a, b):
    return (a[0] * b[0] + a[1] * b[1]) + (a[2] * b[2] + a[3] * b[3]) + a[4] * b[4]


def to_state(lin, s, rbar, nbar, cells, direction):
    q = cells[direction]
    kappa = s[1] * cells[U1] + s[2] * cells[U2] + s[3] * cells[U3] + s[4] * cells[HT]
    kappa = kappa + cells[BX + direction] * rbar
    sq = s[4] * q
    pbar = nbar + sq + s[direction + 1] + cells[CP] * rbar
    scaled = (gamma_gas - 1.0) * pbar
    g = [None] * FIELDS
    g[0] = lin[0] - q * kappa - cells[CR] * rbar + cells[EK] * pbar
    for k in range(3):
        g[k + 1] = lin[k + 1] + q * s[k + 1] - cells[k] * scaled
    g[direction + 1] = g[direction + 1] + (s[0] + kappa)
    g[4] = lin[4] + sq + scaled
    return g


def rolled_transpose(psi, faces, cells, direction, axis, mask=None):
    w = [x - up_by(x, axis, 1) for x in psi]
    if mask is not None:
        w = [jnp.where(mask, x, 0.0) for x in w]
    gl = dot5(w, [faces(DL + k) for k in range(FIELDS)])
    ge = dot5(w, [faces(ES + k) for k in range(FIELDS)])
    a2, a4 = faces(A2), faces(A4)
    lin, s = [], []
    for x in w:
        c = a4 * x
        z = a2 * x + 2.0 * c - up_by(c, axis, 1) - up_by(c, axis, -1)
        lin.append(z - up_by(z, axis, -1))
        s.append(0.5 * (x + up_by(x, axis, -1)))
    rbar = gl + up_by(gl, axis, -1)
    nu_bar = ge + up_by(ge, axis, -1)
    v = faces(N1) * nu_bar
    nbar = faces(N0) * nu_bar + up_by(v, axis, 1) + up_by(v, axis, -1)
    return to_state(lin, s, rbar, nbar, cells, direction)


def packed_rows(tiles):
    row = iota((8, LANES), 0)
    out = tiles[0]
    for l in range(1, LAYERS):
        out = jnp.where(row >= 2 * l, pltpu.roll(tiles[l], 2 * l, axis=0), out)
    return out


def packed_strip(layers):
    lane = iota((ROWS, LANES), 1)
    out = jnp.zeros((ROWS, LANES), jnp.float32)
    for l, x in enumerate(layers):
        base = SEG * l
        out = jnp.where((lane >= base) & (lane < base + 8), pltpu.roll(x, (base + 8) % LANES, axis=1), out)
        out = jnp.where(
            (lane >= base + 24) & (lane < base + 32), pltpu.roll(x, (base + 24) % LANES, axis=1), out
        )
    return out


def from_strip(strip, l):
    lane = iota((ROWS, LANES), 1)
    base = SEG * l
    low = pltpu.roll(strip, (-(base + 24)) % LANES, axis=1)
    high = pltpu.roll(strip, (-(base + 8)) % LANES, axis=1)
    return jnp.where(lane < 8, low, jnp.where(lane >= LANES - 8, high, 0.0))


def place_in_segment():
    return jnp.bitwise_and(iota((ROWS, LANES), 1), SEG - 1)


def pack_kernel(flags, flow, strip, to_a, to_b):
    even = flagged(flags, B_EVEN, (8, LANES))
    for k in range(FIELDS):
        strip[k] = packed_strip([flow[k, l] for l in range(LAYERS)])
        lower = [flow[k, l, 0:8] for l in range(LAYERS)]
        upper = [pltpu.roll(flow[k, l, 8:16], 2, axis=0) for l in range(LAYERS)]
        low, high = packed_rows(lower), packed_rows(upper)
        to_a[k] = jnp.where(even, high, low)
        to_b[k] = jnp.where(even, low, high)


def mapped(near, far, maps, transposed):
    dims = (((1,), (0,)), ((), ())) if transposed else (((1,), (1,)), ((), ()))
    near = near[...].reshape(FIELDS * 8, LANES)
    far = far[...].reshape(FIELDS * 8, LANES)
    out = lax.dot_general(near, maps[0], dims, precision=highest, preferred_element_type=jnp.float32)
    out = out + lax.dot_general(far, maps[1], dims, precision=highest, preferred_element_type=jnp.float32)
    return out.reshape(FIELDS, 8, LANES)


def lower_and_upper(flags, from_a, near, through):
    even = flagged(flags, B_EVEN, (8, LANES))
    plane = flagged(flags, LOWER_PLANE, (8, LANES)) | flagged(flags, UPPER_PLANE, (8, LANES))
    lower, upper = [], []
    for k in range(FIELDS):
        b = jnp.where(plane, through[k], near[k])
        a = from_a[k]
        lower.append(jnp.where(even, b, a))
        upper.append(jnp.where(even, a, b))
    return lower, upper


def left_and_right(flags, from_a, from_b, k):
    even = flagged(flags, S_EVEN, (ROWS, LANES))
    a, b = from_a[k], from_b[k]
    return jnp.where(even, b, a), jnp.where(even, a, b)


def coefficients(flags, flow, own, from_a, from_b, zone_a, near, far, maps, cm, ch, cs, xf, tf, lf, ln):
    through = mapped(near, far, maps, False)
    lower, upper = lower_and_upper(flags, zone_a, near, through)
    row = iota((8, LANES), 0)
    inlet = flagged(flags, INLET, (8, LANES))
    outlet = flagged(flags, OUTLET, (8, LANES))
    for l in range(LAYERS):
        u = []
        for k in range(FIELDS):
            main = flow[k, l]
            up = pltpu.roll(upper[k], (-2 * l) % 8, axis=0)
            low = pltpu.roll(lower[k], (6 - 2 * l) % 8, axis=0)
            up = jnp.where(outlet, jnp.broadcast_to(main[15:16], (8, LANES)), up)
            low = jnp.where(inlet, jnp.broadcast_to(main[0:1], (8, LANES)), low)
            halo = jnp.where(
                row < 2,
                up,
                jnp.where(
                    row < 4,
                    pltpu.roll(up, 2, axis=0),
                    jnp.where(row < 6, pltpu.roll(low, 6, axis=0), low),
                ),
            )
            u.append(jnp.concatenate([main, halo], axis=0))
        prim = primitives(u)
        for i, x in enumerate(cell_coefficients(u, prim)):
            cm[i, l] = x[:16]
            ch[i, l] = x[16:]
        for i, x in enumerate(rolled_faces(u, prim, 0, 0)):
            xf[i, l] = x
    sub = place_in_segment()
    for slot in range(LAYERS + 1):
        if slot < LAYERS:
            u = [flow[k, slot] for k in range(FIELDS)]
        else:
            u = []
            for k in range(FIELDS):
                left, right = left_and_right(flags, from_a, from_b, k)
                x = jnp.where((sub >= 8) & (sub < 16), pltpu.roll(right, LANES - 16, axis=1), own[k])
                u.append(jnp.where((sub >= 16) & (sub < 24), pltpu.roll(left, 16, axis=1), x))
        prim = primitives(u)
        if slot == LAYERS:
            for i, x in enumerate(cell_coefficients(u, prim)):
                cs[i] = x
        for i, x in enumerate(rolled_faces(u, prim, 1, 1)):
            tf[i, slot] = x
    for half in range(2):
        rows = slice(8 * half, 8 * half + 8)
        cell = [[flow[k, l, rows] for k in range(FIELDS)] for l in range(LAYERS)]
        prims = [primitives(u) for u in cell]
        clamp = lambda j: min(max(j, 0), LAYERS - 1)
        nus = {}
        for j in range(-1, LAYERS + 1):
            nu, n0, n1 = sensor_terms(*[prims[clamp(j + d)][3] for d in (-1, 0, 1)])
            nus[j] = nu
            ln[0, j + 1, rows] = n0
            ln[1, j + 1, rows] = n1
        radius = [pr[5][2] + pr[4] for pr in prims]
        for f in range(-1, LAYERS):
            terms = face_terms(
                nus[f],
                nus[f + 1],
                radius[clamp(f)],
                radius[clamp(f + 1)],
                *[cell[clamp(f + d)] for d in (-1, 0, 1, 2)],
            )
            for i, x in enumerate(terms):
                lf[i, f + 1, rows] = x


def transposed_terms(flags, psi, coefs, acc, strip, to_a, to_b, ghost):
    cm, ch, cs, xf, tf, lf, ln = coefs
    row = iota((8, LANES), 0)
    inlet = flagged(flags, INLET, (8, LANES))
    outlet = flagged(flags, OUTLET, (8, LANES))
    even = flagged(flags, B_EVEN, (8, LANES))
    empty = jnp.zeros((8, LANES), jnp.float32)
    for l in range(LAYERS):
        wide = [jnp.concatenate([psi[k, l], empty], axis=0) for k in range(FIELDS)]
        cells = [jnp.concatenate([cm[i, l], ch[i, l]], axis=0) for i in range(CELLS)]
        g = rolled_transpose(wide, lambda i: xf[i, l], cells, 0, 0)
        for k in range(FIELDS):
            out = g[k][16:]
            ghost[k, l] = out
            first = pltpu.roll(out, 2, axis=0) + pltpu.roll(out, 1, axis=0)
            last = pltpu.roll(out, 7, axis=0) + pltpu.roll(out, 6, axis=0)
            acc[k, l, 0:8] = g[k][0:8] + jnp.where(inlet & (row == 0), first, 0.0)
            acc[k, l, 8:16] = g[k][8:16] + jnp.where(outlet & (row == 7), last, 0.0)
    for k in range(FIELDS):
        high = packed_rows([ghost[k, l] for l in range(LAYERS)])
        low = packed_rows([pltpu.roll(ghost[k, l], 2, axis=0) for l in range(LAYERS)])
        to_a[k] = jnp.where(even, high, low)
        to_b[k] = jnp.where(even, low, high)
    lane = iota((ROWS, LANES), 1)
    sub = place_in_segment()
    inner = (lane >= 1) & (lane < LANES - 2)
    edges = ((sub >= 6) & (sub < 8)) | ((sub >= 23) & (sub < 25))
    for slot in range(LAYERS + 1):
        if slot < LAYERS:
            values = [psi[k, slot] for k in range(FIELDS)]
            cells = [cm[i, slot] for i in range(CELLS)]
            mask = inner
        else:
            values = [packed_strip([psi[k, l] for l in range(LAYERS)]) for k in range(FIELDS)]
            cells = [cs[i] for i in range(CELLS)]
            mask = edges
        g = rolled_transpose(values, lambda i: tf[i, slot], cells, 1, 1, mask)
        for k in range(FIELDS):
            if slot < LAYERS:
                acc[k, slot] = acc[k, slot] + g[k]
            else:
                strip[k] = g[k]
    last = LAYERS - 1
    for half in range(2):
        rows = slice(8 * half, 8 * half + 8)
        value = [[psi[k, l, rows] for k in range(FIELDS)] for l in range(LAYERS)]
        w, c, gl, ge = {}, {}, {}, {}
        for f in range(-1, LAYERS):
            if f < 0:
                w[f] = [-x for x in value[0]]
            elif f == last:
                w[f] = value[last]
            else:
                w[f] = [x - y for x, y in zip(value[f], value[f + 1])]
            face = lambda i: lf[i, f + 1, rows]
            gl[f] = dot5(w[f], [face(DL + k) for k in range(FIELDS)])
            ge[f] = dot5(w[f], [face(ES + k) for k in range(FIELDS)])
            c[f] = [face(A4) * x for x in w[f]]
        z = {}
        for f in range(last):
            a2 = lf[A2, f + 1, rows]
            z[f] = [a2 * w[f][k] + 2.0 * c[f][k] - c[f + 1][k] - c[f - 1][k] for k in range(FIELDS)]
        nbar = [None] * LAYERS
        for j in range(-1, LAYERS + 1):
            nu_bar = ge.get(j, 0.0) + ge.get(j - 1, 0.0)
            here = ln[0, j + 1, rows] * nu_bar
            side = ln[1, j + 1, rows] * nu_bar
            for to, x in ((j, here), (j - 1, side), (j + 1, side)):
                to = min(max(to, 0), last)
                nbar[to] = x if nbar[to] is None else nbar[to] + x
        for j in range(LAYERS):
            if j == 0:
                s = [0.5 * w[0][k] + w[-1][k] for k in range(FIELDS)]
                lin = z[0]
                rbar = gl[0] + 2.0 * gl[-1]
            elif j == last:
                s = [0.5 * w[last - 1][k] + w[last][k] for k in range(FIELDS)]
                lin = [-x for x in z[last - 1]]
                rbar = gl[last - 1] + 2.0 * gl[last]
            else:
                s = [0.5 * (w[j][k] + w[j - 1][k]) for k in range(FIELDS)]
                lin = [z[j][k] - z[j - 1][k] for k in range(FIELDS)]
                rbar = gl[j] + gl[j - 1]
            g = to_state(lin, s, rbar, nbar[j], [cm[i, j, rows] for i in range(CELLS)], 2)
            for k in range(FIELDS):
                acc[k, j, rows] = acc[k, j, rows] + g[k]


def start_kernel(
    flags, flow, own, from_a, from_b, zone_a, near, far, maps, adjoint, later, gradient, volume,
    keep, factor, pushed, acc, strip, to_a, to_b, cm, ch, cs, xf, tf, lf, ln, ghost,
):
    coefficients(
        flags, flow, own, from_a, from_b, zone_a, near, far, maps, cm, ch, cs, xf, tf, lf, ln
    )
    for l in range(LAYERS):
        u = [flow[k, l] for k in range(FIELDS)]
        _, _, _, _, sound, roots = primitives(u)
        vol = volume[l]
        radius_sum = roots[0] + roots[1] + roots[2] + 3.0 * sound
        f = courant / (radius_sum + (1.5 * courant / physical_step) * vol)
        factor[l] = f
        keep[l] = 1.0 - f * ((1.5 / physical_step) * vol)
        for k in range(FIELDS):
            source = gradient[k, l] + vol * (2.0 * later[0, k, l] - 0.5 * later[1, k, l]) / physical_step
            pushed[k, l] = f * source
    transposed_terms(flags, adjoint, (cm, ch, cs, xf, tf, lf, ln), acc, strip, to_a, to_b, ghost)


def advance(flags, psi, acc, strip, from_a, from_b, zone_a, near, far, maps, keep, factor, pushed, out):
    through = mapped(near, far, maps, True)
    lower, upper = lower_and_upper(flags, zone_a, near, through)
    row = iota((8, LANES), 0)
    first = (row < 2) & jnp.logical_not(flagged(flags, INLET, (8, LANES)))
    last = (row >= 6) & jnp.logical_not(flagged(flags, OUTLET, (8, LANES)))
    sub = place_in_segment()
    for k in range(FIELDS):
        left, right = left_and_right(flags, from_a, from_b, k)
        whole = strip[k]
        whole = whole + jnp.where(sub >= 24, pltpu.roll(left, 16, axis=1), 0.0)
        whole = whole + jnp.where(sub < 8, pltpu.roll(right, LANES - 16, axis=1), 0.0)
        for l in range(LAYERS):
            low = jnp.where(first, pltpu.roll(lower[k], (-2 * l) % 8, axis=0), 0.0)
            high = jnp.where(last, pltpu.roll(upper[k], (6 - 2 * l) % 8, axis=0), 0.0)
            total = acc[k, l] + from_strip(whole, l) + jnp.concatenate([low, high], axis=0)
            out[k, l] = psi[k, l] * keep[l] - factor[l] * total + pushed[k, l]


def step_kernel(
    flags, psi, acc, strip, from_a, from_b, zone_a, near, far, maps, keep, factor, pushed,
    cm, ch, cs, xf, tf, lf, ln, out, acc_out, strip_out, to_a, to_b, ghost,
):
    advance(flags, psi, acc, strip, from_a, from_b, zone_a, near, far, maps, keep, factor, pushed, out)
    transposed_terms(flags, out, (cm, ch, cs, xf, tf, lf, ln), acc_out, strip_out, to_a, to_b, ghost)


def last_kernel(flags, psi, acc, strip, from_a, from_b, zone_a, near, far, maps, keep, factor, pushed, out):
    advance(flags, psi, acc, strip, from_a, from_b, zone_a, near, far, maps, keep, factor, pushed, out)


def f32(*shape):
    return jax.ShapeDtypeStruct(shape, jnp.float32)


STATE = (FIELDS, LAYERS, ROWS, LANES)
STRIP = (FIELDS, ROWS, LANES)
PANEL = (FIELDS, 8, LANES)
SCALAR = (LAYERS, ROWS, LANES)
TERMS = (f32(*STATE), f32(*STRIP), f32(*PANEL), f32(*PANEL))
COEFS = (
    f32(CELLS, *SCALAR),
    f32(CELLS, LAYERS, 8, LANES),
    f32(CELLS, ROWS, LANES),
    f32(FACES, LAYERS, ROWS + 8, LANES),
    f32(FACES, LAYERS + 1, ROWS, LANES),
    f32(12, LAYERS + 1, ROWS, LANES),
    f32(2, LAYERS + 2, ROWS, LANES),
)


def call(kernel, outs, args, ghost=False, name=None):
    vmem = pl.BlockSpec(memory_space=pltpu.VMEM)
    smem = pl.BlockSpec(memory_space=pltpu.SMEM)
    return pl.pallas_call(
        kernel,
        out_shape=outs,
        in_specs=[smem] + [vmem] * (len(args) - 1),
        out_specs=[vmem] * len(outs) if isinstance(outs, tuple) else vmem,
        scratch_shapes=[pltpu.VMEM((FIELDS, LAYERS, 8, LANES), jnp.float32)] if ghost else [],
        compiler_params=pltpu.CompilerParams(vmem_limit_bytes=32 * 1024 * 1024),
        name=name,
    )(*args)


def swaps(names, sectors, blocks, turn):
    half = blocks // 2
    assert half % 2 == 0
    where = {"sector": sectors, "block": blocks}
    minor = where[names[1]]

    def flat(b, s):
        first, second = (s, b) if names[0] == "sector" else (b, s)
        return first * minor + second

    sector_a, sector_b, block_a, near, far = [], [], [], [], []
    for b in range(blocks):
        for s in range(sectors):
            me = flat(b, s)
            sector_a.append((me, flat(b, s ^ 1)))
            sector_b.append((me, flat(b, (s + (1 if s % 2 else -1)) % sectors)))
            block_a.append((me, flat(b ^ 1, s)))
            if b == half - 1:
                near.append((me, flat(half, (s + turn) % sectors)))
                far.append((me, flat(half, (s + turn + 1) % sectors)))
            elif b == half:
                near.append((me, flat(half - 1, (s - turn) % sectors)))
                far.append((me, flat(half - 1, (s - turn - 1) % sectors)))
            else:
                other = b + 1 if b % 2 else b - 1
                near.append((me, flat(other, s) if 0 <= other < blocks else me))
                far.append((me, me))
    return sector_a, sector_b, block_a, near, far


def exchange(names, sectors, blocks, offset, strip, to_a, to_b):
    def branch(shift):
        sector_a, sector_b, block_a, near, far = swaps(names, sectors, blocks, shift)

        def run(strip, to_a, to_b):
            move = lambda x, pairs: lax.ppermute(x, names, pairs)
            return (
                move(strip, sector_a),
                move(strip, sector_b),
                move(to_a, block_a),
                move(to_b, near),
                move(to_b, far),
            )

        return run

    return lax.switch(offset, [branch(shift) for shift in range(sectors)], strip, to_a, to_b)


def shards(flow, adjoint, adjoint_later, objective_grad, volume, panel_maps, rotor_step, names):
    blocks = lax.axis_size("block")
    sectors = lax.axis_size("sector")
    place = lax.axis_index("block")
    half = blocks // 2
    stator = place >= half
    turn = rotor_step[0]
    offset = (turn // PHASES) % sectors
    maps = lax.dynamic_index_in_dim(panel_maps, turn % PHASES, 0, keepdims=False)
    state_maps = jnp.where(stator, maps[:2], maps[2:])
    grad_maps = jnp.where(stator, maps[2:], maps[:2])
    flags = jnp.stack(
        [
            lax.axis_index("sector") % 2 == 0,
            place % 2 == 0,
            place == 0,
            place == blocks - 1,
            place == half,
            place == half - 1,
            place < 0,
            place < 0,
        ]
    ).astype(jnp.int32)
    send = partial(exchange, names, sectors, blocks, offset)
    packed = tuple(call(pack_kernel, (f32(*STRIP), f32(*PANEL), f32(*PANEL)), (flags, flow), name="pack"))
    out = call(
        start_kernel,
        (f32(*SCALAR), f32(*SCALAR), f32(*STATE)) + TERMS + COEFS,
        (flags, flow, packed[0])
        + send(*packed)
        + (state_maps, adjoint, adjoint_later, objective_grad, volume),
        ghost=True,
        name="start",
    )
    update, terms, coefs = tuple(out[:3]), tuple(out[3:7]), tuple(out[7:])
    current = adjoint
    for sweep in range(ITERS):
        args = (flags, current) + terms[:2] + send(*terms[1:]) + (grad_maps,) + update
        if sweep == ITERS - 1:
            return call(last_kernel, f32(*STATE), args, name="last")
        out = call(step_kernel, (f32(*STATE),) + TERMS, args + coefs, ghost=True, name="step")
        current, terms = out[0], tuple(out[1:])


def solution(mesh):
    placed = (
        P(None, None, "block", "sector"),
        P(None, None, "block", "sector"),
        P(None, None, None, "block", "sector"),
        P(None, None, "block", "sector"),
        P(None, "block", "sector"),
        P(),
        P(),
    )
    return jax.shard_map(
        partial(shards, names=tuple(mesh.axis_names)),
        mesh=mesh,
        in_specs=placed,
        out_specs=P(None, None, "block", "sector"),
        check_vma=False,
    )
```

```python
from functools import partial

import jax
import jax.numpy as jnp
from jax import lax
from jax.experimental import pallas as pl
from jax.experimental.pallas import tpu as pltpu
from jax.sharding import PartitionSpec as P

PHASES = 4
ITERS = 4
LANES = 128
ROWS = 16
LAYERS = 4
FIELDS = 5
SEG = LANES // LAYERS

gamma_gas = 1.4
second_coef = 0.5
fourth_coef = 1.0 / 32.0
courant = 0.6
physical_step = 2.0
sensor_floor = 0.0001
highest = lax.Precision.HIGHEST

S_EVEN, B_EVEN, INLET, OUTLET, PLANE, PHASE, STATE_MAPS, GRAD_MAPS = range(8)
U1, U2, U3, HT, BX, BT, BL, CR, CP, EK = range(10)
CELLS = 10
A2, A4, DL, ES, N0, N1 = 0, 1, 2, 7, 12, 13
FACES = 14


def up_by(x, axis, k):
    n = x.shape[axis]
    return pltpu.roll(x, (-k) % n, axis=axis)


def iota(shape, axis):
    return lax.broadcasted_iota(jnp.int32, shape, axis)


def flagged(flags, which, shape):
    return jnp.broadcast_to(flags[which], shape) == 1


def primitives(u):
    inverse = 1.0 / u[0]
    vel = [u[1] * inverse, u[2] * inverse, u[3] * inverse]
    square = vel[0] * vel[0] + vel[1] * vel[1] + vel[2] * vel[2]
    p = (gamma_gas - 1.0) * (u[4] - 0.5 * u[0] * square)
    sound = jnp.sqrt(gamma_gas * p * inverse)
    roots = [jnp.sqrt(q * q + 0.01) for q in vel]
    return inverse, vel, square, p, sound, roots


def cell_coefficients(u, prim):
    inverse, vel, square, p, sound, roots = prim
    return (
        vel
        + [(u[4] + p) * inverse]
        + [q / r * inverse for q, r in zip(vel, roots)]
        + [0.5 * sound * inverse, 0.5 * sound / p, (0.5 * (gamma_gas - 1.0)) * square]
    )


def sensor_terms(below, here, above):
    bend = above - 2.0 * here + below
    total = above + 2.0 * here + below
    root = jnp.sqrt(bend * bend + sensor_floor)
    over = 1.0 / total
    nu = root * over
    a = bend / root * over
    b = nu * over
    return nu, -2.0 * a - 2.0 * b, a - b


def face_terms(nu_left, nu_right, rad_left, rad_right, behind, left, right, ahead):
    e2 = (0.5 * second_coef) * (nu_left + nu_right)
    ratio = fourth_coef / (fourth_coef + e2)
    e4 = fourth_coef * ratio
    slope = ratio * ratio
    lam = 0.5 * (rad_left + rad_right)
    radial, sensed = [], []
    for b, l, r, a in zip(behind, left, right, ahead):
        first = r - l
        third = a - 3.0 * first - b
        radial.append(-0.5 * (e2 * first - e4 * third))
        sensed.append((-0.25) * lam * (first + slope * third))
    return [lam * e2, lam * e4] + radial + sensed


def rolled_faces(u, prim, direction, axis):
    _, _, _, p, sound, roots = prim
    nu, n0, n1 = sensor_terms(up_by(p, axis, -1), p, up_by(p, axis, 1))
    radius = roots[direction] + sound
    right = [up_by(x, axis, 1) for x in u]
    behind = [up_by(x, axis, -1) for x in u]
    ahead = [up_by(x, axis, 2) for x in u]
    return face_terms(
        nu, up_by(nu, axis, 1), radius, up_by(radius, axis, 1), behind, u, right, ahead
    ) + [n0, n1]


def dot5(a, b):
    return (a[0] * b[0] + a[1] * b[1]) + (a[2] * b[2] + a[3] * b[3]) + a[4] * b[4]


def to_state(lin, s, rbar, nbar, cells, direction):
    q = cells[direction]
    kappa = s[1] * cells[U1] + s[2] * cells[U2] + s[3] * cells[U3] + s[4] * cells[HT]
    kappa = kappa + cells[BX + direction] * rbar
    sq = s[4] * q
    pbar = nbar + sq + s[direction + 1] + cells[CP] * rbar
    scaled = (gamma_gas - 1.0) * pbar
    g = [None] * FIELDS
    g[0] = lin[0] - q * kappa - cells[CR] * rbar + cells[EK] * pbar
    for k in range(3):
        g[k + 1] = lin[k + 1] + q * s[k + 1] - cells[k] * scaled
    g[direction + 1] = g[direction + 1] + (s[0] + kappa)
    g[4] = lin[4] + sq + scaled
    return g


def rolled_transpose(psi, faces, cells, direction, axis, mask=None):
    w = [x - up_by(x, axis, 1) for x in psi]
    if mask is not None:
        w = [jnp.where(mask, x, 0.0) for x in w]
    gl = dot5(w, [faces(DL + k) for k in range(FIELDS)])
    ge = dot5(w, [faces(ES + k) for k in range(FIELDS)])
    a2, a4 = faces(A2), faces(A4)
    lin, s = [], []
    for x in w:
        c = a4 * x
        z = a2 * x + 2.0 * c - up_by(c, axis, 1) - up_by(c, axis, -1)
        lin.append(z - up_by(z, axis, -1))
        s.append(0.5 * (x + up_by(x, axis, -1)))
    rbar = gl + up_by(gl, axis, -1)
    nu_bar = ge + up_by(ge, axis, -1)
    v = faces(N1) * nu_bar
    nbar = faces(N0) * nu_bar + up_by(v, axis, 1) + up_by(v, axis, -1)
    return to_state(lin, s, rbar, nbar, cells, direction)


def packed_rows(tiles):
    row = iota((8, LANES), 0)
    out = tiles[0]
    for l in range(1, LAYERS):
        out = jnp.where(row >= 2 * l, pltpu.roll(tiles[l], 2 * l, axis=0), out)
    return out


def packed_quads(tiles):
    row = iota((8, LANES), 0)
    pairs = [
        jnp.where(row < 4, tiles[l], pltpu.roll(tiles[l + 1], 4, axis=0)) for l in range(0, LAYERS, 2)
    ]
    return jnp.concatenate(pairs, axis=0)


def quad(packed, l, high):
    tile = packed[8 * (l // 2) : 8 * (l // 2) + 8]
    return pltpu.roll(tile, 4, axis=0) if (l % 2 == 1) != high else tile


def pair(packed, l, to):
    shift = (to - 2 * l) % 8
    return pltpu.roll(packed, shift, axis=0) if shift else packed


def packed_strip(layers):
    lane = iota((ROWS, LANES), 1)
    out = jnp.zeros((ROWS, LANES), jnp.float32)
    for l, x in enumerate(layers):
        base = SEG * l
        out = jnp.where((lane >= base) & (lane < base + 8), pltpu.roll(x, (base + 8) % LANES, axis=1), out)
        out = jnp.where(
            (lane >= base + 24) & (lane < base + 32), pltpu.roll(x, (base + 24) % LANES, axis=1), out
        )
    return out


def packed_edges(layers, others):
    lane = iota((ROWS, LANES), 1)
    out = packed_strip(layers)
    for l, x in enumerate(others):
        base = SEG * l + 16
        out = jnp.where((lane >= base - 8) & (lane < base + 8), pltpu.roll(x, base, axis=1), out)
    return out


def from_strip(strip, l):
    lane = iota((ROWS, LANES), 1)
    base = SEG * l
    low = pltpu.roll(strip, (-(base + 24)) % LANES, axis=1)
    high = pltpu.roll(strip, (-(base + 8)) % LANES, axis=1)
    return jnp.where(lane < 8, low, jnp.where(lane >= LANES - 8, high, 0.0))


def place_in_segment():
    return jnp.bitwise_and(iota((ROWS, LANES), 1), SEG - 1)


def clamp(j):
    return min(max(j, 0), LAYERS - 1)


def fetched(pairs, sems):
    copies = [pltpu.make_async_copy(s, d, sems.at[i]) for i, (s, d) in enumerate(pairs)]
    for copy in copies:
        copy.start()
    return copies


def pack_kernel(flags, flow, psi, to_t, to_a, to_b):
    even = flagged(flags, B_EVEN, (8, LANES))
    even2 = flagged(flags, B_EVEN, (16, LANES))
    for k in range(FIELDS):
        to_t[k, 0:16] = packed_edges([flow[k, l] for l in range(LAYERS)], [psi[k, l] for l in range(LAYERS)])
        low = packed_rows([flow[k, l, 0:8] for l in range(LAYERS)])
        high = packed_rows([pltpu.roll(flow[k, l, 8:16], 2, axis=0) for l in range(LAYERS)])
        to_t[k, 16:24] = jnp.where(even, low, high)
        low = packed_quads([flow[k, l, 0:8] for l in range(LAYERS)])
        high = packed_quads([pltpu.roll(flow[k, l, 8:16], 4, axis=0) for l in range(LAYERS)])
        to_a[k, 0:16] = jnp.where(even2, high, low)
        to_b[k, 0:16] = jnp.where(even2, low, high)
        low = packed_rows([psi[k, l, 0:8] for l in range(LAYERS)])
        high = packed_rows([pltpu.roll(psi[k, l, 8:16], 2, axis=0) for l in range(LAYERS)])
        to_a[k, 16:24] = jnp.where(even, high, low)
        to_b[k, 16:24] = jnp.where(even, low, high)


def mapped(near, far, maps, transposed):
    shape = near.shape
    dims = (((1,), (0,)), ((), ())) if transposed else (((1,), (1,)), ((), ()))
    near = near.reshape(shape[0] * shape[1], LANES)
    far = far.reshape(shape[0] * shape[1], LANES)
    out = lax.dot_general(near, maps[0], dims, precision=highest, preferred_element_type=jnp.float32)
    out = out + lax.dot_general(far, maps[1], dims, precision=highest, preferred_element_type=jnp.float32)
    return out.reshape(shape)


def left_and_right(flags, a, b):
    even = flagged(flags, S_EVEN, a.shape)
    return jnp.where(even, b, a), jnp.where(even, a, b)


def widened(flags, own, a, b):
    sub = place_in_segment()
    left, right = left_and_right(flags, a, b)
    x = jnp.where((sub >= 8) & (sub < 16), pltpu.roll(right, LANES - 16, axis=1), own)
    return jnp.where((sub >= 16) & (sub < 24), pltpu.roll(left, 16, axis=1), x)


def widened_other(flags, own, a, b):
    sub = place_in_segment()
    left, right = left_and_right(flags, a, b)
    low = pltpu.roll(jnp.where((sub >= 16) & (sub < 24), right, own), LANES - 8, axis=1)
    high = pltpu.roll(jnp.where((sub >= 8) & (sub < 16), left, own), 8, axis=1)
    return jnp.where(sub < 16, low, high)


def coefficients(flags, flow, own, from_a, from_b, zone_a, near, far, maps, cm, ch, cs, xf, tf, lf, ln):
    through = mapped(near[:, 0:16], far[:, 0:16], maps, False)
    even = flagged(flags, B_EVEN, (16, LANES))
    plane = flagged(flags, PLANE, (16, LANES))
    row = iota((8, LANES), 0)
    inlet = flagged(flags, INLET, (8, LANES))
    outlet = flagged(flags, OUTLET, (8, LANES))
    lower, upper = [], []
    for k in range(FIELDS):
        b = jnp.where(plane, through[k], near[k, 0:16])
        a = zone_a[k, 0:16]
        lower.append(jnp.where(even, b, a))
        upper.append(jnp.where(even, a, b))
    for l in range(LAYERS):
        u = []
        for k in range(FIELDS):
            main = flow[k, l]
            up = jnp.where(outlet, jnp.broadcast_to(main[15:16], (8, LANES)), quad(upper[k], l, False))
            low = jnp.where(inlet, jnp.broadcast_to(main[0:1], (8, LANES)), quad(lower[k], l, True))
            u.append(jnp.concatenate([main, jnp.where(row < 4, up, low)], axis=0))
        prim = primitives(u)
        for i, x in enumerate(cell_coefficients(u, prim)):
            cm[i, l] = x[:16]
            ch[i, l] = x[16:]
        for i, x in enumerate(rolled_faces(u, prim, 0, 0)):
            xf[i, l] = x
    for slot in range(LAYERS + 1):
        if slot < LAYERS:
            u = [flow[k, slot] for k in range(FIELDS)]
        else:
            u = [widened(flags, own[k, 0:16], from_a[k, 0:16], from_b[k, 0:16]) for k in range(FIELDS)]
        prim = primitives(u)
        if slot == LAYERS:
            for i, x in enumerate(cell_coefficients(u, prim)):
                cs[i] = x
        for i, x in enumerate(rolled_faces(u, prim, 1, 1)):
            tf[i, slot] = x
    for half in range(2):
        rows = slice(8 * half, 8 * half + 8)
        cell = [[flow[k, l, rows] for k in range(FIELDS)] for l in range(LAYERS)]
        prims = [primitives(u) for u in cell]
        nus = {}
        for j in range(-1, LAYERS + 1):
            nu, n0, n1 = sensor_terms(*[prims[clamp(j + d)][3] for d in (-1, 0, 1)])
            nus[j] = nu
            ln[0, j + 1, rows] = n0
            ln[1, j + 1, rows] = n1
        radius = [pr[5][2] + pr[4] for pr in prims]
        for f in range(-1, LAYERS):
            terms = face_terms(
                nus[f],
                nus[f + 1],
                radius[clamp(f)],
                radius[clamp(f + 1)],
                *[cell[clamp(f + d)] for d in (-1, 0, 1, 2)],
            )
            for i, x in enumerate(terms):
                lf[i, f + 1, rows] = x


def x_terms(flags, psi, halo, coefs, acc, ghost):
    cm, ch, _, xf, _, _, _ = coefs
    row = iota((8, LANES), 0)
    inlet = flagged(flags, INLET, (8, LANES)) & (row == 0)
    outlet = flagged(flags, OUTLET, (8, LANES)) & (row == 7)
    for l in range(LAYERS):
        wide = [jnp.concatenate([psi[k, l], halo(k, l)], axis=0) for k in range(FIELDS)]
        cells = [jnp.concatenate([cm[i, l], ch[i, l]], axis=0) for i in range(CELLS)]
        g = rolled_transpose(wide, lambda i: xf[i, l], cells, 0, 0)
        for k in range(FIELDS):
            out = g[k][16:]
            if ghost is not None:
                ghost[k, l] = out
            first = pltpu.roll(out, 2, axis=0) + pltpu.roll(out, 1, axis=0)
            last = pltpu.roll(out, 7, axis=0) + pltpu.roll(out, 6, axis=0)
            acc[k, l, 0:8] = g[k][0:8] + jnp.where(inlet, first, 0.0)
            acc[k, l, 8:16] = g[k][8:16] + jnp.where(outlet, last, 0.0)


def t_terms(psi, values, edges, coefs, acc, strip):
    cm, _, cs, _, tf, _, _ = coefs
    lane = iota((ROWS, LANES), 1)
    inner = (lane >= 1) & (lane < LANES - 2)
    for slot in range(LAYERS + 1):
        own = slot < LAYERS
        g = rolled_transpose(
            [psi[k, slot] for k in range(FIELDS)] if own else values,
            lambda i: tf[i, slot],
            [cm[i, slot] if own else cs[i] for i in range(CELLS)],
            1,
            1,
            inner if own else edges,
        )
        for k in range(FIELDS):
            if own:
                acc[k, slot] = acc[k, slot] + g[k]
            else:
                strip[k] = g[k]


def l_terms(psi, coefs, acc):
    cm, _, _, _, _, lf, ln = coefs
    last = LAYERS - 1
    for half in range(2):
        rows = slice(8 * half, 8 * half + 8)
        value = [[psi[k, l, rows] for k in range(FIELDS)] for l in range(LAYERS)]
        w, c, gl, ge = {}, {}, {}, {}
        for f in range(-1, LAYERS):
            if f < 0:
                w[f] = [-x for x in value[0]]
            elif f == last:
                w[f] = value[last]
            else:
                w[f] = [x - y for x, y in zip(value[f], value[f + 1])]
            gl[f] = dot5(w[f], [lf[DL + k, f + 1, rows] for k in range(FIELDS)])
            ge[f] = dot5(w[f], [lf[ES + k, f + 1, rows] for k in range(FIELDS)])
            a4 = lf[A4, f + 1, rows]
            c[f] = [a4 * x for x in w[f]]
        z = {}
        for f in range(last):
            a2 = lf[A2, f + 1, rows]
            z[f] = [a2 * w[f][k] + 2.0 * c[f][k] - c[f + 1][k] - c[f - 1][k] for k in range(FIELDS)]
        nbar = [None] * LAYERS
        for j in range(-1, LAYERS + 1):
            nu_bar = ge.get(j, 0.0) + ge.get(j - 1, 0.0)
            here = ln[0, j + 1, rows] * nu_bar
            side = ln[1, j + 1, rows] * nu_bar
            for to, x in ((j, here), (j - 1, side), (j + 1, side)):
                to = clamp(to)
                nbar[to] = x if nbar[to] is None else nbar[to] + x
        for j in range(LAYERS):
            if j == 0:
                s = [0.5 * w[0][k] + w[-1][k] for k in range(FIELDS)]
                lin = z[0]
                rbar = gl[0] + 2.0 * gl[-1]
            elif j == last:
                s = [0.5 * w[last - 1][k] + w[last][k] for k in range(FIELDS)]
                lin = [-x for x in z[last - 1]]
                rbar = gl[last - 1] + 2.0 * gl[last]
            else:
                s = [0.5 * (w[j][k] + w[j - 1][k]) for k in range(FIELDS)]
                lin = [z[j][k] - z[j - 1][k] for k in range(FIELDS)]
                rbar = gl[j] + gl[j - 1]
            g = to_state(lin, s, rbar, nbar[j], [cm[i, j, rows] for i in range(CELLS)], 2)
            for k in range(FIELDS):
                acc[k, j, rows] = acc[k, j, rows] + g[k]


def transposed_terms(flags, psi, coefs, acc, strip, to_a, to_b, ghost):
    even = flagged(flags, B_EVEN, (8, LANES))
    empty = jnp.zeros((8, LANES), jnp.float32)
    x_terms(flags, psi, lambda k, l: empty, coefs, acc, ghost)
    for k in range(FIELDS):
        high = packed_rows([ghost[k, l] for l in range(LAYERS)])
        low = packed_rows([pltpu.roll(ghost[k, l], 2, axis=0) for l in range(LAYERS)])
        to_a[k] = jnp.where(even, high, low)
        to_b[k] = jnp.where(even, low, high)
    sub = place_in_segment()
    edges = ((sub >= 6) & (sub < 8)) | ((sub >= 23) & (sub < 25))
    values = [packed_strip([psi[k, l] for l in range(LAYERS)]) for k in range(FIELDS)]
    t_terms(psi, values, edges, coefs, acc, strip)
    l_terms(psi, coefs, acc)


def settle(psi, acc, keep, factor, pushed, base):
    for k in range(FIELDS):
        for l in range(LAYERS):
            base[k, l] = psi[k, l] * keep[l] - factor[l] * acc[k, l] + pushed[k, l]


def arrived_rows(flags, lower, upper):
    row = iota((8, LANES), 0)
    first = (row < 2) & jnp.logical_not(flagged(flags, INLET, (8, LANES)))
    last = (row >= 6) & jnp.logical_not(flagged(flags, OUTLET, (8, LANES)))

    def rows(k, l):
        low = jnp.where(first, pair(lower[k], l, 0), 0.0)
        high = jnp.where(last, pair(upper[k], l, 6), 0.0)
        return jnp.concatenate([low, high], axis=0)

    return rows


def facing_gradients(flags, own, from_a, from_b, near, far, maps):
    rotor = jnp.logical_not(flagged(flags, B_EVEN, (8, LANES)))
    row = iota((8, LANES), 0)
    panel = own[:, 16:24]
    first, second = [], []
    for k in range(FIELDS):
        left, right = left_and_right(flags, from_a[k, 16:24], from_b[k, 16:24])
        first.append(jnp.where(rotor, left, right))
        second.append(jnp.where(rotor, right, left))
    ghosts = (
        mapped(panel, jnp.stack(first), maps, False),
        mapped(jnp.stack(second), panel, maps, False),
    )
    kept = (row == 7) | (rotor & (row == 0)) | (jnp.logical_not(rotor) & (row == 6))
    out = []
    for ghost, facing in zip(ghosts, (near, far)):
        layers = []
        for l in range(LAYERS):
            u, psi = [], []
            for k in range(FIELDS):
                cells = facing[k, 0:16]
                below = pair(ghost[k], l, 6)
                above = pair(ghost[k], l, 0)
                as_rotor = jnp.where(
                    row < 4,
                    quad(cells, l, False),
                    jnp.where(row < 6, pltpu.roll(below, 6, axis=0), below),
                )
                as_stator = jnp.where(
                    row < 2,
                    above,
                    jnp.where(row < 4, pltpu.roll(above, 2, axis=0), quad(cells, l, True)),
                )
                u.append(jnp.where(rotor, as_rotor, as_stator))
                value = facing[k, 16:24]
                psi.append(
                    jnp.where(
                        rotor,
                        jnp.where(row < 2, pair(value, l, 0), 0.0),
                        jnp.where(row >= 6, pair(value, l, 6), 0.0),
                    )
                )
            prim = primitives(u)
            faces = rolled_faces(u, prim, 0, 0)
            g = rolled_transpose(psi, lambda i: faces[i], cell_coefficients(u, prim), 0, 0, kept)
            layers.append([jnp.where(rotor, pltpu.roll(x, 2, axis=0), x) for x in g])
        out.append(jnp.stack([packed_rows([layers[l][k] for l in range(LAYERS)]) for k in range(FIELDS)]))
    return out


def start_kernel(
    flags, flow, own, from_a, from_b, zone_a, near, far, panel_maps, adjoint_in, later_in, gradient_in,
    volume_in, keep, factor, pushed, grad_maps, base, strip, to_a, to_b, cm, ch, cs, xf, tf, lf, ln,
    state_maps, adjoint, later, gradient, volume, landed, sems, psi, acc, ghost,
):
    pair_of = lambda which: panel_maps.at[flags[PHASE], pl.ds(flags[which], 2)]
    copies = fetched(
        [
            (pair_of(STATE_MAPS), state_maps),
            (volume_in, volume),
            (later_in, later),
            (gradient_in, gradient),
            (adjoint_in, adjoint),
            (pair_of(GRAD_MAPS), landed),
        ],
        sems,
    )
    coefs = (cm, ch, cs, xf, tf, lf, ln)
    copies[0].wait()
    coefficients(flags, flow, own, from_a, from_b, zone_a, near, far, state_maps, *coefs)
    for copy in copies[1:]:
        copy.wait()
    grad_maps[...] = landed[...]
    for l in range(LAYERS):
        u = [flow[k, l] for k in range(FIELDS)]
        _, _, _, _, sound, roots = primitives(u)
        vol = volume[l]
        radius_sum = roots[0] + roots[1] + roots[2] + 3.0 * sound
        f = courant / (radius_sum + (1.5 * courant / physical_step) * vol)
        factor[l] = f
        keep[l] = 1.0 - f * ((1.5 / physical_step) * vol)
        for k in range(FIELDS):
            source = gradient[k, l] + vol * (2.0 * later[0, k, l] - 0.5 * later[1, k, l]) / physical_step
            pushed[k, l] = f * source

    even = flagged(flags, B_EVEN, (8, LANES))
    plane = flagged(flags, PLANE, (8, LANES))
    row = iota((8, LANES), 0)
    use_upper = (row < 2) & jnp.logical_not(flagged(flags, OUTLET, (8, LANES)))
    use_lower = (row >= 6) & jnp.logical_not(flagged(flags, INLET, (8, LANES)))

    def halo(k, l):
        a = zone_a[k, 16:24]
        b = jnp.where(plane, 0.0, near[k, 16:24])
        upper = pair(jnp.where(even, a, b), l, 0)
        lower = pair(jnp.where(even, b, a), l, 6)
        return jnp.where(use_upper, upper, jnp.where(use_lower, lower, 0.0))

    x_terms(flags, adjoint, halo, coefs, acc, None)
    sub = place_in_segment()
    edges = ((sub >= 6) & (sub < 9)) | ((sub >= 22) & (sub < 25))
    values = [widened_other(flags, own[k, 0:16], from_a[k, 0:16], from_b[k, 0:16]) for k in range(FIELDS)]
    t_terms(adjoint, values, edges, coefs, acc, strip)
    l_terms(adjoint, coefs, acc)
    panels = facing_gradients(flags, own, from_a, from_b, near, far, grad_maps)
    through = mapped(panels[0], panels[1], grad_maps, True)
    lower, upper = [], []
    for k in range(FIELDS):
        b = jnp.where(plane, through[k], 0.0)
        lower.append(jnp.where(even, b, 0.0))
        upper.append(jnp.where(even, 0.0, b))
    rows = arrived_rows(flags, lower, upper)
    settle(adjoint, acc, keep, factor, pushed, psi)
    for k in range(FIELDS):
        for l in range(LAYERS):
            psi[k, l] = psi[k, l] - factor[l] * (from_strip(strip[k], l) + rows(k, l))
    transposed_terms(flags, psi, coefs, acc, strip, to_a, to_b, ghost)
    settle(psi, acc, keep, factor, pushed, base)


def advance(flags, base, strip, from_a, from_b, zone_a, near, far, maps, factor, out):
    through = mapped(near[...], far[...], maps, True)
    even = flagged(flags, B_EVEN, (8, LANES))
    plane = flagged(flags, PLANE, (8, LANES))
    sub = place_in_segment()
    whole, lower, upper = [], [], []
    for k in range(FIELDS):
        left, right = left_and_right(flags, from_a[k], from_b[k])
        right = jnp.where(sub < 8, pltpu.roll(right, LANES - 16, axis=1), 0.0)
        whole.append(strip[k] + jnp.where(sub >= 24, pltpu.roll(left, 16, axis=1), right))
        b = jnp.where(plane, through[k], near[k])
        a = zone_a[k]
        lower.append(jnp.where(even, b, a))
        upper.append(jnp.where(even, a, b))
    rows = arrived_rows(flags, lower, upper)
    for k in range(FIELDS):
        for l in range(LAYERS):
            out[k, l] = base[k, l] - factor[l] * (from_strip(whole[k], l) + rows(k, l))


def step_kernel(
    flags, base, strip, from_a, from_b, zone_a, near, far, maps, factor, keep, pushed,
    cm, ch, cs, xf, tf, lf, ln, base_out, strip_out, to_a, to_b, psi, acc, ghost,
):
    advance(flags, base, strip, from_a, from_b, zone_a, near, far, maps, factor, psi)
    transposed_terms(flags, psi, (cm, ch, cs, xf, tf, lf, ln), acc, strip_out, to_a, to_b, ghost)
    settle(psi, acc, keep, factor, pushed, base_out)


def last_kernel(flags, base, strip, from_a, from_b, zone_a, near, far, maps, factor, out):
    advance(flags, base, strip, from_a, from_b, zone_a, near, far, maps, factor, out)


def f32(*shape):
    return jax.ShapeDtypeStruct(shape, jnp.float32)


STATE = (FIELDS, LAYERS, ROWS, LANES)
STRIP = (FIELDS, ROWS, LANES)
PANEL = (FIELDS, 8, LANES)
SCALAR = (LAYERS, ROWS, LANES)
TERMS = (f32(*STATE), f32(*STRIP), f32(*PANEL), f32(*PANEL))
MAPS = (2, LANES, LANES)
FIXED = (f32(*SCALAR), f32(*SCALAR), f32(*STATE), f32(*MAPS))
FIRST = ((FIELDS, 24, LANES),) * 3
WORK = (STATE, STATE, (FIELDS, LAYERS, 8, LANES))
COEFS = (
    f32(CELLS, *SCALAR),
    f32(CELLS, LAYERS, 8, LANES),
    f32(CELLS, ROWS, LANES),
    f32(FACES, LAYERS, ROWS + 8, LANES),
    f32(FACES, LAYERS + 1, ROWS, LANES),
    f32(12, LAYERS + 1, ROWS, LANES),
    f32(2, LAYERS + 2, ROWS, LANES),
)


def call(kernel, outs, args, away=(), landing=(), work=(), name=None, grant=32):
    vmem = pl.BlockSpec(memory_space=pltpu.VMEM)
    smem = pl.BlockSpec(memory_space=pltpu.SMEM)
    there = pl.BlockSpec(memory_space=pltpu.HBM)
    return pl.pallas_call(
        kernel,
        out_shape=outs,
        in_specs=[smem] + [there if i in away else vmem for i in range(1, len(args))],
        out_specs=[vmem] * len(outs) if isinstance(outs, tuple) else vmem,
        scratch_shapes=[pltpu.VMEM(shape, jnp.float32) for shape in landing]
        + ([pltpu.SemaphoreType.DMA((len(landing),))] if landing else [])
        + [pltpu.VMEM(shape, jnp.float32) for shape in work],
        compiler_params=pltpu.CompilerParams(vmem_limit_bytes=grant * 1024 * 1024),
        name=name,
    )(*args)


def swaps(names, sectors, blocks, turn):
    half = blocks // 2
    assert half % 2 == 0
    where = {"sector": sectors, "block": blocks}
    minor = where[names[1]]

    def flat(b, s):
        first, second = (s, b) if names[0] == "sector" else (b, s)
        return first * minor + second

    sector_a, sector_b, block_a, near, far = [], [], [], [], []
    for b in range(blocks):
        for s in range(sectors):
            me = flat(b, s)
            sector_a.append((me, flat(b, s ^ 1)))
            sector_b.append((me, flat(b, (s + (1 if s % 2 else -1)) % sectors)))
            block_a.append((me, flat(b ^ 1, s)))
            if b == half - 1:
                near.append((me, flat(half, (s + turn) % sectors)))
                far.append((me, flat(half, (s + turn + 1) % sectors)))
            elif b == half:
                near.append((me, flat(half - 1, (s - turn) % sectors)))
                far.append((me, flat(half - 1, (s - turn - 1) % sectors)))
            else:
                other = b + 1 if b % 2 else b - 1
                near.append((me, flat(other, s) if 0 <= other < blocks else me))
                far.append((me, me))
    return sector_a, sector_b, block_a, near, far


def exchange(names, sectors, blocks, offset, strip, to_a, to_b):
    def branch(shift):
        sector_a, sector_b, block_a, near, far = swaps(names, sectors, blocks, shift)

        def run(strip, to_a, to_b):
            move = lambda x, pairs: lax.ppermute(x, names, pairs)
            return (
                move(strip, sector_a),
                move(strip, sector_b),
                move(to_a, block_a),
                move(to_b, near),
                move(to_b, far),
            )

        return run

    return lax.switch(offset, [branch(shift) for shift in range(sectors)], strip, to_a, to_b)


def shards(flow, adjoint, adjoint_later, objective_grad, volume, panel_maps, rotor_step, names):
    blocks = lax.axis_size("block")
    sectors = lax.axis_size("sector")
    place = lax.axis_index("block")
    half = blocks // 2
    stator = place >= half
    turn = rotor_step[0]
    offset = (turn // PHASES) % sectors
    flags = jnp.stack(
        [
            (lax.axis_index("sector") % 2 == 0).astype(jnp.int32),
            (place % 2 == 0).astype(jnp.int32),
            (place == 0).astype(jnp.int32),
            (place == blocks - 1).astype(jnp.int32),
            ((place == half) | (place == half - 1)).astype(jnp.int32),
            turn % PHASES,
            jnp.where(stator, 0, 2).astype(jnp.int32),
            jnp.where(stator, 2, 0).astype(jnp.int32),
        ]
    )
    send = partial(exchange, names, sectors, blocks, offset)
    packed = tuple(
        call(
            pack_kernel,
            tuple(f32(*shape) for shape in FIRST),
            (flags, flow, adjoint),
            name="pack",
        )
    )
    out = call(
        start_kernel,
        FIXED + TERMS + COEFS,
        (flags, flow, packed[0])
        + tuple(send(*packed))
        + (panel_maps, adjoint, adjoint_later, objective_grad, volume),
        range(8, 13),
        (MAPS, STATE, (2, *STATE), STATE, SCALAR, MAPS),
        WORK,
        name="start",
        grant=32,
    )
    (keep, factor, pushed, maps), terms, coefs = tuple(out[:4]), tuple(out[4:8]), tuple(out[8:])
    for sweep in range(1, ITERS):
        args = (flags,) + terms[:2] + tuple(send(*terms[1:])) + (maps, factor)
        if sweep == ITERS - 1:
            return call(last_kernel, f32(*STATE), args, name="last")
        terms = tuple(call(step_kernel, TERMS, args + (keep, pushed) + coefs, work=WORK, name="step"))


def solution(mesh):
    placed = (
        P(None, None, "block", "sector"),
        P(None, None, "block", "sector"),
        P(None, None, None, "block", "sector"),
        P(None, None, "block", "sector"),
        P(None, "block", "sector"),
        P(),
        P(),
    )
    return jax.shard_map(
        partial(shards, names=tuple(mesh.axis_names)),
        mesh=mesh,
        in_specs=placed,
        out_specs=P(None, None, "block", "sector"),
        check_vma=False,
    )
```

```python
from functools import partial

import jax
import jax.numpy as jnp
from jax import lax
from jax.experimental import pallas as pl
from jax.experimental.pallas import tpu as pltpu
from jax.sharding import PartitionSpec as P

PHASES = 4
ITERS = 4
LANES = 128
ROWS = 16
LAYERS = 4
FIELDS = 5
SEG = LANES // LAYERS

gamma_gas = 1.4
second_coef = 0.5
fourth_coef = 1.0 / 32.0
courant = 0.6
physical_step = 2.0
sensor_floor = 0.0001
highest = lax.Precision.HIGHEST

S_EVEN, B_EVEN, INLET, OUTLET, PLANE = range(5)
U1, U2, U3, HT, BX, BT, BL, CR, CP = range(9)
CELLS = 9
A2, A4, DL, ES, N0, N1 = 0, 1, 2, 7, 12, 13
FACES = 14


def up_by(x, axis, k):
    n = x.shape[axis]
    return pltpu.roll(x, (-k) % n, axis=axis)


def iota(shape, axis):
    return lax.broadcasted_iota(jnp.int32, shape, axis)


def flagged(flags, which, shape):
    return jnp.broadcast_to(flags[which], shape) == 1


def primitives(u):
    inverse = 1.0 / u[0]
    vel = [u[1] * inverse, u[2] * inverse, u[3] * inverse]
    square = vel[0] * vel[0] + vel[1] * vel[1] + vel[2] * vel[2]
    p = (gamma_gas - 1.0) * (u[4] - 0.5 * u[0] * square)
    heat = gamma_gas * p * inverse
    slow = lax.rsqrt(heat)
    sound = heat * slow
    radius, slopes = [], []
    for q in vel:
        x = q * q + 0.01
        y = lax.rsqrt(x)
        radius.append(x * y + sound)
        slopes.append(q * y * inverse)
    half = 0.5 * inverse
    cells = vel + [(u[4] + p) * inverse] + slopes + [sound * half, gamma_gas * half * slow]
    return p, radius, sound, cells


def sensor_terms(below, here, above):
    bend = above - 2.0 * here + below
    total = above + 2.0 * here + below
    inside = bend * bend + sensor_floor
    slope = lax.rsqrt(inside)
    over = 1.0 / total
    nu = inside * slope * over
    a = bend * slope * over
    b = nu * over
    return nu, -2.0 * a - 2.0 * b, a - b


def face_terms(nu_left, nu_right, rad_left, rad_right, behind, left, right, ahead):
    e2 = (0.5 * second_coef) * (nu_left + nu_right)
    ratio = fourth_coef / (fourth_coef + e2)
    e4 = fourth_coef * ratio
    slope = ratio * ratio
    lam = 0.5 * (rad_left + rad_right)
    radial, sensed = [], []
    for b, l, r, a in zip(behind, left, right, ahead):
        first = r - l
        third = a - 3.0 * first - b
        radial.append(-0.5 * (e2 * first - e4 * third))
        sensed.append((-0.25) * lam * (first + slope * third))
    return [lam * e2, lam * e4] + radial + sensed


def rolled_faces(u, p, radius, axis):
    nu, n0, n1 = sensor_terms(up_by(p, axis, -1), p, up_by(p, axis, 1))
    right = [up_by(x, axis, 1) for x in u]
    behind = [up_by(x, axis, -1) for x in u]
    ahead = [up_by(x, axis, 2) for x in u]
    return face_terms(
        nu, up_by(nu, axis, 1), radius, up_by(radius, axis, 1), behind, u, right, ahead
    ) + [n0, n1]


def dot5(a, b):
    return (a[0] * b[0] + a[1] * b[1]) + (a[2] * b[2] + a[3] * b[3]) + a[4] * b[4]


def to_state(lin, s, rbar, nbar, cells, direction):
    q = cells[direction]
    kappa = s[1] * cells[U1] + s[2] * cells[U2] + s[3] * cells[U3] + s[4] * cells[HT]
    kappa = kappa + cells[BX + direction] * rbar
    sq = s[4] * q
    pbar = nbar + sq + s[direction + 1] + cells[CP] * rbar
    scaled = (gamma_gas - 1.0) * pbar
    g = [None] * FIELDS
    square = cells[U1] * cells[U1] + cells[U2] * cells[U2] + cells[U3] * cells[U3]
    g[0] = lin[0] - q * kappa - cells[CR] * rbar + 0.5 * square * scaled
    for k in range(3):
        g[k + 1] = lin[k + 1] + q * s[k + 1] - cells[k] * scaled
    g[direction + 1] = g[direction + 1] + (s[0] + kappa)
    g[4] = lin[4] + sq + scaled
    return g


def rolled_transpose(psi, faces, cells, direction, axis, mask=None):
    w = [x - up_by(x, axis, 1) for x in psi]
    if mask is not None:
        w = [jnp.where(mask, x, 0.0) for x in w]
    gl = dot5(w, [faces(DL + k) for k in range(FIELDS)])
    ge = dot5(w, [faces(ES + k) for k in range(FIELDS)])
    a2, a4 = faces(A2), faces(A4)
    lin, s = [], []
    for x in w:
        c = a4 * x
        v = c - up_by(c, axis, -1)
        z = a2 * x + (v - up_by(v, axis, 1))
        lin.append(z - up_by(z, axis, -1))
        s.append(0.5 * (x + up_by(x, axis, -1)))
    rbar = gl + up_by(gl, axis, -1)
    nu_bar = ge + up_by(ge, axis, -1)
    v = faces(N1) * nu_bar
    nbar = faces(N0) * nu_bar + up_by(v, axis, 1) + up_by(v, axis, -1)
    return to_state(lin, s, rbar, nbar, cells, direction)


def packed_rows(tiles):
    row = iota((8, LANES), 0)
    out = tiles[0]
    for l in range(1, LAYERS):
        out = jnp.where(row >= 2 * l, pltpu.roll(tiles[l], 2 * l, axis=0), out)
    return out


def packed_quads(tiles):
    row = iota((8, LANES), 0)
    pairs = [
        jnp.where(row < 4, tiles[l], pltpu.roll(tiles[l + 1], 4, axis=0)) for l in range(0, LAYERS, 2)
    ]
    return jnp.concatenate(pairs, axis=0)


def quad(packed, l, high):
    tile = packed[8 * (l // 2) : 8 * (l // 2) + 8]
    return pltpu.roll(tile, 4, axis=0) if (l % 2 == 1) != high else tile


def pair(packed, l, to):
    shift = (to - 2 * l) % 8
    return pltpu.roll(packed, shift, axis=0) if shift else packed


def packed_strip(layers):
    lane = iota((ROWS, LANES), 1)
    out = jnp.zeros((ROWS, LANES), jnp.float32)
    for l, x in enumerate(layers):
        base = SEG * l
        out = jnp.where((lane >= base) & (lane < base + 8), pltpu.roll(x, (base + 8) % LANES, axis=1), out)
        out = jnp.where(
            (lane >= base + 24) & (lane < base + 32), pltpu.roll(x, (base + 24) % LANES, axis=1), out
        )
    return out


def packed_edges(layers, others):
    lane = iota((ROWS, LANES), 1)
    out = packed_strip(layers)
    for l, x in enumerate(others):
        base = SEG * l + 16
        out = jnp.where((lane >= base - 8) & (lane < base + 8), pltpu.roll(x, base, axis=1), out)
    return out


def from_strip(strip, l):
    lane = iota((ROWS, LANES), 1)
    base = SEG * l
    low = pltpu.roll(strip, (-(base + 24)) % LANES, axis=1)
    high = pltpu.roll(strip, (-(base + 8)) % LANES, axis=1)
    return jnp.where(lane < 8, low, jnp.where(lane >= LANES - 8, high, 0.0))


def place_in_segment():
    return jnp.bitwise_and(iota((ROWS, LANES), 1), SEG - 1)


def each(count, looped):
    def run(body):
        if looped:
            lax.fori_loop(0, count, lambda i, c: (body(i), c)[1], 0)
        else:
            for i in range(count):
                body(i)

    return run


def half_rows(half):
    return slice(8 * half, 8 * half + 8) if isinstance(half, int) else pl.ds(pl.multiple_of(8 * half, 8), 8)


def clamp(j):
    return min(max(j, 0), LAYERS - 1)


def pack_kernel(flags, flow, psi, to_t, to_a, to_b):
    even = flagged(flags, B_EVEN, (8, LANES))
    even2 = flagged(flags, B_EVEN, (16, LANES))
    for k in range(FIELDS):
        to_t[k, 0:16] = packed_edges([flow[k, l] for l in range(LAYERS)], [psi[k, l] for l in range(LAYERS)])
        low = packed_rows([flow[k, l, 0:8] for l in range(LAYERS)])
        high = packed_rows([pltpu.roll(flow[k, l, 8:16], 2, axis=0) for l in range(LAYERS)])
        to_t[k, 16:24] = jnp.where(even, low, high)
        low = packed_quads([flow[k, l, 0:8] for l in range(LAYERS)])
        high = packed_quads([pltpu.roll(flow[k, l, 8:16], 4, axis=0) for l in range(LAYERS)])
        to_a[k, 0:16] = jnp.where(even2, high, low)
        to_b[k, 0:16] = jnp.where(even2, low, high)
        low = packed_rows([psi[k, l, 0:8] for l in range(LAYERS)])
        high = packed_rows([pltpu.roll(psi[k, l, 8:16], 2, axis=0) for l in range(LAYERS)])
        to_a[k, 16:24] = jnp.where(even, high, low)
        to_b[k, 16:24] = jnp.where(even, low, high)


def mapped(near, far, maps):
    shape = near.shape
    dims = (((1,), (1,)), ((), ()))
    near = near.reshape(shape[0] * shape[1], LANES)
    far = far.reshape(shape[0] * shape[1], LANES)
    out = lax.dot_general(near, maps[0], dims, precision=highest, preferred_element_type=jnp.float32)
    out = out + lax.dot_general(far, maps[1], dims, precision=highest, preferred_element_type=jnp.float32)
    return out.reshape(shape)


def mapped_back(near, far, maps):
    shape = near.shape
    both = jnp.concatenate([near, far], axis=2).reshape(shape[0] * shape[1], 2 * LANES)
    table = maps[...].reshape(2 * LANES, LANES)
    out = jnp.dot(both, table, precision=highest, preferred_element_type=jnp.float32)
    return out.reshape(shape)


def left_and_right(flags, a, b):
    even = flagged(flags, S_EVEN, a.shape)
    return jnp.where(even, b, a), jnp.where(even, a, b)


def widened(flags, own, a, b):
    sub = place_in_segment()
    left, right = left_and_right(flags, a, b)
    x = jnp.where((sub >= 8) & (sub < 16), pltpu.roll(right, LANES - 16, axis=1), own)
    return jnp.where((sub >= 16) & (sub < 24), pltpu.roll(left, 16, axis=1), x)


def widened_other(flags, own, a, b):
    sub = place_in_segment()
    left, right = left_and_right(flags, a, b)
    low = pltpu.roll(jnp.where((sub >= 16) & (sub < 24), right, own), LANES - 8, axis=1)
    high = pltpu.roll(jnp.where((sub >= 8) & (sub < 16), left, own), 8, axis=1)
    return jnp.where(sub < 16, low, high)


def inner_coefficients(flow, cm, tf, lf, ln, shared):
    @each(LAYERS, True)
    def _(l):
        u = [flow[k, l] for k in range(FIELDS)]
        p, radius, _, cells = primitives(u)
        for i, x in enumerate(cells):
            cm[i, l] = x
        for i, x in enumerate([p] + radius):
            shared[i, l] = x
        for i, x in enumerate(rolled_faces(u, p, radius[1], 1)):
            tf[i, l] = x

    @each(2, True)
    def _(half):
        rows = half_rows(half)
        cell = [[flow[k, l, rows] for k in range(FIELDS)] for l in range(LAYERS)]
        pressure = [shared[0, l, rows] for l in range(LAYERS)]
        radius = [shared[3, l, rows] for l in range(LAYERS)]
        nus = {}
        for j in range(-1, LAYERS + 1):
            nu, n0, n1 = sensor_terms(*[pressure[clamp(j + d)] for d in (-1, 0, 1)])
            nus[j] = nu
            ln[0, j + 1, rows] = n0
            ln[1, j + 1, rows] = n1
        for f in range(-1, LAYERS):
            terms = face_terms(
                nus[f],
                nus[f + 1],
                radius[clamp(f)],
                radius[clamp(f + 1)],
                *[cell[clamp(f + d)] for d in (-1, 0, 1, 2)],
            )
            for i, x in enumerate(terms):
                lf[i, f + 1, rows] = x


def outer_coefficients(flags, flow, own, from_a, from_b, zone_a, near, far, maps, shared, ch, cs, xf, ts):
    through = mapped(near[:, 0:16], far[:, 0:16], maps)
    even = flagged(flags, B_EVEN, (16, LANES))
    plane = flagged(flags, PLANE, (16, LANES))
    row = iota((8, LANES), 0)
    inlet = flagged(flags, INLET, (8, LANES))
    outlet = flagged(flags, OUTLET, (8, LANES))
    lower, upper = [], []
    for k in range(FIELDS):
        b = jnp.where(plane, through[k], near[k, 0:16])
        a = zone_a[k, 0:16]
        lower.append(jnp.where(even, b, a))
        upper.append(jnp.where(even, a, b))
    for l in range(LAYERS):
        u, halo = [], []
        for k in range(FIELDS):
            main = flow[k, l]
            up = jnp.where(outlet, jnp.broadcast_to(main[15:16], (8, LANES)), quad(upper[k], l, False))
            low = jnp.where(inlet, jnp.broadcast_to(main[0:1], (8, LANES)), quad(lower[k], l, True))
            halo.append(jnp.where(row < 4, up, low))
            u.append(jnp.concatenate([main, halo[k]], axis=0))
        p, radius, _, cells = primitives(halo)
        for i, x in enumerate(cells):
            ch[i, l] = x
        p = jnp.concatenate([shared[0, l], p], axis=0)
        radius = jnp.concatenate([shared[1, l], radius[0]], axis=0)
        for i, x in enumerate(rolled_faces(u, p, radius, 0)):
            xf[i, l] = x
    u = [widened(flags, own[k], from_a[k, 0:16], from_b[k, 0:16]) for k in range(FIELDS)]
    p, radius, _, cells = primitives(u)
    for i, x in enumerate(cells):
        cs[i] = x
    for i, x in enumerate(rolled_faces(u, p, radius[1], 1)):
        ts[i] = x


def x_terms(flags, psi, halo, coefs, acc, ghost):
    cm, ch, _, xf, _ = coefs
    row = iota((8, LANES), 0)
    inlet = flagged(flags, INLET, (8, LANES)) & (row == 0)
    outlet = flagged(flags, OUTLET, (8, LANES)) & (row == 7)
    for l in range(LAYERS):
        wide = [jnp.concatenate([psi[k, l], halo(k, l)], axis=0) for k in range(FIELDS)]
        cells = [jnp.concatenate([cm[i, l], ch[i, l]], axis=0) for i in range(CELLS)]
        g = rolled_transpose(wide, lambda i: xf[i, l], cells, 0, 0)
        for k in range(FIELDS):
            out = g[k][16:]
            if ghost is not None:
                ghost[k, l] = out
            first = pltpu.roll(out, 2, axis=0) + pltpu.roll(out, 1, axis=0)
            last = pltpu.roll(out, 7, axis=0) + pltpu.roll(out, 6, axis=0)
            acc[k, l, 0:8] = g[k][0:8] + jnp.where(inlet, first, 0.0)
            acc[k, l, 8:16] = g[k][8:16] + jnp.where(outlet, last, 0.0)


def strip_terms(values, edges, coefs, strip):
    _, _, cs, _, ts = coefs
    g = rolled_transpose(values, lambda i: ts[i], [cs[i] for i in range(CELLS)], 1, 1, edges)
    for k in range(FIELDS):
        strip[k] = g[k]


def t_terms(psi, cm, tf, acc, looped):
    lane = iota((ROWS, LANES), 1)
    inner = (lane >= 1) & (lane < LANES - 2)

    @each(LAYERS, looped)
    def _(l):
        g = rolled_transpose(
            [psi[k, l] for k in range(FIELDS)],
            lambda i: tf[i, l],
            [cm[i, l] for i in range(CELLS)],
            1,
            1,
            inner,
        )
        for k in range(FIELDS):
            acc[k, l] = g[k]


def l_terms(psi, cm, lf, ln, acc, looped):
    last = LAYERS - 1

    @each(2, looped)
    def _(half):
        rows = half_rows(half)
        value = [[psi[k, l, rows] for k in range(FIELDS)] for l in range(LAYERS)]
        w, c, gl, ge = {}, {}, {}, {}
        for f in range(-1, LAYERS):
            if f < 0:
                w[f] = [-x for x in value[0]]
            elif f == last:
                w[f] = value[last]
            else:
                w[f] = [x - y for x, y in zip(value[f], value[f + 1])]
            gl[f] = dot5(w[f], [lf[DL + k, f + 1, rows] for k in range(FIELDS)])
            ge[f] = dot5(w[f], [lf[ES + k, f + 1, rows] for k in range(FIELDS)])
            a4 = lf[A4, f + 1, rows]
            c[f] = [a4 * x for x in w[f]]
        z = {}
        for f in range(last):
            a2 = lf[A2, f + 1, rows]
            z[f] = [a2 * w[f][k] + 2.0 * c[f][k] - c[f + 1][k] - c[f - 1][k] for k in range(FIELDS)]
        nbar = [None] * LAYERS
        for j in range(-1, LAYERS + 1):
            nu_bar = ge.get(j, 0.0) + ge.get(j - 1, 0.0)
            here = ln[0, j + 1, rows] * nu_bar
            side = ln[1, j + 1, rows] * nu_bar
            for to, x in ((j, here), (j - 1, side), (j + 1, side)):
                to = clamp(to)
                nbar[to] = x if nbar[to] is None else nbar[to] + x
        for j in range(LAYERS):
            if j == 0:
                s = [0.5 * w[0][k] + w[-1][k] for k in range(FIELDS)]
                lin = z[0]
                rbar = gl[0] + 2.0 * gl[-1]
            elif j == last:
                s = [0.5 * w[last - 1][k] + w[last][k] for k in range(FIELDS)]
                lin = [-x for x in z[last - 1]]
                rbar = gl[last - 1] + 2.0 * gl[last]
            else:
                s = [0.5 * (w[j][k] + w[j - 1][k]) for k in range(FIELDS)]
                lin = [z[j][k] - z[j - 1][k] for k in range(FIELDS)]
                rbar = gl[j] + gl[j - 1]
            g = to_state(lin, s, rbar, nbar[j], [cm[i, j, rows] for i in range(CELLS)], 2)
            for k in range(FIELDS):
                acc[k, j, rows] = acc[k, j, rows] + g[k]


def outer_terms(flags, psi, coefs, acc, strip, to_a, to_b, ghost):
    even = flagged(flags, B_EVEN, (8, LANES))
    empty = jnp.zeros((8, LANES), jnp.float32)
    x_terms(flags, psi, lambda k, l: empty, coefs, acc, ghost)
    for k in range(FIELDS):
        high = packed_rows([ghost[k, l] for l in range(LAYERS)])
        low = packed_rows([pltpu.roll(ghost[k, l], 2, axis=0) for l in range(LAYERS)])
        to_a[k] = jnp.where(even, high, low)
        to_b[k] = jnp.where(even, low, high)
    sub = place_in_segment()
    edges = ((sub >= 6) & (sub < 8)) | ((sub >= 23) & (sub < 25))
    values = [packed_strip([psi[k, l] for l in range(LAYERS)]) for k in range(FIELDS)]
    strip_terms(values, edges, coefs, strip)


def settle(psi, outer, inner, keep, factor, pushed, base, looped):
    @each(LAYERS, looped)
    def _(l):
        for k in range(FIELDS):
            total = inner[k, l] if outer is None else outer[k, l] + inner[k, l]
            base[k, l] = psi[k, l] * keep[l] - factor[l] * total + pushed[k, l]


def arrived_rows(flags, lower, upper):
    row = iota((8, LANES), 0)
    first = (row < 2) & jnp.logical_not(flagged(flags, INLET, (8, LANES)))
    last = (row >= 6) & jnp.logical_not(flagged(flags, OUTLET, (8, LANES)))

    def rows(k, l):
        low = jnp.where(first, pair(lower[k], l, 0), 0.0)
        high = jnp.where(last, pair(upper[k], l, 6), 0.0)
        return jnp.concatenate([low, high], axis=0)

    return rows


def facing_gradients(flags, flow, from_a, from_b, near, far, maps):
    rotor = jnp.logical_not(flagged(flags, B_EVEN, (8, LANES)))
    row = iota((8, LANES), 0)
    panel = []
    for k in range(FIELDS):
        low = packed_rows([flow[k, l, 0:8] for l in range(LAYERS)])
        high = packed_rows([pltpu.roll(flow[k, l, 8:16], 2, axis=0) for l in range(LAYERS)])
        panel.append(jnp.where(rotor, high, low))
    panel = jnp.stack(panel)
    first, second = [], []
    for k in range(FIELDS):
        left, right = left_and_right(flags, from_a[k, 16:24], from_b[k, 16:24])
        first.append(jnp.where(rotor, left, right))
        second.append(jnp.where(rotor, right, left))
    ghosts = (
        mapped(panel, jnp.stack(first), maps),
        mapped(jnp.stack(second), panel, maps),
    )
    kept = (row == 7) | (rotor & (row == 0)) | (jnp.logical_not(rotor) & (row == 6))
    out = []
    for ghost, facing in zip(ghosts, (near, far)):
        layers = []
        for l in range(LAYERS):
            u, psi = [], []
            for k in range(FIELDS):
                cells = facing[k, 0:16]
                below = pair(ghost[k], l, 6)
                above = pair(ghost[k], l, 0)
                as_rotor = jnp.where(
                    row < 4,
                    quad(cells, l, False),
                    jnp.where(row < 6, pltpu.roll(below, 6, axis=0), below),
                )
                as_stator = jnp.where(
                    row < 2,
                    above,
                    jnp.where(row < 4, pltpu.roll(above, 2, axis=0), quad(cells, l, True)),
                )
                u.append(jnp.where(rotor, as_rotor, as_stator))
                value = facing[k, 16:24]
                psi.append(
                    jnp.where(
                        rotor,
                        jnp.where(row < 2, pair(value, l, 0), 0.0),
                        jnp.where(row >= 6, pair(value, l, 6), 0.0),
                    )
                )
            p, radius, _, cells = primitives(u)
            faces = rolled_faces(u, p, radius[0], 0)
            g = rolled_transpose(psi, lambda i: faces[i], cells, 0, 0, kept)
            layers.append([jnp.where(rotor, pltpu.roll(x, 2, axis=0), x) for x in g])
        out.append(jnp.stack([packed_rows([layers[l][k] for l in range(LAYERS)]) for k in range(FIELDS)]))
    return out


def prepare_kernel(
    flags, flow, adjoint, later, gradient, volume,
    keep, factor, pushed, own, base, cm, tf, lf, ln, shared, acc,
):
    inner_coefficients(flow, cm, tf, lf, ln, shared)

    @each(LAYERS, True)
    def _(l):
        vol = volume[l]
        radius_sum = shared[1, l] + shared[2, l] + shared[3, l]
        f = courant / (radius_sum + (1.5 * courant / physical_step) * vol)
        factor[l] = f
        keep[l] = 1.0 - f * ((1.5 / physical_step) * vol)
        for k in range(FIELDS):
            source = gradient[k, l] + vol * (2.0 * later[0, k, l] - 0.5 * later[1, k, l]) / physical_step
            pushed[k, l] = f * source

    @each(FIELDS, True)
    def _(k):
        own[k] = packed_edges([flow[k, l] for l in range(LAYERS)], [adjoint[k, l] for l in range(LAYERS)])

    t_terms(adjoint, cm, tf, acc, True)
    l_terms(adjoint, cm, lf, ln, acc, True)
    settle(adjoint, None, acc, keep, factor, pushed, base, True)


def start_kernel(
    flags, flow, adjoint, from_a, from_b, zone_a, near, far, state_maps, grad_maps, factor, own, base, cm, shared,
    psi, acc, strip, to_a, to_b, ch, cs, xf, ts, ghost,
):
    coefs = (cm, ch, cs, xf, ts)
    outer_coefficients(flags, flow, own, from_a, from_b, zone_a, near, far, state_maps, shared, ch, cs, xf, ts)
    even = flagged(flags, B_EVEN, (8, LANES))
    plane = flagged(flags, PLANE, (8, LANES))
    row = iota((8, LANES), 0)
    use_upper = (row < 2) & jnp.logical_not(flagged(flags, OUTLET, (8, LANES)))
    use_lower = (row >= 6) & jnp.logical_not(flagged(flags, INLET, (8, LANES)))

    def halo(k, l):
        a = zone_a[k, 16:24]
        b = jnp.where(plane, 0.0, near[k, 16:24])
        upper = pair(jnp.where(even, a, b), l, 0)
        lower = pair(jnp.where(even, b, a), l, 6)
        return jnp.where(use_upper, upper, jnp.where(use_lower, lower, 0.0))

    x_terms(flags, adjoint, halo, coefs, acc, None)
    sub = place_in_segment()
    edges = ((sub >= 6) & (sub < 9)) | ((sub >= 22) & (sub < 25))
    values = [widened_other(flags, own[k], from_a[k, 0:16], from_b[k, 0:16]) for k in range(FIELDS)]
    strip_terms(values, edges, coefs, strip)
    panels = facing_gradients(flags, flow, from_a, from_b, near, far, grad_maps)
    through = mapped_back(panels[0], panels[1], grad_maps)
    lower, upper = [], []
    for k in range(FIELDS):
        b = jnp.where(plane, through[k], 0.0)
        lower.append(jnp.where(even, b, 0.0))
        upper.append(jnp.where(even, 0.0, b))
    rows = arrived_rows(flags, lower, upper)
    for k in range(FIELDS):
        for l in range(LAYERS):
            total = acc[k, l] + from_strip(strip[k], l) + rows(k, l)
            psi[k, l] = base[k, l] - factor[l] * total
    outer_terms(flags, psi, coefs, acc, strip, to_a, to_b, ghost)


def inner_kernel(flags, psi, outer, keep, factor, pushed, cm, tf, lf, ln, base, acc):
    t_terms(psi, cm, tf, acc, False)
    l_terms(psi, cm, lf, ln, acc, False)
    settle(psi, outer, acc, keep, factor, pushed, base, False)


def advance(flags, base, strip, from_a, from_b, zone_a, near, far, maps, factor, out):
    through = mapped_back(near[...], far[...], maps)
    even = flagged(flags, B_EVEN, (8, LANES))
    plane = flagged(flags, PLANE, (8, LANES))
    sub = place_in_segment()
    whole, lower, upper = [], [], []
    for k in range(FIELDS):
        left, right = left_and_right(flags, from_a[k], from_b[k])
        right = jnp.where(sub < 8, pltpu.roll(right, LANES - 16, axis=1), 0.0)
        whole.append(strip[k] + jnp.where(sub >= 24, pltpu.roll(left, 16, axis=1), right))
        b = jnp.where(plane, through[k], near[k])
        a = zone_a[k]
        lower.append(jnp.where(even, b, a))
        upper.append(jnp.where(even, a, b))
    rows = arrived_rows(flags, lower, upper)
    for k in range(FIELDS):
        for l in range(LAYERS):
            out[k, l] = base[k, l] - factor[l] * (from_strip(whole[k], l) + rows(k, l))


def step_kernel(
    flags, base, strip, from_a, from_b, zone_a, near, far, maps, factor, cm, ch, cs, xf, ts,
    psi, acc, strip_out, to_a, to_b, ghost,
):
    advance(flags, base, strip, from_a, from_b, zone_a, near, far, maps, factor, psi)
    outer_terms(flags, psi, (cm, ch, cs, xf, ts), acc, strip_out, to_a, to_b, ghost)


def last_kernel(flags, base, strip, from_a, from_b, zone_a, near, far, maps, factor, out):
    advance(flags, base, strip, from_a, from_b, zone_a, near, far, maps, factor, out)


def f32(*shape):
    return jax.ShapeDtypeStruct(shape, jnp.float32)


STATE = (FIELDS, LAYERS, ROWS, LANES)
STRIP = (FIELDS, ROWS, LANES)
PANEL = (FIELDS, 8, LANES)
SCALAR = (LAYERS, ROWS, LANES)
FIRST = ((FIELDS, 24, LANES),) * 3
MAPS = (2, LANES, LANES)
GHOST = (FIELDS, LAYERS, 8, LANES)
TERMS = (f32(*STATE), f32(*STATE), f32(*STRIP), f32(*PANEL), f32(*PANEL))
FIXED = (f32(*SCALAR), f32(*SCALAR), f32(*STATE))
INNER = (
    f32(CELLS, *SCALAR),
    f32(FACES, *SCALAR),
    f32(12, LAYERS + 1, ROWS, LANES),
    f32(2, LAYERS + 2, ROWS, LANES),
)
SHARED = f32(4, *SCALAR)
OUTER = (
    f32(CELLS, LAYERS, 8, LANES),
    f32(CELLS, ROWS, LANES),
    f32(FACES, LAYERS, ROWS + 8, LANES),
    f32(FACES, ROWS, LANES),
)


def call(kernel, outs, args, work=(), name=None, in_place=None):
    vmem = pl.BlockSpec(memory_space=pltpu.VMEM)
    smem = pl.BlockSpec(memory_space=pltpu.SMEM)
    return pl.pallas_call(
        kernel,
        out_shape=outs,
        in_specs=[smem] + [vmem] * (len(args) - 1),
        out_specs=[vmem] * len(outs) if isinstance(outs, tuple) else vmem,
        scratch_shapes=[pltpu.VMEM(shape, jnp.float32) for shape in work],
        compiler_params=pltpu.CompilerParams(vmem_limit_bytes=32 * 1024 * 1024),
        input_output_aliases=in_place or {},
        name=name,
    )(*args)


def swaps(names, sectors, blocks, turn):
    half = blocks // 2
    assert half % 2 == 0
    where = {"sector": sectors, "block": blocks}
    minor = where[names[1]]

    def flat(b, s):
        first, second = (s, b) if names[0] == "sector" else (b, s)
        return first * minor + second

    sector_a, sector_b, block_a, near, far = [], [], [], [], []
    for b in range(blocks):
        for s in range(sectors):
            me = flat(b, s)
            sector_a.append((me, flat(b, s ^ 1)))
            sector_b.append((me, flat(b, (s + (1 if s % 2 else -1)) % sectors)))
            block_a.append((me, flat(b ^ 1, s)))
            if b == half - 1:
                near.append((me, flat(half, (s + turn) % sectors)))
                far.append((me, flat(half, (s + turn + 1) % sectors)))
            elif b == half:
                near.append((me, flat(half - 1, (s - turn) % sectors)))
                far.append((me, flat(half - 1, (s - turn - 1) % sectors)))
            else:
                other = b + 1 if b % 2 else b - 1
                near.append((me, flat(other, s) if 0 <= other < blocks else me))
                far.append((me, me))
    return sector_a, sector_b, block_a, near, far


def exchange(names, sectors, blocks, offset, strip, to_a, to_b, beside=None, args=()):
    def branch(shift):
        sector_a, sector_b, block_a, near, far = swaps(names, sectors, blocks, shift)

        def run(strip, to_a, to_b, *args):
            move = lambda x, pairs: lax.ppermute(x, names, pairs)
            moved = (
                move(strip, sector_a),
                move(strip, sector_b),
                move(to_a, block_a),
                move(to_b, near),
                move(to_b, far),
            )
            return moved if beside is None else moved + tuple(beside(*args))

        return run

    return tuple(
        lax.switch(offset, [branch(shift) for shift in range(sectors)], strip, to_a, to_b, *args)
    )


def first_beside(flags, panel_maps, phase, start, *arrays):
    def map_pair(at):
        begin = (phase, at, jnp.zeros_like(phase), jnp.zeros_like(phase))
        return lax.dynamic_slice(panel_maps, begin, (1, 2, LANES, LANES))[0]

    prepared = call(
        prepare_kernel,
        FIXED + (f32(*STRIP), f32(*STATE)) + INNER + (SHARED,),
        (flags, *arrays),
        (STATE,),
        name="prepare",
    )
    return (map_pair(start), map_pair(2 - start), *prepared)


def next_beside(*args):
    return (call(inner_kernel, f32(*STATE), args, (STATE,), name="inner", in_place={2: 0}),)


def shards(flow, adjoint, adjoint_later, objective_grad, volume, panel_maps, rotor_step, names):
    blocks = lax.axis_size("block")
    sectors = lax.axis_size("sector")
    place = lax.axis_index("block")
    half = blocks // 2
    stator = place >= half
    turn = rotor_step[0]
    offset = (turn // PHASES) % sectors
    flags = jnp.stack(
        [
            (lax.axis_index("sector") % 2 == 0).astype(jnp.int32),
            (place % 2 == 0).astype(jnp.int32),
            (place == 0).astype(jnp.int32),
            (place == blocks - 1).astype(jnp.int32),
            ((place == half) | (place == half - 1)).astype(jnp.int32),
            (place < 0).astype(jnp.int32),
            (place < 0).astype(jnp.int32),
            (place < 0).astype(jnp.int32),
        ]
    )
    send = partial(exchange, names, sectors, blocks, offset)
    packed = tuple(
        call(
            pack_kernel,
            tuple(f32(*shape) for shape in FIRST),
            (flags, flow, adjoint),
            name="pack",
        )
    )
    arrived = send(
        *packed,
        beside=first_beside,
        args=(
            flags,
            panel_maps,
            turn % PHASES,
            jnp.where(stator, 0, 2).astype(jnp.int32),
            flow,
            adjoint,
            adjoint_later,
            objective_grad,
            volume,
        ),
    )
    (state_maps, maps, keep, factor, pushed, own, base), inner, shared = arrived[5:12], arrived[12:16], arrived[16]
    cm = inner[0]
    out = call(
        start_kernel,
        TERMS + OUTER,
        (flags, flow, adjoint) + arrived[:5] + (state_maps, maps, factor, own, base, cm, shared),
        (GHOST,),
        name="start",
    )
    terms, outer = tuple(out[:5]), tuple(out[5:])
    for sweep in range(1, ITERS):
        psi, acc, strip, to_a, to_b = terms
        arrived = send(
            strip, to_a, to_b, beside=next_beside, args=(flags, psi, acc, keep, factor, pushed) + inner
        )
        args = (flags, arrived[5], strip) + arrived[:5] + (maps, factor)
        if sweep == ITERS - 1:
            return call(last_kernel, f32(*STATE), args, name="last")
        terms = tuple(call(step_kernel, TERMS, args + (cm,) + outer, (GHOST,), name="step"))


def solution(mesh):
    placed = (
        P(None, None, "block", "sector"),
        P(None, None, "block", "sector"),
        P(None, None, None, "block", "sector"),
        P(None, None, "block", "sector"),
        P(None, "block", "sector"),
        P(),
        P(),
    )
    return jax.shard_map(
        partial(shards, names=tuple(mesh.axis_names)),
        mesh=mesh,
        in_specs=placed,
        out_specs=P(None, None, "block", "sector"),
        check_vma=False,
    )
```

```python
from functools import partial

import jax
import jax.numpy as jnp
from jax import lax
from jax.experimental import pallas as pl
from jax.experimental.pallas import tpu as pltpu
from jax.sharding import PartitionSpec as P

PHASES = 4
ITERS = 4
LANES = 128
ROWS = 16
LAYERS = 4
FIELDS = 5
SEG = LANES // LAYERS

gamma_gas = 1.4
second_coef = 0.5
fourth_coef = 1.0 / 32.0
courant = 0.6
physical_step = 2.0
sensor_floor = 0.0001
highest = lax.Precision.HIGHEST

S_EVEN, B_EVEN, INLET, OUTLET, PLANE, PHASE, STATE_MAPS, GRAD_MAPS = range(8)
U1, U2, U3, HT, BX, BT, BL, CR, CP = range(9)
CELLS = 9
A2, A4, DL, ES, N0, N1 = 0, 1, 2, 7, 12, 13
FACES = 14


def up_by(x, axis, k):
    n = x.shape[axis]
    return pltpu.roll(x, (-k) % n, axis=axis)


def iota(shape, axis):
    return lax.broadcasted_iota(jnp.int32, shape, axis)


def flagged(flags, which, shape):
    return jnp.broadcast_to(flags[which], shape) == 1


def primitives(u):
    inverse = 1.0 / u[0]
    vel = [u[1] * inverse, u[2] * inverse, u[3] * inverse]
    square = vel[0] * vel[0] + vel[1] * vel[1] + vel[2] * vel[2]
    p = (gamma_gas - 1.0) * (u[4] - 0.5 * u[0] * square)
    heat = gamma_gas * p * inverse
    slow = lax.rsqrt(heat)
    sound = heat * slow
    radius, slopes = [], []
    for q in vel:
        x = q * q + 0.01
        y = lax.rsqrt(x)
        radius.append(x * y + sound)
        slopes.append(q * y * inverse)
    half = 0.5 * inverse
    cells = vel + [(u[4] + p) * inverse] + slopes + [sound * half, gamma_gas * half * slow]
    return p, radius, sound, cells


def sensor_terms(below, here, above):
    bend = above - 2.0 * here + below
    total = above + 2.0 * here + below
    inside = bend * bend + sensor_floor
    slope = lax.rsqrt(inside)
    over = 1.0 / total
    nu = inside * slope * over
    a = bend * slope * over
    b = nu * over
    return nu, -2.0 * a - 2.0 * b, a - b


def face_terms(nu_left, nu_right, rad_left, rad_right, behind, left, right, ahead):
    e2 = (0.5 * second_coef) * (nu_left + nu_right)
    ratio = fourth_coef / (fourth_coef + e2)
    e4 = fourth_coef * ratio
    slope = ratio * ratio
    lam = 0.5 * (rad_left + rad_right)
    radial, sensed = [], []
    for b, l, r, a in zip(behind, left, right, ahead):
        first = r - l
        third = a - 3.0 * first - b
        radial.append(-0.5 * (e2 * first - e4 * third))
        sensed.append((-0.25) * lam * (first + slope * third))
    return [lam * e2, lam * e4] + radial + sensed


def rolled_faces(u, p, radius, axis):
    nu, n0, n1 = sensor_terms(up_by(p, axis, -1), p, up_by(p, axis, 1))
    right = [up_by(x, axis, 1) for x in u]
    behind = [up_by(x, axis, -1) for x in u]
    ahead = [up_by(x, axis, 2) for x in u]
    return face_terms(
        nu, up_by(nu, axis, 1), radius, up_by(radius, axis, 1), behind, u, right, ahead
    ) + [n0, n1]


def dot5(a, b):
    return (a[0] * b[0] + a[1] * b[1]) + (a[2] * b[2] + a[3] * b[3]) + a[4] * b[4]


def to_state(lin, s, rbar, nbar, cells, direction):
    q = cells[direction]
    kappa = s[1] * cells[U1] + s[2] * cells[U2] + s[3] * cells[U3] + s[4] * cells[HT]
    kappa = kappa + cells[BX + direction] * rbar
    sq = s[4] * q
    pbar = nbar + sq + s[direction + 1] + cells[CP] * rbar
    scaled = (gamma_gas - 1.0) * pbar
    g = [None] * FIELDS
    square = cells[U1] * cells[U1] + cells[U2] * cells[U2] + cells[U3] * cells[U3]
    g[0] = lin[0] - q * kappa - cells[CR] * rbar + 0.5 * square * scaled
    for k in range(3):
        g[k + 1] = lin[k + 1] + q * s[k + 1] - cells[k] * scaled
    g[direction + 1] = g[direction + 1] + (s[0] + kappa)
    g[4] = lin[4] + sq + scaled
    return g


def rolled_transpose(psi, faces, cells, direction, axis, mask=None):
    w = [x - up_by(x, axis, 1) for x in psi]
    if mask is not None:
        w = [jnp.where(mask, x, 0.0) for x in w]
    gl = dot5(w, [faces(DL + k) for k in range(FIELDS)])
    ge = dot5(w, [faces(ES + k) for k in range(FIELDS)])
    a2, a4 = faces(A2), faces(A4)
    lin, s = [], []
    for x in w:
        c = a4 * x
        v = c - up_by(c, axis, -1)
        z = a2 * x + (v - up_by(v, axis, 1))
        lin.append(z - up_by(z, axis, -1))
        s.append(0.5 * (x + up_by(x, axis, -1)))
    rbar = gl + up_by(gl, axis, -1)
    nu_bar = ge + up_by(ge, axis, -1)
    v = faces(N1) * nu_bar
    nbar = faces(N0) * nu_bar + up_by(v, axis, 1) + up_by(v, axis, -1)
    return to_state(lin, s, rbar, nbar, cells, direction)


def packed_rows(tiles):
    row = iota((8, LANES), 0)
    out = tiles[0]
    for l in range(1, LAYERS):
        out = jnp.where(row >= 2 * l, pltpu.roll(tiles[l], 2 * l, axis=0), out)
    return out


def packed_quads(tiles):
    row = iota((8, LANES), 0)
    pairs = [
        jnp.where(row < 4, tiles[l], pltpu.roll(tiles[l + 1], 4, axis=0)) for l in range(0, LAYERS, 2)
    ]
    return jnp.concatenate(pairs, axis=0)


def quad(packed, l, high):
    tile = packed[8 * (l // 2) : 8 * (l // 2) + 8]
    return pltpu.roll(tile, 4, axis=0) if (l % 2 == 1) != high else tile


def pair(packed, l, to):
    shift = (to - 2 * l) % 8
    return pltpu.roll(packed, shift, axis=0) if shift else packed


def packed_strip(layers):
    lane = iota((ROWS, LANES), 1)
    out = jnp.zeros((ROWS, LANES), jnp.float32)
    for l, x in enumerate(layers):
        base = SEG * l
        out = jnp.where((lane >= base) & (lane < base + 8), pltpu.roll(x, (base + 8) % LANES, axis=1), out)
        out = jnp.where(
            (lane >= base + 24) & (lane < base + 32), pltpu.roll(x, (base + 24) % LANES, axis=1), out
        )
    return out


def packed_edges(layers, others):
    lane = iota((ROWS, LANES), 1)
    out = packed_strip(layers)
    for l, x in enumerate(others):
        base = SEG * l + 16
        out = jnp.where((lane >= base - 8) & (lane < base + 8), pltpu.roll(x, base, axis=1), out)
    return out


def from_strip(strip, l):
    lane = iota((ROWS, LANES), 1)
    base = SEG * l
    low = pltpu.roll(strip, (-(base + 24)) % LANES, axis=1)
    high = pltpu.roll(strip, (-(base + 8)) % LANES, axis=1)
    return jnp.where(lane < 8, low, jnp.where(lane >= LANES - 8, high, 0.0))


def place_in_segment():
    return jnp.bitwise_and(iota((ROWS, LANES), 1), SEG - 1)


def each(count, looped):
    def run(body):
        if looped:
            lax.fori_loop(0, count, lambda i, c: (body(i), c)[1], 0)
        else:
            for i in range(count):
                body(i)

    return run


def half_rows(half):
    return slice(8 * half, 8 * half + 8) if isinstance(half, int) else pl.ds(pl.multiple_of(8 * half, 8), 8)


def clamp(j):
    return min(max(j, 0), LAYERS - 1)


def pack_kernel(flags, flow, psi, to_t, to_a, to_b):
    even = flagged(flags, B_EVEN, (8, LANES))
    even2 = flagged(flags, B_EVEN, (16, LANES))
    for k in range(FIELDS):
        to_t[k, 0:16] = packed_edges([flow[k, l] for l in range(LAYERS)], [psi[k, l] for l in range(LAYERS)])
        low = packed_rows([flow[k, l, 0:8] for l in range(LAYERS)])
        high = packed_rows([pltpu.roll(flow[k, l, 8:16], 2, axis=0) for l in range(LAYERS)])
        to_t[k, 16:24] = jnp.where(even, low, high)
        low = packed_quads([flow[k, l, 0:8] for l in range(LAYERS)])
        high = packed_quads([pltpu.roll(flow[k, l, 8:16], 4, axis=0) for l in range(LAYERS)])
        to_a[k, 0:16] = jnp.where(even2, high, low)
        to_b[k, 0:16] = jnp.where(even2, low, high)
        low = packed_rows([psi[k, l, 0:8] for l in range(LAYERS)])
        high = packed_rows([pltpu.roll(psi[k, l, 8:16], 2, axis=0) for l in range(LAYERS)])
        to_a[k, 16:24] = jnp.where(even, high, low)
        to_b[k, 16:24] = jnp.where(even, low, high)


def mapped(near, far, maps):
    shape = near.shape
    dims = (((1,), (1,)), ((), ()))
    near = near.reshape(shape[0] * shape[1], LANES)
    far = far.reshape(shape[0] * shape[1], LANES)
    out = lax.dot_general(near, maps[0], dims, precision=highest, preferred_element_type=jnp.float32)
    out = out + lax.dot_general(far, maps[1], dims, precision=highest, preferred_element_type=jnp.float32)
    return out.reshape(shape)


def mapped_back(near, far, maps):
    shape = near.shape
    both = jnp.concatenate([near, far], axis=2).reshape(shape[0] * shape[1], 2 * LANES)
    table = maps[...].reshape(2 * LANES, LANES)
    out = jnp.dot(both, table, precision=highest, preferred_element_type=jnp.float32)
    return out.reshape(shape)


def left_and_right(flags, a, b):
    even = flagged(flags, S_EVEN, a.shape)
    return jnp.where(even, b, a), jnp.where(even, a, b)


def widened(flags, own, a, b):
    sub = place_in_segment()
    left, right = left_and_right(flags, a, b)
    x = jnp.where((sub >= 8) & (sub < 16), pltpu.roll(right, LANES - 16, axis=1), own)
    return jnp.where((sub >= 16) & (sub < 24), pltpu.roll(left, 16, axis=1), x)


def widened_other(flags, own, a, b):
    sub = place_in_segment()
    left, right = left_and_right(flags, a, b)
    low = pltpu.roll(jnp.where((sub >= 16) & (sub < 24), right, own), LANES - 8, axis=1)
    high = pltpu.roll(jnp.where((sub >= 8) & (sub < 16), left, own), 8, axis=1)
    return jnp.where(sub < 16, low, high)


def inner_coefficients(flow, cm, tf, lf, ln, shared, radii, at_cell):
    @each(LAYERS, True)
    def _(l):
        u = [flow[k, l] for k in range(FIELDS)]
        p, radius, _, cells = primitives(u)
        for i, x in enumerate(cells):
            cm[i, l] = x
        shared[0, l] = p
        shared[1, l] = radius[0]
        radii[l] = radius[2]
        at_cell(l, radius[0] + radius[1] + radius[2])
        for i, x in enumerate(rolled_faces(u, p, radius[1], 1)):
            tf[i, l] = x

    @each(2, True)
    def _(half):
        rows = half_rows(half)
        cell = [[flow[k, l, rows] for k in range(FIELDS)] for l in range(LAYERS)]
        pressure = [shared[0, l, rows] for l in range(LAYERS)]
        radius = [radii[l, rows] for l in range(LAYERS)]
        nus = {}
        for j in range(-1, LAYERS + 1):
            nu, n0, n1 = sensor_terms(*[pressure[clamp(j + d)] for d in (-1, 0, 1)])
            nus[j] = nu
            ln[0, j + 1, rows] = n0
            ln[1, j + 1, rows] = n1
        for f in range(-1, LAYERS):
            terms = face_terms(
                nus[f],
                nus[f + 1],
                radius[clamp(f)],
                radius[clamp(f + 1)],
                *[cell[clamp(f + d)] for d in (-1, 0, 1, 2)],
            )
            for i, x in enumerate(terms):
                lf[i, f + 1, rows] = x


def outer_coefficients(flags, flow, own, from_a, from_b, zone_a, near, far, maps, shared, ch, cs, xf, ts):
    through = mapped(near[:, 0:16], far[:, 0:16], maps)
    even = flagged(flags, B_EVEN, (16, LANES))
    plane = flagged(flags, PLANE, (16, LANES))
    row = iota((8, LANES), 0)
    inlet = flagged(flags, INLET, (8, LANES))
    outlet = flagged(flags, OUTLET, (8, LANES))
    lower, upper = [], []
    for k in range(FIELDS):
        b = jnp.where(plane, through[k], near[k, 0:16])
        a = zone_a[k, 0:16]
        lower.append(jnp.where(even, b, a))
        upper.append(jnp.where(even, a, b))
    for l in range(LAYERS):
        u, halo = [], []
        for k in range(FIELDS):
            main = flow[k, l]
            up = jnp.where(outlet, jnp.broadcast_to(main[15:16], (8, LANES)), quad(upper[k], l, False))
            low = jnp.where(inlet, jnp.broadcast_to(main[0:1], (8, LANES)), quad(lower[k], l, True))
            halo.append(jnp.where(row < 4, up, low))
            u.append(jnp.concatenate([main, halo[k]], axis=0))
        p, radius, _, cells = primitives(halo)
        for i, x in enumerate(cells):
            ch[i, l] = x
        p = jnp.concatenate([shared[0, l], p], axis=0)
        radius = jnp.concatenate([shared[1, l], radius[0]], axis=0)
        for i, x in enumerate(rolled_faces(u, p, radius, 0)):
            xf[i, l] = x
    u = [widened(flags, own[k], from_a[k, 0:16], from_b[k, 0:16]) for k in range(FIELDS)]
    p, radius, _, cells = primitives(u)
    for i, x in enumerate(cells):
        cs[i] = x
    for i, x in enumerate(rolled_faces(u, p, radius[1], 1)):
        ts[i] = x


def x_terms(flags, psi, halo, coefs, acc, ghost):
    cm, ch, _, xf, _ = coefs
    row = iota((8, LANES), 0)
    inlet = flagged(flags, INLET, (8, LANES)) & (row == 0)
    outlet = flagged(flags, OUTLET, (8, LANES)) & (row == 7)
    for l in range(LAYERS):
        wide = [jnp.concatenate([psi[k, l], halo(k, l)], axis=0) for k in range(FIELDS)]
        cells = [jnp.concatenate([cm[i, l], ch[i, l]], axis=0) for i in range(CELLS)]
        g = rolled_transpose(wide, lambda i: xf[i, l], cells, 0, 0)
        for k in range(FIELDS):
            out = g[k][16:]
            if ghost is not None:
                ghost[k, l] = out
            first = pltpu.roll(out, 2, axis=0) + pltpu.roll(out, 1, axis=0)
            last = pltpu.roll(out, 7, axis=0) + pltpu.roll(out, 6, axis=0)
            acc[k, l, 0:8] = g[k][0:8] + jnp.where(inlet, first, 0.0)
            acc[k, l, 8:16] = g[k][8:16] + jnp.where(outlet, last, 0.0)


def strip_terms(values, edges, coefs, strip):
    _, _, cs, _, ts = coefs
    g = rolled_transpose(values, lambda i: ts[i], [cs[i] for i in range(CELLS)], 1, 1, edges)
    for k in range(FIELDS):
        strip[k] = g[k]


def t_terms(psi, cm, tf, acc, looped):
    lane = iota((ROWS, LANES), 1)
    inner = (lane >= 1) & (lane < LANES - 2)

    @each(LAYERS, looped)
    def _(l):
        g = rolled_transpose(
            [psi[k, l] for k in range(FIELDS)],
            lambda i: tf[i, l],
            [cm[i, l] for i in range(CELLS)],
            1,
            1,
            inner,
        )
        for k in range(FIELDS):
            acc[k, l] = g[k]


def l_terms(psi, cm, lf, ln, acc, looped):
    last = LAYERS - 1

    @each(2, looped)
    def _(half):
        rows = half_rows(half)
        value = [[psi[k, l, rows] for k in range(FIELDS)] for l in range(LAYERS)]
        w, c, gl, ge = {}, {}, {}, {}
        for f in range(-1, LAYERS):
            if f < 0:
                w[f] = [-x for x in value[0]]
            elif f == last:
                w[f] = value[last]
            else:
                w[f] = [x - y for x, y in zip(value[f], value[f + 1])]
            gl[f] = dot5(w[f], [lf[DL + k, f + 1, rows] for k in range(FIELDS)])
            ge[f] = dot5(w[f], [lf[ES + k, f + 1, rows] for k in range(FIELDS)])
            a4 = lf[A4, f + 1, rows]
            c[f] = [a4 * x for x in w[f]]
        z = {}
        for f in range(last):
            a2 = lf[A2, f + 1, rows]
            z[f] = [a2 * w[f][k] + 2.0 * c[f][k] - c[f + 1][k] - c[f - 1][k] for k in range(FIELDS)]
        nbar = [None] * LAYERS
        for j in range(-1, LAYERS + 1):
            nu_bar = ge.get(j, 0.0) + ge.get(j - 1, 0.0)
            here = ln[0, j + 1, rows] * nu_bar
            side = ln[1, j + 1, rows] * nu_bar
            for to, x in ((j, here), (j - 1, side), (j + 1, side)):
                to = clamp(to)
                nbar[to] = x if nbar[to] is None else nbar[to] + x
        for j in range(LAYERS):
            if j == 0:
                s = [0.5 * w[0][k] + w[-1][k] for k in range(FIELDS)]
                lin = z[0]
                rbar = gl[0] + 2.0 * gl[-1]
            elif j == last:
                s = [0.5 * w[last - 1][k] + w[last][k] for k in range(FIELDS)]
                lin = [-x for x in z[last - 1]]
                rbar = gl[last - 1] + 2.0 * gl[last]
            else:
                s = [0.5 * (w[j][k] + w[j - 1][k]) for k in range(FIELDS)]
                lin = [z[j][k] - z[j - 1][k] for k in range(FIELDS)]
                rbar = gl[j] + gl[j - 1]
            g = to_state(lin, s, rbar, nbar[j], [cm[i, j, rows] for i in range(CELLS)], 2)
            for k in range(FIELDS):
                acc[k, j, rows] = acc[k, j, rows] + g[k]


def outer_terms(flags, psi, coefs, acc, strip, to_a, to_b, ghost):
    even = flagged(flags, B_EVEN, (8, LANES))
    empty = jnp.zeros((8, LANES), jnp.float32)
    x_terms(flags, psi, lambda k, l: empty, coefs, acc, ghost)
    for k in range(FIELDS):
        high = packed_rows([ghost[k, l] for l in range(LAYERS)])
        low = packed_rows([pltpu.roll(ghost[k, l], 2, axis=0) for l in range(LAYERS)])
        to_a[k] = jnp.where(even, high, low)
        to_b[k] = jnp.where(even, low, high)
    sub = place_in_segment()
    edges = ((sub >= 6) & (sub < 8)) | ((sub >= 23) & (sub < 25))
    values = [packed_strip([psi[k, l] for l in range(LAYERS)]) for k in range(FIELDS)]
    strip_terms(values, edges, coefs, strip)


def settle(psi, outer, inner, keep, factor, pushed, base, looped):
    @each(LAYERS, looped)
    def _(l):
        for k in range(FIELDS):
            total = inner[k, l] if outer is None else outer[k, l] + inner[k, l]
            base[k, l] = psi[k, l] * keep[l] - factor[l] * total + pushed[k, l]


def arrived_rows(flags, lower, upper):
    row = iota((8, LANES), 0)
    first = (row < 2) & jnp.logical_not(flagged(flags, INLET, (8, LANES)))
    last = (row >= 6) & jnp.logical_not(flagged(flags, OUTLET, (8, LANES)))

    def rows(k, l):
        low = jnp.where(first, pair(lower[k], l, 0), 0.0)
        high = jnp.where(last, pair(upper[k], l, 6), 0.0)
        return jnp.concatenate([low, high], axis=0)

    return rows


def facing_gradients(flags, flow, from_a, from_b, near, far, maps):
    rotor = jnp.logical_not(flagged(flags, B_EVEN, (8, LANES)))
    row = iota((8, LANES), 0)
    panel = []
    for k in range(FIELDS):
        low = packed_rows([flow[k, l, 0:8] for l in range(LAYERS)])
        high = packed_rows([pltpu.roll(flow[k, l, 8:16], 2, axis=0) for l in range(LAYERS)])
        panel.append(jnp.where(rotor, high, low))
    panel = jnp.stack(panel)
    first, second = [], []
    for k in range(FIELDS):
        left, right = left_and_right(flags, from_a[k, 16:24], from_b[k, 16:24])
        first.append(jnp.where(rotor, left, right))
        second.append(jnp.where(rotor, right, left))
    ghosts = (
        mapped(panel, jnp.stack(first), maps),
        mapped(jnp.stack(second), panel, maps),
    )
    kept = (row == 7) | (rotor & (row == 0)) | (jnp.logical_not(rotor) & (row == 6))
    out = []
    for ghost, facing in zip(ghosts, (near, far)):
        layers = []
        for l in range(LAYERS):
            u, psi = [], []
            for k in range(FIELDS):
                cells = facing[k, 0:16]
                below = pair(ghost[k], l, 6)
                above = pair(ghost[k], l, 0)
                as_rotor = jnp.where(
                    row < 4,
                    quad(cells, l, False),
                    jnp.where(row < 6, pltpu.roll(below, 6, axis=0), below),
                )
                as_stator = jnp.where(
                    row < 2,
                    above,
                    jnp.where(row < 4, pltpu.roll(above, 2, axis=0), quad(cells, l, True)),
                )
                u.append(jnp.where(rotor, as_rotor, as_stator))
                value = facing[k, 16:24]
                psi.append(
                    jnp.where(
                        rotor,
                        jnp.where(row < 2, pair(value, l, 0), 0.0),
                        jnp.where(row >= 6, pair(value, l, 6), 0.0),
                    )
                )
            p, radius, _, cells = primitives(u)
            faces = rolled_faces(u, p, radius[0], 0)
            g = rolled_transpose(psi, lambda i: faces[i], cells, 0, 0, kept)
            layers.append([jnp.where(rotor, pltpu.roll(x, 2, axis=0), x) for x in g])
        out.append(jnp.stack([packed_rows([layers[l][k] for l in range(LAYERS)]) for k in range(FIELDS)]))
    return out


def prepare_kernel(
    flags, panel_maps, flow, adjoint, later, gradient, volume,
    state_maps, grad_maps, keep, factor, pushed, own, base, cm, tf, lf, ln, shared, sems, acc, radii,
):
    of_phase = panel_maps.at[flags[PHASE]]
    copies = [
        pltpu.make_async_copy(of_phase.at[pl.ds(flags[which], 2)], to, sems.at[i])
        for i, (which, to) in enumerate(((STATE_MAPS, state_maps), (GRAD_MAPS, grad_maps)))
    ]
    for copy in copies:
        copy.start()

    def at_cell(l, radius_sum):
        vol = volume[l]
        f = courant / (radius_sum + (1.5 * courant / physical_step) * vol)
        factor[l] = f
        keep[l] = 1.0 - f * ((1.5 / physical_step) * vol)
        for k in range(FIELDS):
            source = gradient[k, l] + vol * (2.0 * later[0, k, l] - 0.5 * later[1, k, l]) / physical_step
            pushed[k, l] = f * source

    inner_coefficients(flow, cm, tf, lf, ln, shared, radii, at_cell)

    @each(FIELDS, True)
    def _(k):
        own[k] = packed_edges([flow[k, l] for l in range(LAYERS)], [adjoint[k, l] for l in range(LAYERS)])

    t_terms(adjoint, cm, tf, acc, True)
    l_terms(adjoint, cm, lf, ln, acc, True)
    settle(adjoint, None, acc, keep, factor, pushed, base, True)
    for copy in copies:
        copy.wait()


def start_kernel(
    flags, flow, adjoint, from_a, from_b, zone_a, near, far, state_maps, grad_maps, factor, own, base, cm, shared,
    psi, acc, strip, to_a, to_b, ch, cs, xf, ts, ghost,
):
    coefs = (cm, ch, cs, xf, ts)
    outer_coefficients(flags, flow, own, from_a, from_b, zone_a, near, far, state_maps, shared, ch, cs, xf, ts)
    even = flagged(flags, B_EVEN, (8, LANES))
    plane = flagged(flags, PLANE, (8, LANES))
    row = iota((8, LANES), 0)
    use_upper = (row < 2) & jnp.logical_not(flagged(flags, OUTLET, (8, LANES)))
    use_lower = (row >= 6) & jnp.logical_not(flagged(flags, INLET, (8, LANES)))

    def halo(k, l):
        a = zone_a[k, 16:24]
        b = jnp.where(plane, 0.0, near[k, 16:24])
        upper = pair(jnp.where(even, a, b), l, 0)
        lower = pair(jnp.where(even, b, a), l, 6)
        return jnp.where(use_upper, upper, jnp.where(use_lower, lower, 0.0))

    x_terms(flags, adjoint, halo, coefs, acc, None)
    sub = place_in_segment()
    edges = ((sub >= 6) & (sub < 9)) | ((sub >= 22) & (sub < 25))
    values = [widened_other(flags, own[k], from_a[k, 0:16], from_b[k, 0:16]) for k in range(FIELDS)]
    strip_terms(values, edges, coefs, strip)
    panels = facing_gradients(flags, flow, from_a, from_b, near, far, grad_maps)
    through = mapped_back(panels[0], panels[1], grad_maps)
    lower, upper = [], []
    for k in range(FIELDS):
        b = jnp.where(plane, through[k], 0.0)
        lower.append(jnp.where(even, b, 0.0))
        upper.append(jnp.where(even, 0.0, b))
    rows = arrived_rows(flags, lower, upper)
    for k in range(FIELDS):
        for l in range(LAYERS):
            total = acc[k, l] + from_strip(strip[k], l) + rows(k, l)
            psi[k, l] = base[k, l] - factor[l] * total
    outer_terms(flags, psi, coefs, acc, strip, to_a, to_b, ghost)


def inner_kernel(flags, psi, outer, keep, factor, pushed, cm, tf, lf, ln, base, acc):
    t_terms(psi, cm, tf, acc, False)
    l_terms(psi, cm, lf, ln, acc, False)
    settle(psi, outer, acc, keep, factor, pushed, base, False)


def advance(flags, base, strip, from_a, from_b, zone_a, near, far, maps, factor, out):
    through = mapped_back(near[...], far[...], maps)
    even = flagged(flags, B_EVEN, (8, LANES))
    plane = flagged(flags, PLANE, (8, LANES))
    sub = place_in_segment()
    whole, lower, upper = [], [], []
    for k in range(FIELDS):
        left, right = left_and_right(flags, from_a[k], from_b[k])
        right = jnp.where(sub < 8, pltpu.roll(right, LANES - 16, axis=1), 0.0)
        whole.append(strip[k] + jnp.where(sub >= 24, pltpu.roll(left, 16, axis=1), right))
        b = jnp.where(plane, through[k], near[k])
        a = zone_a[k]
        lower.append(jnp.where(even, b, a))
        upper.append(jnp.where(even, a, b))
    rows = arrived_rows(flags, lower, upper)
    for k in range(FIELDS):
        for l in range(LAYERS):
            out[k, l] = base[k, l] - factor[l] * (from_strip(whole[k], l) + rows(k, l))


def step_kernel(
    flags, base, strip, from_a, from_b, zone_a, near, far, maps, factor, cm, ch, cs, xf, ts,
    psi, acc, strip_out, to_a, to_b, ghost,
):
    advance(flags, base, strip, from_a, from_b, zone_a, near, far, maps, factor, psi)
    outer_terms(flags, psi, (cm, ch, cs, xf, ts), acc, strip_out, to_a, to_b, ghost)


def last_kernel(flags, base, strip, from_a, from_b, zone_a, near, far, maps, factor, out):
    advance(flags, base, strip, from_a, from_b, zone_a, near, far, maps, factor, out)


def f32(*shape):
    return jax.ShapeDtypeStruct(shape, jnp.float32)


STATE = (FIELDS, LAYERS, ROWS, LANES)
STRIP = (FIELDS, ROWS, LANES)
PANEL = (FIELDS, 8, LANES)
SCALAR = (LAYERS, ROWS, LANES)
FIRST = ((FIELDS, 24, LANES),) * 3
MAPS = (2, LANES, LANES)
GHOST = (FIELDS, LAYERS, 8, LANES)
TERMS = (f32(*STATE), f32(*STATE), f32(*STRIP), f32(*PANEL), f32(*PANEL))
FIXED = (f32(*SCALAR), f32(*SCALAR), f32(*STATE))
INNER = (
    f32(CELLS, *SCALAR),
    f32(FACES, *SCALAR),
    f32(12, LAYERS + 1, ROWS, LANES),
    f32(2, LAYERS + 2, ROWS, LANES),
)
SHARED = f32(2, *SCALAR)
OUTER = (
    f32(CELLS, LAYERS, 8, LANES),
    f32(CELLS, ROWS, LANES),
    f32(FACES, LAYERS, ROWS + 8, LANES),
    f32(FACES, ROWS, LANES),
)


def call(kernel, outs, args, work=(), name=None, in_place=None, away=(), copies=0):
    vmem = pl.BlockSpec(memory_space=pltpu.VMEM)
    smem = pl.BlockSpec(memory_space=pltpu.SMEM)
    there = pl.BlockSpec(memory_space=pltpu.HBM)
    return pl.pallas_call(
        kernel,
        out_shape=outs,
        in_specs=[smem] + [there if i in away else vmem for i in range(1, len(args))],
        out_specs=[vmem] * len(outs) if isinstance(outs, tuple) else vmem,
        scratch_shapes=([pltpu.SemaphoreType.DMA((copies,))] if copies else [])
        + [pltpu.VMEM(shape, jnp.float32) for shape in work],
        compiler_params=pltpu.CompilerParams(vmem_limit_bytes=32 * 1024 * 1024),
        input_output_aliases=in_place or {},
        name=name,
    )(*args)


def swaps(names, sectors, blocks, turn):
    half = blocks // 2
    assert half % 2 == 0
    where = {"sector": sectors, "block": blocks}
    minor = where[names[1]]

    def flat(b, s):
        first, second = (s, b) if names[0] == "sector" else (b, s)
        return first * minor + second

    sector_a, sector_b, block_a, near, far = [], [], [], [], []
    for b in range(blocks):
        for s in range(sectors):
            me = flat(b, s)
            sector_a.append((me, flat(b, s ^ 1)))
            sector_b.append((me, flat(b, (s + (1 if s % 2 else -1)) % sectors)))
            block_a.append((me, flat(b ^ 1, s)))
            if b == half - 1:
                near.append((me, flat(half, (s + turn) % sectors)))
                far.append((me, flat(half, (s + turn + 1) % sectors)))
            elif b == half:
                near.append((me, flat(half - 1, (s - turn) % sectors)))
                far.append((me, flat(half - 1, (s - turn - 1) % sectors)))
            else:
                other = b + 1 if b % 2 else b - 1
                near.append((me, flat(other, s) if 0 <= other < blocks else me))
                far.append((me, me))
    return sector_a, sector_b, block_a, near, far


def exchange(names, sectors, blocks, offset, strip, to_a, to_b, beside=None, args=()):
    def branch(shift):
        sector_a, sector_b, block_a, near, far = swaps(names, sectors, blocks, shift)

        def run(strip, to_a, to_b, *args):
            move = lambda x, pairs: lax.ppermute(x, names, pairs)
            moved = (
                move(strip, sector_a),
                move(strip, sector_b),
                move(to_a, block_a),
                move(to_b, near),
                move(to_b, far),
            )
            return moved if beside is None else moved + tuple(beside(*args))

        return run

    return tuple(
        lax.switch(offset, [branch(shift) for shift in range(sectors)], strip, to_a, to_b, *args)
    )


def first_beside(*args):
    return call(
        prepare_kernel,
        (f32(*MAPS), f32(*MAPS)) + FIXED + (f32(*STRIP), f32(*STATE)) + INNER + (SHARED,),
        args,
        (STATE, SCALAR),
        name="prepare",
        away=(1,),
        copies=2,
    )


def next_beside(*args):
    return (call(inner_kernel, f32(*STATE), args, (STATE,), name="inner", in_place={2: 0}),)


def shards(flow, adjoint, adjoint_later, objective_grad, volume, panel_maps, rotor_step, names):
    blocks = lax.axis_size("block")
    sectors = lax.axis_size("sector")
    place = lax.axis_index("block")
    half = blocks // 2
    stator = place >= half
    turn = rotor_step[0]
    offset = (turn // PHASES) % sectors
    flags = jnp.stack(
        [
            (lax.axis_index("sector") % 2 == 0).astype(jnp.int32),
            (place % 2 == 0).astype(jnp.int32),
            (place == 0).astype(jnp.int32),
            (place == blocks - 1).astype(jnp.int32),
            ((place == half) | (place == half - 1)).astype(jnp.int32),
            turn % PHASES,
            jnp.where(stator, 0, 2).astype(jnp.int32),
            jnp.where(stator, 2, 0).astype(jnp.int32),
        ]
    )
    send = partial(exchange, names, sectors, blocks, offset)
    packed = tuple(
        call(
            pack_kernel,
            tuple(f32(*shape) for shape in FIRST),
            (flags, flow, adjoint),
            name="pack",
        )
    )
    arrived = send(
        *packed,
        beside=first_beside,
        args=(
            flags,
            panel_maps,
            flow,
            adjoint,
            adjoint_later,
            objective_grad,
            volume,
        ),
    )
    (state_maps, maps, keep, factor, pushed, own, base), inner, shared = arrived[5:12], arrived[12:16], arrived[16]
    cm = inner[0]
    out = call(
        start_kernel,
        TERMS + OUTER,
        (flags, flow, adjoint) + arrived[:5] + (state_maps, maps, factor, own, base, cm, shared),
        (GHOST,),
        name="start",
    )
    terms, outer = tuple(out[:5]), tuple(out[5:])
    for sweep in range(1, ITERS):
        psi, acc, strip, to_a, to_b = terms
        arrived = send(
            strip, to_a, to_b, beside=next_beside, args=(flags, psi, acc, keep, factor, pushed) + inner
        )
        args = (flags, arrived[5], strip) + arrived[:5] + (maps, factor)
        if sweep == ITERS - 1:
            return call(last_kernel, f32(*STATE), args, name="last")
        terms = tuple(call(step_kernel, TERMS, args + (cm,) + outer, (GHOST,), name="step"))


def solution(mesh):
    placed = (
        P(None, None, "block", "sector"),
        P(None, None, "block", "sector"),
        P(None, None, None, "block", "sector"),
        P(None, None, "block", "sector"),
        P(None, "block", "sector"),
        P(),
        P(),
    )
    return jax.shard_map(
        partial(shards, names=tuple(mesh.axis_names)),
        mesh=mesh,
        in_specs=placed,
        out_specs=P(None, None, "block", "sector"),
        check_vma=False,
    )
```

```python
from functools import partial

import jax
import jax.numpy as jnp
from jax import lax
from jax.experimental import pallas as pl
from jax.experimental.pallas import tpu as pltpu
from jax.sharding import PartitionSpec as P

PHASES = 4
ITERS = 4
LANES = 128
ROWS = 16
LAYERS = 4
FIELDS = 5
SEG = LANES // LAYERS

gamma_gas = 1.4
second_coef = 0.5
fourth_coef = 1.0 / 32.0
courant = 0.6
physical_step = 2.0
sensor_floor = 0.0001
highest = lax.Precision.HIGHEST

S_EVEN, B_EVEN, INLET, OUTLET, PLANE, PHASE, STATE_MAPS, GRAD_MAPS = range(8)
U1, U2, U3, HT, BX, BT, BL, CR, CP = range(9)
CELLS = 9
A2, A4, DL, ES, N0, N1 = 0, 1, 2, 7, 12, 13
FACES = 14


def up_by(x, axis, k):
    n = x.shape[axis]
    return pltpu.roll(x, (-k) % n, axis=axis)


def iota(shape, axis):
    return lax.broadcasted_iota(jnp.int32, shape, axis)


def flagged(flags, which, shape):
    return jnp.broadcast_to(flags[which], shape) == 1


def primitives(u):
    inverse = 1.0 / u[0]
    vel = [u[1] * inverse, u[2] * inverse, u[3] * inverse]
    square = vel[0] * vel[0] + vel[1] * vel[1] + vel[2] * vel[2]
    p = (gamma_gas - 1.0) * (u[4] - 0.5 * u[0] * square)
    heat = gamma_gas * p * inverse
    slow = lax.rsqrt(heat)
    sound = heat * slow
    radius, slopes = [], []
    for q in vel:
        x = q * q + 0.01
        y = lax.rsqrt(x)
        radius.append(x * y + sound)
        slopes.append(q * y * inverse)
    half = 0.5 * inverse
    cells = vel + [(u[4] + p) * inverse] + slopes + [sound * half, gamma_gas * half * slow]
    return p, radius, sound, cells


def sensor_terms(below, here, above):
    bend = above - 2.0 * here + below
    total = above + 2.0 * here + below
    inside = bend * bend + sensor_floor
    slope = lax.rsqrt(inside)
    over = 1.0 / total
    nu = inside * slope * over
    a = bend * slope * over
    b = nu * over
    return nu, -2.0 * a - 2.0 * b, a - b


def face_terms(nu_left, nu_right, rad_left, rad_right, behind, left, right, ahead):
    e2 = (0.5 * second_coef) * (nu_left + nu_right)
    ratio = fourth_coef / (fourth_coef + e2)
    e4 = fourth_coef * ratio
    slope = ratio * ratio
    lam = 0.5 * (rad_left + rad_right)
    radial, sensed = [], []
    for b, l, r, a in zip(behind, left, right, ahead):
        first = r - l
        third = a - 3.0 * first - b
        radial.append(-0.5 * (e2 * first - e4 * third))
        sensed.append((-0.25) * lam * (first + slope * third))
    return [lam * e2, lam * e4] + radial + sensed


def rolled_faces(u, p, radius, axis):
    nu, n0, n1 = sensor_terms(up_by(p, axis, -1), p, up_by(p, axis, 1))
    right = [up_by(x, axis, 1) for x in u]
    behind = [up_by(x, axis, -1) for x in u]
    ahead = [up_by(x, axis, 2) for x in u]
    return face_terms(
        nu, up_by(nu, axis, 1), radius, up_by(radius, axis, 1), behind, u, right, ahead
    ) + [n0, n1]


def dot5(a, b):
    return (a[0] * b[0] + a[1] * b[1]) + (a[2] * b[2] + a[3] * b[3]) + a[4] * b[4]


def to_state(lin, s, rbar, nbar, cells, direction):
    q = cells[direction]
    kappa = s[1] * cells[U1] + s[2] * cells[U2] + s[3] * cells[U3] + s[4] * cells[HT]
    kappa = kappa + cells[BX + direction] * rbar
    sq = s[4] * q
    pbar = nbar + sq + s[direction + 1] + cells[CP] * rbar
    scaled = (gamma_gas - 1.0) * pbar
    g = [None] * FIELDS
    square = cells[U1] * cells[U1] + cells[U2] * cells[U2] + cells[U3] * cells[U3]
    g[0] = lin[0] - q * kappa - cells[CR] * rbar + 0.5 * square * scaled
    for k in range(3):
        g[k + 1] = lin[k + 1] + q * s[k + 1] - cells[k] * scaled
    g[direction + 1] = g[direction + 1] + (s[0] + kappa)
    g[4] = lin[4] + sq + scaled
    return g


def rolled_transpose(psi, faces, cells, direction, axis, mask=None):
    w = [x - up_by(x, axis, 1) for x in psi]
    if mask is not None:
        w = [jnp.where(mask, x, 0.0) for x in w]
    gl = dot5(w, [faces(DL + k) for k in range(FIELDS)])
    ge = dot5(w, [faces(ES + k) for k in range(FIELDS)])
    a2, a4 = faces(A2), faces(A4)
    lin, s = [], []
    for x in w:
        c = a4 * x
        v = c - up_by(c, axis, -1)
        z = a2 * x + (v - up_by(v, axis, 1))
        lin.append(z - up_by(z, axis, -1))
        s.append(0.5 * (x + up_by(x, axis, -1)))
    rbar = gl + up_by(gl, axis, -1)
    nu_bar = ge + up_by(ge, axis, -1)
    v = faces(N1) * nu_bar
    nbar = faces(N0) * nu_bar + up_by(v, axis, 1) + up_by(v, axis, -1)
    return to_state(lin, s, rbar, nbar, cells, direction)


def packed_rows(tiles):
    row = iota((8, LANES), 0)
    out = tiles[0]
    for l in range(1, LAYERS):
        out = jnp.where(row >= 2 * l, pltpu.roll(tiles[l], 2 * l, axis=0), out)
    return out


def packed_quads(tiles):
    row = iota((8, LANES), 0)
    pairs = [
        jnp.where(row < 4, tiles[l], pltpu.roll(tiles[l + 1], 4, axis=0)) for l in range(0, LAYERS, 2)
    ]
    return jnp.concatenate(pairs, axis=0)


def quad(packed, l, high):
    tile = packed[8 * (l // 2) : 8 * (l // 2) + 8]
    return pltpu.roll(tile, 4, axis=0) if (l % 2 == 1) != high else tile


def pair(packed, l, to):
    shift = (to - 2 * l) % 8
    return pltpu.roll(packed, shift, axis=0) if shift else packed


def packed_strip(layers):
    lane = iota((ROWS, LANES), 1)
    out = jnp.zeros((ROWS, LANES), jnp.float32)
    for l, x in enumerate(layers):
        base = SEG * l
        out = jnp.where((lane >= base) & (lane < base + 8), pltpu.roll(x, (base + 8) % LANES, axis=1), out)
        out = jnp.where(
            (lane >= base + 24) & (lane < base + 32), pltpu.roll(x, (base + 24) % LANES, axis=1), out
        )
    return out


def packed_edges(layers, others):
    lane = iota((ROWS, LANES), 1)
    out = packed_strip(layers)
    for l, x in enumerate(others):
        base = SEG * l + 16
        out = jnp.where((lane >= base - 8) & (lane < base + 8), pltpu.roll(x, base, axis=1), out)
    return out


def from_strip(strip, l):
    lane = iota((ROWS, LANES), 1)
    base = SEG * l
    low = pltpu.roll(strip, (-(base + 24)) % LANES, axis=1)
    high = pltpu.roll(strip, (-(base + 8)) % LANES, axis=1)
    return jnp.where(lane < 8, low, jnp.where(lane >= LANES - 8, high, 0.0))


def place_in_segment():
    return jnp.bitwise_and(iota((ROWS, LANES), 1), SEG - 1)


def each(count, looped):
    def run(body):
        if looped:
            lax.fori_loop(0, count, lambda i, c: (body(i), c)[1], 0)
        else:
            for i in range(count):
                body(i)

    return run


def half_rows(half):
    return slice(8 * half, 8 * half + 8) if isinstance(half, int) else pl.ds(pl.multiple_of(8 * half, 8), 8)


def clamp(j):
    return min(max(j, 0), LAYERS - 1)


def pack_kernel(flags, flow, psi, to_t, to_a, to_b):
    even = flagged(flags, B_EVEN, (8, LANES))
    even2 = flagged(flags, B_EVEN, (16, LANES))
    for k in range(FIELDS):
        to_t[k, 0:16] = packed_edges([flow[k, l] for l in range(LAYERS)], [psi[k, l] for l in range(LAYERS)])
        low = packed_rows([flow[k, l, 0:8] for l in range(LAYERS)])
        high = packed_rows([pltpu.roll(flow[k, l, 8:16], 2, axis=0) for l in range(LAYERS)])
        to_t[k, 16:24] = jnp.where(even, low, high)
        low = packed_quads([flow[k, l, 0:8] for l in range(LAYERS)])
        high = packed_quads([pltpu.roll(flow[k, l, 8:16], 4, axis=0) for l in range(LAYERS)])
        to_a[k, 0:16] = jnp.where(even2, high, low)
        to_b[k, 0:16] = jnp.where(even2, low, high)
        low = packed_rows([psi[k, l, 0:8] for l in range(LAYERS)])
        high = packed_rows([pltpu.roll(psi[k, l, 8:16], 2, axis=0) for l in range(LAYERS)])
        to_a[k, 16:24] = jnp.where(even, high, low)
        to_b[k, 16:24] = jnp.where(even, low, high)


def mapped(near, far, maps):
    shape = near.shape
    dims = (((1,), (1,)), ((), ()))
    near = near.reshape(shape[0] * shape[1], LANES)
    far = far.reshape(shape[0] * shape[1], LANES)
    out = lax.dot_general(near, maps[0], dims, precision=highest, preferred_element_type=jnp.float32)
    out = out + lax.dot_general(far, maps[1], dims, precision=highest, preferred_element_type=jnp.float32)
    return out.reshape(shape)


def mapped_back(near, far, maps):
    shape = near.shape
    both = jnp.concatenate([near, far], axis=2).reshape(shape[0] * shape[1], 2 * LANES)
    table = maps[...].reshape(2 * LANES, LANES)
    out = jnp.dot(both, table, precision=highest, preferred_element_type=jnp.float32)
    return out.reshape(shape)


def left_and_right(flags, a, b):
    even = flagged(flags, S_EVEN, a.shape)
    return jnp.where(even, b, a), jnp.where(even, a, b)


def three(panels):
    return [panels.at[:, :, pl.ds(LANES * i, LANES)] for i in range(3)]


def widened(flags, own, a, b):
    sub = place_in_segment()
    left, right = left_and_right(flags, a, b)
    x = jnp.where((sub >= 8) & (sub < 16), pltpu.roll(right, LANES - 16, axis=1), own)
    return jnp.where((sub >= 16) & (sub < 24), pltpu.roll(left, 16, axis=1), x)


def widened_other(flags, own, a, b):
    sub = place_in_segment()
    left, right = left_and_right(flags, a, b)
    low = pltpu.roll(jnp.where((sub >= 16) & (sub < 24), right, own), LANES - 8, axis=1)
    high = pltpu.roll(jnp.where((sub >= 8) & (sub < 16), left, own), 8, axis=1)
    return jnp.where(sub < 16, low, high)


def inner_coefficients(flow, cm, tf, lf, ln, shared, radii, at_cell):
    @each(LAYERS, True)
    def _(l):
        u = [flow[k, l] for k in range(FIELDS)]
        p, radius, _, cells = primitives(u)
        for i, x in enumerate(cells):
            cm[i, l] = x
        shared[0, l] = p
        shared[1, l] = radius[0]
        radii[l] = radius[2]
        at_cell(l, radius[0] + radius[1] + radius[2])
        for i, x in enumerate(rolled_faces(u, p, radius[1], 1)):
            tf[i, l] = x

    @each(2, True)
    def _(half):
        rows = half_rows(half)
        cell = [[flow[k, l, rows] for k in range(FIELDS)] for l in range(LAYERS)]
        pressure = [shared[0, l, rows] for l in range(LAYERS)]
        radius = [radii[l, rows] for l in range(LAYERS)]
        nus = {}
        for j in range(-1, LAYERS + 1):
            nu, n0, n1 = sensor_terms(*[pressure[clamp(j + d)] for d in (-1, 0, 1)])
            nus[j] = nu
            ln[0, j + 1, rows] = n0
            ln[1, j + 1, rows] = n1
        for f in range(-1, LAYERS):
            terms = face_terms(
                nus[f],
                nus[f + 1],
                radius[clamp(f)],
                radius[clamp(f + 1)],
                *[cell[clamp(f + d)] for d in (-1, 0, 1, 2)],
            )
            for i, x in enumerate(terms):
                lf[i, f + 1, rows] = x


def outer_coefficients(flags, flow, own, from_a, from_b, zone_a, near, far, maps, shared, ch, cs, xf, ts):
    through = mapped(near[:, 0:16], far[:, 0:16], maps)
    even = flagged(flags, B_EVEN, (16, LANES))
    plane = flagged(flags, PLANE, (16, LANES))
    row = iota((8, LANES), 0)
    inlet = flagged(flags, INLET, (8, LANES))
    outlet = flagged(flags, OUTLET, (8, LANES))
    lower, upper = [], []
    for k in range(FIELDS):
        b = jnp.where(plane, through[k], near[k, 0:16])
        a = zone_a[k, 0:16]
        lower.append(jnp.where(even, b, a))
        upper.append(jnp.where(even, a, b))
    for l in range(LAYERS):
        u, halo = [], []
        for k in range(FIELDS):
            main = flow[k, l]
            up = jnp.where(outlet, jnp.broadcast_to(main[15:16], (8, LANES)), quad(upper[k], l, False))
            low = jnp.where(inlet, jnp.broadcast_to(main[0:1], (8, LANES)), quad(lower[k], l, True))
            halo.append(jnp.where(row < 4, up, low))
            u.append(jnp.concatenate([main, halo[k]], axis=0))
        p, radius, _, cells = primitives(halo)
        for i, x in enumerate(cells):
            ch[i, l] = x
        p = jnp.concatenate([shared[0, l], p], axis=0)
        radius = jnp.concatenate([shared[1, l], radius[0]], axis=0)
        for i, x in enumerate(rolled_faces(u, p, radius, 0)):
            xf[i, l] = x
    u = [widened(flags, own[k], from_a[k, 0:16], from_b[k, 0:16]) for k in range(FIELDS)]
    p, radius, _, cells = primitives(u)
    for i, x in enumerate(cells):
        cs[i] = x
    for i, x in enumerate(rolled_faces(u, p, radius[1], 1)):
        ts[i] = x


def x_terms(flags, psi, halo, coefs, acc, ghost):
    cm, ch, _, xf, _ = coefs
    row = iota((8, LANES), 0)
    inlet = flagged(flags, INLET, (8, LANES)) & (row == 0)
    outlet = flagged(flags, OUTLET, (8, LANES)) & (row == 7)
    for l in range(LAYERS):
        wide = [jnp.concatenate([psi[k, l], halo(k, l)], axis=0) for k in range(FIELDS)]
        cells = [jnp.concatenate([cm[i, l], ch[i, l]], axis=0) for i in range(CELLS)]
        g = rolled_transpose(wide, lambda i: xf[i, l], cells, 0, 0)
        for k in range(FIELDS):
            out = g[k][16:]
            if ghost is not None:
                ghost[k, l] = out
            first = pltpu.roll(out, 2, axis=0) + pltpu.roll(out, 1, axis=0)
            last = pltpu.roll(out, 7, axis=0) + pltpu.roll(out, 6, axis=0)
            acc[k, l, 0:8] = g[k][0:8] + jnp.where(inlet, first, 0.0)
            acc[k, l, 8:16] = g[k][8:16] + jnp.where(outlet, last, 0.0)


def strip_terms(values, edges, coefs, strip):
    _, _, cs, _, ts = coefs
    g = rolled_transpose(values, lambda i: ts[i], [cs[i] for i in range(CELLS)], 1, 1, edges)
    for k in range(FIELDS):
        strip[k] = g[k]


def t_terms(psi, cm, tf, acc, looped):
    lane = iota((ROWS, LANES), 1)
    inner = (lane >= 1) & (lane < LANES - 2)

    @each(LAYERS, looped)
    def _(l):
        g = rolled_transpose(
            [psi[k, l] for k in range(FIELDS)],
            lambda i: tf[i, l],
            [cm[i, l] for i in range(CELLS)],
            1,
            1,
            inner,
        )
        for k in range(FIELDS):
            acc[k, l] = g[k]


def l_terms(psi, cm, lf, ln, acc, looped):
    last = LAYERS - 1

    @each(2, looped)
    def _(half):
        rows = half_rows(half)
        value = [[psi[k, l, rows] for k in range(FIELDS)] for l in range(LAYERS)]
        w, c, gl, ge = {}, {}, {}, {}
        for f in range(-1, LAYERS):
            if f < 0:
                w[f] = [-x for x in value[0]]
            elif f == last:
                w[f] = value[last]
            else:
                w[f] = [x - y for x, y in zip(value[f], value[f + 1])]
            gl[f] = dot5(w[f], [lf[DL + k, f + 1, rows] for k in range(FIELDS)])
            ge[f] = dot5(w[f], [lf[ES + k, f + 1, rows] for k in range(FIELDS)])
            a4 = lf[A4, f + 1, rows]
            c[f] = [a4 * x for x in w[f]]
        z = {}
        for f in range(last):
            a2 = lf[A2, f + 1, rows]
            z[f] = [a2 * w[f][k] + 2.0 * c[f][k] - c[f + 1][k] - c[f - 1][k] for k in range(FIELDS)]
        nbar = [None] * LAYERS
        for j in range(-1, LAYERS + 1):
            nu_bar = ge.get(j, 0.0) + ge.get(j - 1, 0.0)
            here = ln[0, j + 1, rows] * nu_bar
            side = ln[1, j + 1, rows] * nu_bar
            for to, x in ((j, here), (j - 1, side), (j + 1, side)):
                to = clamp(to)
                nbar[to] = x if nbar[to] is None else nbar[to] + x
        for j in range(LAYERS):
            if j == 0:
                s = [0.5 * w[0][k] + w[-1][k] for k in range(FIELDS)]
                lin = z[0]
                rbar = gl[0] + 2.0 * gl[-1]
            elif j == last:
                s = [0.5 * w[last - 1][k] + w[last][k] for k in range(FIELDS)]
                lin = [-x for x in z[last - 1]]
                rbar = gl[last - 1] + 2.0 * gl[last]
            else:
                s = [0.5 * (w[j][k] + w[j - 1][k]) for k in range(FIELDS)]
                lin = [z[j][k] - z[j - 1][k] for k in range(FIELDS)]
                rbar = gl[j] + gl[j - 1]
            g = to_state(lin, s, rbar, nbar[j], [cm[i, j, rows] for i in range(CELLS)], 2)
            for k in range(FIELDS):
                acc[k, j, rows] = acc[k, j, rows] + g[k]


def outer_terms(flags, psi, coefs, acc, strip, to_a, to_b, ghost):
    even = flagged(flags, B_EVEN, (8, LANES))
    empty = jnp.zeros((8, LANES), jnp.float32)
    x_terms(flags, psi, lambda k, l: empty, coefs, acc, ghost)
    for k in range(FIELDS):
        high = packed_rows([ghost[k, l] for l in range(LAYERS)])
        low = packed_rows([pltpu.roll(ghost[k, l], 2, axis=0) for l in range(LAYERS)])
        to_a[k] = jnp.where(even, high, low)
        to_b[k] = jnp.where(even, low, high)
    sub = place_in_segment()
    edges = ((sub >= 6) & (sub < 8)) | ((sub >= 23) & (sub < 25))
    values = [packed_strip([psi[k, l] for l in range(LAYERS)]) for k in range(FIELDS)]
    strip_terms(values, edges, coefs, strip)


def settle(psi, outer, inner, keep, factor, pushed, base, looped):
    @each(LAYERS, looped)
    def _(l):
        for k in range(FIELDS):
            total = inner[k, l] if outer is None else outer[k, l] + inner[k, l]
            base[k, l] = psi[k, l] * keep[l] - factor[l] * total + pushed[k, l]


def arrived_rows(flags, lower, upper):
    row = iota((8, LANES), 0)
    first = (row < 2) & jnp.logical_not(flagged(flags, INLET, (8, LANES)))
    last = (row >= 6) & jnp.logical_not(flagged(flags, OUTLET, (8, LANES)))

    def rows(k, l):
        low = jnp.where(first, pair(lower[k], l, 0), 0.0)
        high = jnp.where(last, pair(upper[k], l, 6), 0.0)
        return jnp.concatenate([low, high], axis=0)

    return rows


def facing_gradients(flags, flow, from_a, from_b, near, far, maps):
    rotor = jnp.logical_not(flagged(flags, B_EVEN, (8, LANES)))
    row = iota((8, LANES), 0)
    panel = []
    for k in range(FIELDS):
        low = packed_rows([flow[k, l, 0:8] for l in range(LAYERS)])
        high = packed_rows([pltpu.roll(flow[k, l, 8:16], 2, axis=0) for l in range(LAYERS)])
        panel.append(jnp.where(rotor, high, low))
    panel = jnp.stack(panel)
    first, second = [], []
    for k in range(FIELDS):
        left, right = left_and_right(flags, from_a[k, 16:24], from_b[k, 16:24])
        first.append(jnp.where(rotor, left, right))
        second.append(jnp.where(rotor, right, left))
    ghosts = (
        mapped(panel, jnp.stack(first), maps),
        mapped(jnp.stack(second), panel, maps),
    )
    kept = (row == 7) | (rotor & (row == 0)) | (jnp.logical_not(rotor) & (row == 6))
    out = []
    for ghost, facing in zip(ghosts, (near, far)):
        layers = []
        for l in range(LAYERS):
            u, psi = [], []
            for k in range(FIELDS):
                cells = facing[k, 0:16]
                below = pair(ghost[k], l, 6)
                above = pair(ghost[k], l, 0)
                as_rotor = jnp.where(
                    row < 4,
                    quad(cells, l, False),
                    jnp.where(row < 6, pltpu.roll(below, 6, axis=0), below),
                )
                as_stator = jnp.where(
                    row < 2,
                    above,
                    jnp.where(row < 4, pltpu.roll(above, 2, axis=0), quad(cells, l, True)),
                )
                u.append(jnp.where(rotor, as_rotor, as_stator))
                value = facing[k, 16:24]
                psi.append(
                    jnp.where(
                        rotor,
                        jnp.where(row < 2, pair(value, l, 0), 0.0),
                        jnp.where(row >= 6, pair(value, l, 6), 0.0),
                    )
                )
            p, radius, _, cells = primitives(u)
            faces = rolled_faces(u, p, radius[0], 0)
            g = rolled_transpose(psi, lambda i: faces[i], cells, 0, 0, kept)
            layers.append([jnp.where(rotor, pltpu.roll(x, 2, axis=0), x) for x in g])
        out.append(jnp.stack([packed_rows([layers[l][k] for l in range(LAYERS)]) for k in range(FIELDS)]))
    return out


def prepare_kernel(
    flags, panel_maps, flow, adjoint, later, gradient, volume,
    state_maps, grad_maps, keep, factor, pushed, own, base, cm, tf, lf, ln, shared, sems, acc, radii,
):
    of_phase = panel_maps.at[flags[PHASE]]
    copies = [
        pltpu.make_async_copy(of_phase.at[pl.ds(flags[which], 2)], to, sems.at[i])
        for i, (which, to) in enumerate(((STATE_MAPS, state_maps), (GRAD_MAPS, grad_maps)))
    ]
    for copy in copies:
        copy.start()

    def at_cell(l, radius_sum):
        vol = volume[l]
        f = courant / (radius_sum + (1.5 * courant / physical_step) * vol)
        factor[l] = f
        keep[l] = 1.0 - f * ((1.5 / physical_step) * vol)
        for k in range(FIELDS):
            source = gradient[k, l] + vol * (2.0 * later[0, k, l] - 0.5 * later[1, k, l]) / physical_step
            pushed[k, l] = f * source

    inner_coefficients(flow, cm, tf, lf, ln, shared, radii, at_cell)

    @each(FIELDS, True)
    def _(k):
        own[k] = packed_edges([flow[k, l] for l in range(LAYERS)], [adjoint[k, l] for l in range(LAYERS)])

    t_terms(adjoint, cm, tf, acc, True)
    l_terms(adjoint, cm, lf, ln, acc, True)
    settle(adjoint, None, acc, keep, factor, pushed, base, True)
    for copy in copies:
        copy.wait()


def start_kernel(
    flags, flow, adjoint, from_a, from_b, zone_a, near, far, state_maps, grad_maps, factor, own, base, cm, shared,
    psi, acc, strip, to_a, to_b, ch, cs, xf, ts, ghost,
):
    coefs = (cm, ch, cs, xf, ts)
    outer_coefficients(flags, flow, own, from_a, from_b, zone_a, near, far, state_maps, shared, ch, cs, xf, ts)
    even = flagged(flags, B_EVEN, (8, LANES))
    plane = flagged(flags, PLANE, (8, LANES))
    row = iota((8, LANES), 0)
    use_upper = (row < 2) & jnp.logical_not(flagged(flags, OUTLET, (8, LANES)))
    use_lower = (row >= 6) & jnp.logical_not(flagged(flags, INLET, (8, LANES)))

    def halo(k, l):
        a = zone_a[k, 16:24]
        b = jnp.where(plane, 0.0, near[k, 16:24])
        upper = pair(jnp.where(even, a, b), l, 0)
        lower = pair(jnp.where(even, b, a), l, 6)
        return jnp.where(use_upper, upper, jnp.where(use_lower, lower, 0.0))

    x_terms(flags, adjoint, halo, coefs, acc, None)
    sub = place_in_segment()
    edges = ((sub >= 6) & (sub < 9)) | ((sub >= 22) & (sub < 25))
    values = [widened_other(flags, own[k], from_a[k, 0:16], from_b[k, 0:16]) for k in range(FIELDS)]
    strip_terms(values, edges, coefs, strip)
    panels = facing_gradients(flags, flow, from_a, from_b, near, far, grad_maps)
    through = mapped_back(panels[0], panels[1], grad_maps)
    lower, upper = [], []
    for k in range(FIELDS):
        b = jnp.where(plane, through[k], 0.0)
        lower.append(jnp.where(even, b, 0.0))
        upper.append(jnp.where(even, 0.0, b))
    rows = arrived_rows(flags, lower, upper)
    for k in range(FIELDS):
        for l in range(LAYERS):
            total = acc[k, l] + from_strip(strip[k], l) + rows(k, l)
            psi[k, l] = base[k, l] - factor[l] * total
    outer_terms(flags, psi, coefs, acc, strip, to_a, to_b, ghost)


def inner_kernel(flags, psi, outer, keep, factor, pushed, cm, tf, lf, ln, base, acc):
    t_terms(psi, cm, tf, acc, False)
    l_terms(psi, cm, lf, ln, acc, False)
    settle(psi, outer, acc, keep, factor, pushed, base, False)


def advance(flags, base, strip, from_a, from_b, panels, maps, factor, out):
    near, far, zone_a = three(panels)
    through = mapped_back(near[...], far[...], maps)
    even = flagged(flags, B_EVEN, (8, LANES))
    plane = flagged(flags, PLANE, (8, LANES))
    sub = place_in_segment()
    whole, lower, upper = [], [], []
    for k in range(FIELDS):
        left, right = left_and_right(flags, from_a[k], from_b[k])
        right = jnp.where(sub < 8, pltpu.roll(right, LANES - 16, axis=1), 0.0)
        whole.append(strip[k] + jnp.where(sub >= 24, pltpu.roll(left, 16, axis=1), right))
        b = jnp.where(plane, through[k], near[k])
        a = zone_a[k]
        lower.append(jnp.where(even, b, a))
        upper.append(jnp.where(even, a, b))
    rows = arrived_rows(flags, lower, upper)
    for k in range(FIELDS):
        for l in range(LAYERS):
            out[k, l] = base[k, l] - factor[l] * (from_strip(whole[k], l) + rows(k, l))


def step_kernel(
    flags, base, strip, from_a, from_b, panels, maps, factor, cm, ch, cs, xf, ts,
    psi, acc, strip_out, to_a, to_b, ghost,
):
    advance(flags, base, strip, from_a, from_b, panels, maps, factor, psi)
    outer_terms(flags, psi, (cm, ch, cs, xf, ts), acc, strip_out, to_a, to_b, ghost)


def last_kernel(flags, base, strip, from_a, from_b, panels, maps, factor, out):
    advance(flags, base, strip, from_a, from_b, panels, maps, factor, out)


def f32(*shape):
    return jax.ShapeDtypeStruct(shape, jnp.float32)


STATE = (FIELDS, LAYERS, ROWS, LANES)
STRIP = (FIELDS, ROWS, LANES)
PANEL = (FIELDS, 8, LANES)
SCALAR = (LAYERS, ROWS, LANES)
FIRST = ((FIELDS, 24, LANES),) * 3
MAPS = (2, LANES, LANES)
GHOST = (FIELDS, LAYERS, 8, LANES)
TERMS = (f32(*STATE), f32(*STATE), f32(*STRIP), f32(*PANEL), f32(*PANEL))
FIXED = (f32(*SCALAR), f32(*SCALAR), f32(*STATE))
INNER = (
    f32(CELLS, *SCALAR),
    f32(FACES, *SCALAR),
    f32(12, LAYERS + 1, ROWS, LANES),
    f32(2, LAYERS + 2, ROWS, LANES),
)
SHARED = f32(2, *SCALAR)
OUTER = (
    f32(CELLS, LAYERS, 8, LANES),
    f32(CELLS, ROWS, LANES),
    f32(FACES, LAYERS, ROWS + 8, LANES),
    f32(FACES, ROWS, LANES),
)


def call(kernel, outs, args, work=(), name=None, in_place=None, away=(), copies=0):
    vmem = pl.BlockSpec(memory_space=pltpu.VMEM)
    smem = pl.BlockSpec(memory_space=pltpu.SMEM)
    there = pl.BlockSpec(memory_space=pltpu.HBM)
    return pl.pallas_call(
        kernel,
        out_shape=outs,
        in_specs=[smem] + [there if i in away else vmem for i in range(1, len(args))],
        out_specs=[vmem] * len(outs) if isinstance(outs, tuple) else vmem,
        scratch_shapes=([pltpu.SemaphoreType.DMA((copies,))] if copies else [])
        + [pltpu.VMEM(shape, jnp.float32) for shape in work],
        compiler_params=pltpu.CompilerParams(vmem_limit_bytes=32 * 1024 * 1024),
        input_output_aliases=in_place or {},
        name=name,
    )(*args)


def swaps(names, sectors, blocks, turn):
    half = blocks // 2
    assert half % 2 == 0
    where = {"sector": sectors, "block": blocks}
    minor = where[names[1]]

    def flat(b, s):
        first, second = (s, b) if names[0] == "sector" else (b, s)
        return first * minor + second

    sector_a, sector_b, block_a, near, far = [], [], [], [], []
    for b in range(blocks):
        for s in range(sectors):
            me = flat(b, s)
            sector_a.append((me, flat(b, s ^ 1)))
            sector_b.append((me, flat(b, (s + (1 if s % 2 else -1)) % sectors)))
            block_a.append((me, flat(b ^ 1, s)))
            if b == half - 1:
                near.append((me, flat(half, (s + turn) % sectors)))
                far.append((me, flat(half, (s + turn + 1) % sectors)))
            elif b == half:
                near.append((me, flat(half - 1, (s - turn) % sectors)))
                far.append((me, flat(half - 1, (s - turn - 1) % sectors)))
            else:
                other = b + 1 if b % 2 else b - 1
                near.append((me, flat(other, s) if 0 <= other < blocks else me))
                far.append((me, me))
    return sector_a, sector_b, block_a, near, far


def exchange(names, sectors, blocks, offset, strip, to_a, to_b, beside=None, args=()):
    def branch(shift):
        sector_a, sector_b, block_a, near, far = swaps(names, sectors, blocks, shift)

        def run(strip, to_a, to_b, *args):
            move = lambda x, pairs: lax.ppermute(x, names, pairs)
            moved = (
                move(strip, sector_a),
                move(strip, sector_b),
                move(to_a, block_a),
                move(to_b, near),
                move(to_b, far),
            )
            return tuple(beside(moved, *args))

        return run

    return tuple(
        lax.switch(offset, [branch(shift) for shift in range(sectors)], strip, to_a, to_b, *args)
    )


def first_beside(moved, *args):
    prepared = call(
        prepare_kernel,
        (f32(*MAPS), f32(*MAPS)) + FIXED + (f32(*STRIP), f32(*STATE)) + INNER + (SHARED,),
        args,
        (STATE, SCALAR),
        name="prepare",
        away=(1,),
        copies=2,
    )
    return (*moved, *prepared)


def next_beside(moved, *args):
    a, b, block, near, far = moved
    base = call(inner_kernel, f32(*STATE), args, (STATE,), name="inner", in_place={2: 0})
    return a, b, jnp.concatenate([near, far, block], axis=2), base


def shards(flow, adjoint, adjoint_later, objective_grad, volume, panel_maps, rotor_step, names):
    blocks = lax.axis_size("block")
    sectors = lax.axis_size("sector")
    place = lax.axis_index("block")
    half = blocks // 2
    stator = place >= half
    turn = rotor_step[0]
    offset = (turn // PHASES) % sectors
    flags = jnp.stack(
        [
            (lax.axis_index("sector") % 2 == 0).astype(jnp.int32),
            (place % 2 == 0).astype(jnp.int32),
            (place == 0).astype(jnp.int32),
            (place == blocks - 1).astype(jnp.int32),
            ((place == half) | (place == half - 1)).astype(jnp.int32),
            turn % PHASES,
            jnp.where(stator, 0, 2).astype(jnp.int32),
            jnp.where(stator, 2, 0).astype(jnp.int32),
        ]
    )
    send = partial(exchange, names, sectors, blocks, offset)
    packed = tuple(
        call(
            pack_kernel,
            tuple(f32(*shape) for shape in FIRST),
            (flags, flow, adjoint),
            name="pack",
        )
    )
    arrived = send(
        *packed,
        beside=first_beside,
        args=(
            flags,
            panel_maps,
            flow,
            adjoint,
            adjoint_later,
            objective_grad,
            volume,
        ),
    )
    (state_maps, maps, keep, factor, pushed, own, base), inner, shared = arrived[5:12], arrived[12:16], arrived[16]
    cm = inner[0]
    out = call(
        start_kernel,
        TERMS + OUTER,
        (flags, flow, adjoint) + arrived[:5] + (state_maps, maps, factor, own, base, cm, shared),
        (GHOST,),
        name="start",
    )
    terms, outer = tuple(out[:5]), tuple(out[5:])
    for sweep in range(1, ITERS):
        psi, acc, strip, to_a, to_b = terms
        arrived = send(
            strip, to_a, to_b, beside=next_beside, args=(flags, psi, acc, keep, factor, pushed) + inner
        )
        args = (flags, arrived[3], strip) + arrived[:3] + (maps, factor)
        if sweep == ITERS - 1:
            return call(last_kernel, f32(*STATE), args, name="last")
        terms = tuple(call(step_kernel, TERMS, args + (cm,) + outer, (GHOST,), name="step"))


def solution(mesh):
    placed = (
        P(None, None, "block", "sector"),
        P(None, None, "block", "sector"),
        P(None, None, None, "block", "sector"),
        P(None, None, "block", "sector"),
        P(None, "block", "sector"),
        P(),
        P(),
    )
    return jax.shard_map(
        partial(shards, names=tuple(mesh.axis_names)),
        mesh=mesh,
        in_specs=placed,
        out_specs=P(None, None, "block", "sector"),
        check_vma=False,
    )
```

```python
from functools import partial

import jax
import jax.numpy as jnp
from jax import lax
from jax.experimental import pallas as pl
from jax.experimental.pallas import tpu as pltpu
from jax.sharding import PartitionSpec as P

PHASES = 4
ITERS = 4
LANES = 128
ROWS = 16
LAYERS = 4
FIELDS = 5
SEG = LANES // LAYERS

gamma_gas = 1.4
second_coef = 0.5
fourth_coef = 1.0 / 32.0
courant = 0.6
physical_step = 2.0
sensor_floor = 0.0001
highest = lax.Precision.HIGHEST

S_EVEN, B_EVEN, INLET, OUTLET, PLANE, PHASE, STATE_MAPS, GRAD_MAPS = range(8)
U1, U2, U3, HT, BX, BT, BL, CR, CP = range(9)
CELLS = 9
A2, A4, DL, ES, N0, N1 = 0, 1, 2, 7, 12, 13
FACES = 14


def up_by(x, axis, k):
    n = x.shape[axis]
    return pltpu.roll(x, (-k) % n, axis=axis)


def iota(shape, axis):
    return lax.broadcasted_iota(jnp.int32, shape, axis)


def flagged(flags, which, shape):
    return jnp.broadcast_to(flags[which], shape) == 1


def primitives(u):
    inverse = 1.0 / u[0]
    vel = [u[1] * inverse, u[2] * inverse, u[3] * inverse]
    square = vel[0] * vel[0] + vel[1] * vel[1] + vel[2] * vel[2]
    p = (gamma_gas - 1.0) * (u[4] - 0.5 * u[0] * square)
    heat = gamma_gas * p * inverse
    slow = lax.rsqrt(heat)
    sound = heat * slow
    radius, slopes = [], []
    for q in vel:
        x = q * q + 0.01
        y = lax.rsqrt(x)
        radius.append(x * y + sound)
        slopes.append(q * y * inverse)
    half = 0.5 * inverse
    cells = vel + [(u[4] + p) * inverse] + slopes + [sound * half, gamma_gas * half * slow]
    return p, radius, sound, cells


def sensor_terms(below, here, above):
    bend = above - 2.0 * here + below
    total = above + 2.0 * here + below
    inside = bend * bend + sensor_floor
    slope = lax.rsqrt(inside)
    over = 1.0 / total
    nu = inside * slope * over
    a = bend * slope * over
    b = nu * over
    return nu, -2.0 * a - 2.0 * b, a - b


def face_terms(nu_left, nu_right, rad_left, rad_right, behind, left, right, ahead):
    e2 = (0.5 * second_coef) * (nu_left + nu_right)
    ratio = fourth_coef / (fourth_coef + e2)
    e4 = fourth_coef * ratio
    slope = ratio * ratio
    lam = 0.5 * (rad_left + rad_right)
    radial, sensed = [], []
    for b, l, r, a in zip(behind, left, right, ahead):
        first = r - l
        third = a - 3.0 * first - b
        radial.append(-0.5 * (e2 * first - e4 * third))
        sensed.append((-0.25) * lam * (first + slope * third))
    return [lam * e2, lam * e4] + radial + sensed


def rolled_faces(u, p, radius, axis):
    nu, n0, n1 = sensor_terms(up_by(p, axis, -1), p, up_by(p, axis, 1))
    right = [up_by(x, axis, 1) for x in u]
    behind = [up_by(x, axis, -1) for x in u]
    ahead = [up_by(x, axis, 2) for x in u]
    return face_terms(
        nu, up_by(nu, axis, 1), radius, up_by(radius, axis, 1), behind, u, right, ahead
    ) + [n0, n1]


def dot5(a, b):
    return (a[0] * b[0] + a[1] * b[1]) + (a[2] * b[2] + a[3] * b[3]) + a[4] * b[4]


def to_state(lin, s, rbar, nbar, cells, direction):
    q = cells[direction]
    kappa = s[1] * cells[U1] + s[2] * cells[U2] + s[3] * cells[U3] + s[4] * cells[HT]
    kappa = kappa + cells[BX + direction] * rbar
    sq = s[4] * q
    pbar = nbar + sq + s[direction + 1] + cells[CP] * rbar
    scaled = (gamma_gas - 1.0) * pbar
    g = [None] * FIELDS
    square = cells[U1] * cells[U1] + cells[U2] * cells[U2] + cells[U3] * cells[U3]
    g[0] = lin[0] - q * kappa - cells[CR] * rbar + 0.5 * square * scaled
    for k in range(3):
        g[k + 1] = lin[k + 1] + q * s[k + 1] - cells[k] * scaled
    g[direction + 1] = g[direction + 1] + (s[0] + kappa)
    g[4] = lin[4] + sq + scaled
    return g


def rolled_transpose(psi, faces, cells, direction, axis, mask=None):
    w = [x - up_by(x, axis, 1) for x in psi]
    if mask is not None:
        w = [jnp.where(mask, x, 0.0) for x in w]
    gl = dot5(w, [faces(DL + k) for k in range(FIELDS)])
    ge = dot5(w, [faces(ES + k) for k in range(FIELDS)])
    a2, a4 = faces(A2), faces(A4)
    lin, s = [], []
    for x in w:
        c = a4 * x
        v = c - up_by(c, axis, -1)
        z = a2 * x + (v - up_by(v, axis, 1))
        lin.append(z - up_by(z, axis, -1))
        s.append(0.5 * (x + up_by(x, axis, -1)))
    rbar = gl + up_by(gl, axis, -1)
    nu_bar = ge + up_by(ge, axis, -1)
    v = faces(N1) * nu_bar
    nbar = faces(N0) * nu_bar + up_by(v, axis, 1) + up_by(v, axis, -1)
    return to_state(lin, s, rbar, nbar, cells, direction)


def packed_rows(tiles):
    row = iota((8, LANES), 0)
    out = tiles[0]
    for l in range(1, LAYERS):
        out = jnp.where(row >= 2 * l, pltpu.roll(tiles[l], 2 * l, axis=0), out)
    return out


def packed_quads(tiles):
    row = iota((8, LANES), 0)
    pairs = [
        jnp.where(row < 4, tiles[l], pltpu.roll(tiles[l + 1], 4, axis=0)) for l in range(0, LAYERS, 2)
    ]
    return jnp.concatenate(pairs, axis=0)


def quad(packed, l, high):
    tile = packed[8 * (l // 2) : 8 * (l // 2) + 8]
    return pltpu.roll(tile, 4, axis=0) if (l % 2 == 1) != high else tile


def pair(packed, l, to):
    shift = (to - 2 * l) % 8
    return pltpu.roll(packed, shift, axis=0) if shift else packed


def packed_strip(layers):
    lane = iota((ROWS, LANES), 1)
    out = jnp.zeros((ROWS, LANES), jnp.float32)
    for l, x in enumerate(layers):
        base = SEG * l
        out = jnp.where((lane >= base) & (lane < base + 8), pltpu.roll(x, (base + 8) % LANES, axis=1), out)
        out = jnp.where(
            (lane >= base + 24) & (lane < base + 32), pltpu.roll(x, (base + 24) % LANES, axis=1), out
        )
    return out


def packed_edges(layers, others):
    lane = iota((ROWS, LANES), 1)
    out = packed_strip(layers)
    for l, x in enumerate(others):
        base = SEG * l + 16
        out = jnp.where((lane >= base - 8) & (lane < base + 8), pltpu.roll(x, base, axis=1), out)
    return out


def from_strip(strip, l):
    lane = iota((ROWS, LANES), 1)
    base = SEG * l
    low = pltpu.roll(strip, (-(base + 24)) % LANES, axis=1)
    high = pltpu.roll(strip, (-(base + 8)) % LANES, axis=1)
    return jnp.where(lane < 8, low, jnp.where(lane >= LANES - 8, high, 0.0))


def place_in_segment():
    return jnp.bitwise_and(iota((ROWS, LANES), 1), SEG - 1)


def each(count, looped):
    def run(body):
        if looped:
            lax.fori_loop(0, count, lambda i, c: (body(i), c)[1], 0)
        else:
            for i in range(count):
                body(i)

    return run


def half_rows(half):
    return slice(8 * half, 8 * half + 8) if isinstance(half, int) else pl.ds(pl.multiple_of(8 * half, 8), 8)


def clamp(j):
    return min(max(j, 0), LAYERS - 1)


def pack_kernel(flags, flow, psi, to_t, to_a, to_b):
    even = flagged(flags, B_EVEN, (8, LANES))
    even2 = flagged(flags, B_EVEN, (16, LANES))
    for k in range(FIELDS):
        to_t[k, 0:16] = packed_edges([flow[k, l] for l in range(LAYERS)], [psi[k, l] for l in range(LAYERS)])
        low = packed_rows([flow[k, l, 0:8] for l in range(LAYERS)])
        high = packed_rows([pltpu.roll(flow[k, l, 8:16], 2, axis=0) for l in range(LAYERS)])
        to_t[k, 16:24] = jnp.where(even, low, high)
        low = packed_quads([flow[k, l, 0:8] for l in range(LAYERS)])
        high = packed_quads([pltpu.roll(flow[k, l, 8:16], 4, axis=0) for l in range(LAYERS)])
        to_a[k, 0:16] = jnp.where(even2, high, low)
        to_b[k, 0:16] = jnp.where(even2, low, high)
        low = packed_rows([psi[k, l, 0:8] for l in range(LAYERS)])
        high = packed_rows([pltpu.roll(psi[k, l, 8:16], 2, axis=0) for l in range(LAYERS)])
        to_a[k, 16:24] = jnp.where(even, high, low)
        to_b[k, 16:24] = jnp.where(even, low, high)


def mapped(near, far, maps):
    shape = near.shape
    dims = (((1,), (1,)), ((), ()))
    near = near.reshape(shape[0] * shape[1], LANES)
    far = far.reshape(shape[0] * shape[1], LANES)
    out = lax.dot_general(near, maps[0], dims, precision=highest, preferred_element_type=jnp.float32)
    out = out + lax.dot_general(far, maps[1], dims, precision=highest, preferred_element_type=jnp.float32)
    return out.reshape(shape)


def mapped_back(near, far, maps):
    shape = near.shape
    both = jnp.concatenate([near, far], axis=2).reshape(shape[0] * shape[1], 2 * LANES)
    table = maps[...].reshape(2 * LANES, LANES)
    out = jnp.dot(both, table, precision=highest, preferred_element_type=jnp.float32)
    return out.reshape(shape)


def left_and_right(flags, a, b):
    even = flagged(flags, S_EVEN, a.shape)
    return jnp.where(even, b, a), jnp.where(even, a, b)


def three(panels):
    return [panels.at[:, :, pl.ds(LANES * i, LANES)] for i in range(3)]


def widened(flags, own, a, b):
    sub = place_in_segment()
    left, right = left_and_right(flags, a, b)
    x = jnp.where((sub >= 8) & (sub < 16), pltpu.roll(right, LANES - 16, axis=1), own)
    return jnp.where((sub >= 16) & (sub < 24), pltpu.roll(left, 16, axis=1), x)


def widened_other(flags, own, a, b):
    sub = place_in_segment()
    left, right = left_and_right(flags, a, b)
    low = pltpu.roll(jnp.where((sub >= 16) & (sub < 24), right, own), LANES - 8, axis=1)
    high = pltpu.roll(jnp.where((sub >= 8) & (sub < 16), left, own), 8, axis=1)
    return jnp.where(sub < 16, low, high)


def inner_coefficients(flow, cm, tf, lf, ln, shared, radii, at_cell):
    @each(LAYERS, True)
    def _(l):
        u = [flow[k, l] for k in range(FIELDS)]
        p, radius, _, cells = primitives(u)
        for i, x in enumerate(cells):
            cm[i, l] = x
        shared[0, l] = p
        shared[1, l] = radius[0]
        radii[l] = radius[2]
        at_cell(l, radius[0] + radius[1] + radius[2])
        for i, x in enumerate(rolled_faces(u, p, radius[1], 1)):
            tf[i, l] = x

    @each(2, True)
    def _(half):
        rows = half_rows(half)
        cell = [[flow[k, l, rows] for k in range(FIELDS)] for l in range(LAYERS)]
        pressure = [shared[0, l, rows] for l in range(LAYERS)]
        radius = [radii[l, rows] for l in range(LAYERS)]
        nus = {}
        for j in range(-1, LAYERS + 1):
            nu, n0, n1 = sensor_terms(*[pressure[clamp(j + d)] for d in (-1, 0, 1)])
            nus[j] = nu
            ln[0, j + 1, rows] = n0
            ln[1, j + 1, rows] = n1
        for f in range(-1, LAYERS):
            terms = face_terms(
                nus[f],
                nus[f + 1],
                radius[clamp(f)],
                radius[clamp(f + 1)],
                *[cell[clamp(f + d)] for d in (-1, 0, 1, 2)],
            )
            for i, x in enumerate(terms):
                lf[i, f + 1, rows] = x


def outer_coefficients(flags, flow, own, from_a, from_b, zone_a, near, far, maps, shared, ch, cs, xf, ts):
    through = mapped(near[:, 0:16], far[:, 0:16], maps)
    even = flagged(flags, B_EVEN, (16, LANES))
    plane = flagged(flags, PLANE, (16, LANES))
    row = iota((8, LANES), 0)
    inlet = flagged(flags, INLET, (8, LANES))
    outlet = flagged(flags, OUTLET, (8, LANES))
    lower, upper = [], []
    for k in range(FIELDS):
        b = jnp.where(plane, through[k], near[k, 0:16])
        a = zone_a[k, 0:16]
        lower.append(jnp.where(even, b, a))
        upper.append(jnp.where(even, a, b))
    for l in range(LAYERS):
        u, halo = [], []
        for k in range(FIELDS):
            main = flow[k, l]
            up = jnp.where(outlet, jnp.broadcast_to(main[15:16], (8, LANES)), quad(upper[k], l, False))
            low = jnp.where(inlet, jnp.broadcast_to(main[0:1], (8, LANES)), quad(lower[k], l, True))
            halo.append(jnp.where(row < 4, up, low))
            u.append(jnp.concatenate([main, halo[k]], axis=0))
        p, radius, _, cells = primitives(halo)
        for i, x in enumerate(cells):
            ch[i, l] = x
        p = jnp.concatenate([shared[0, l], p], axis=0)
        radius = jnp.concatenate([shared[1, l], radius[0]], axis=0)
        for i, x in enumerate(rolled_faces(u, p, radius, 0)):
            xf[i, l] = x
    u = [widened(flags, own[k], from_a[k, 0:16], from_b[k, 0:16]) for k in range(FIELDS)]
    p, radius, _, cells = primitives(u)
    for i, x in enumerate(cells):
        cs[i] = x
    for i, x in enumerate(rolled_faces(u, p, radius[1], 1)):
        ts[i] = x


def x_terms(flags, psi, halo, coefs, acc, ghost):
    cm, ch, _, xf, _ = coefs
    row = iota((8, LANES), 0)
    inlet = flagged(flags, INLET, (8, LANES)) & (row == 0)
    outlet = flagged(flags, OUTLET, (8, LANES)) & (row == 7)
    for l in range(LAYERS):
        wide = [jnp.concatenate([psi[k, l], halo(k, l)], axis=0) for k in range(FIELDS)]
        cells = [jnp.concatenate([cm[i, l], ch[i, l]], axis=0) for i in range(CELLS)]
        g = rolled_transpose(wide, lambda i: xf[i, l], cells, 0, 0)
        for k in range(FIELDS):
            out = g[k][16:]
            if ghost is not None:
                ghost[k, l] = out
            first = pltpu.roll(out, 2, axis=0) + pltpu.roll(out, 1, axis=0)
            last = pltpu.roll(out, 7, axis=0) + pltpu.roll(out, 6, axis=0)
            acc[k, l, 0:8] = g[k][0:8] + jnp.where(inlet, first, 0.0)
            acc[k, l, 8:16] = g[k][8:16] + jnp.where(outlet, last, 0.0)


def strip_terms(values, edges, coefs, strip):
    _, _, cs, _, ts = coefs
    g = rolled_transpose(values, lambda i: ts[i], [cs[i] for i in range(CELLS)], 1, 1, edges)
    for k in range(FIELDS):
        strip[k] = g[k]


def t_terms(psi, cm, tf, acc, looped):
    lane = iota((ROWS, LANES), 1)
    inner = (lane >= 1) & (lane < LANES - 2)

    @each(LAYERS, looped)
    def _(l):
        g = rolled_transpose(
            [psi[k, l] for k in range(FIELDS)],
            lambda i: tf[i, l],
            [cm[i, l] for i in range(CELLS)],
            1,
            1,
            inner,
        )
        for k in range(FIELDS):
            acc[k, l] = g[k]


def l_terms(psi, cm, lf, ln, acc, looped):
    last = LAYERS - 1

    @each(2, looped)
    def _(half):
        rows = half_rows(half)
        value = [[psi[k, l, rows] for k in range(FIELDS)] for l in range(LAYERS)]
        w, c, gl, ge = {}, {}, {}, {}
        for f in range(-1, LAYERS):
            if f < 0:
                w[f] = [-x for x in value[0]]
            elif f == last:
                w[f] = value[last]
            else:
                w[f] = [x - y for x, y in zip(value[f], value[f + 1])]
            gl[f] = dot5(w[f], [lf[DL + k, f + 1, rows] for k in range(FIELDS)])
            ge[f] = dot5(w[f], [lf[ES + k, f + 1, rows] for k in range(FIELDS)])
            a4 = lf[A4, f + 1, rows]
            c[f] = [a4 * x for x in w[f]]
        z = {}
        for f in range(last):
            a2 = lf[A2, f + 1, rows]
            z[f] = [a2 * w[f][k] + 2.0 * c[f][k] - c[f + 1][k] - c[f - 1][k] for k in range(FIELDS)]
        nbar = [None] * LAYERS
        for j in range(-1, LAYERS + 1):
            nu_bar = ge.get(j, 0.0) + ge.get(j - 1, 0.0)
            here = ln[0, j + 1, rows] * nu_bar
            side = ln[1, j + 1, rows] * nu_bar
            for to, x in ((j, here), (j - 1, side), (j + 1, side)):
                to = clamp(to)
                nbar[to] = x if nbar[to] is None else nbar[to] + x
        for j in range(LAYERS):
            if j == 0:
                s = [0.5 * w[0][k] + w[-1][k] for k in range(FIELDS)]
                lin = z[0]
                rbar = gl[0] + 2.0 * gl[-1]
            elif j == last:
                s = [0.5 * w[last - 1][k] + w[last][k] for k in range(FIELDS)]
                lin = [-x for x in z[last - 1]]
                rbar = gl[last - 1] + 2.0 * gl[last]
            else:
                s = [0.5 * (w[j][k] + w[j - 1][k]) for k in range(FIELDS)]
                lin = [z[j][k] - z[j - 1][k] for k in range(FIELDS)]
                rbar = gl[j] + gl[j - 1]
            g = to_state(lin, s, rbar, nbar[j], [cm[i, j, rows] for i in range(CELLS)], 2)
            for k in range(FIELDS):
                acc[k, j, rows] = acc[k, j, rows] + g[k]


def outer_terms(flags, psi, coefs, acc, strip, to_a, to_b, ghost):
    even = flagged(flags, B_EVEN, (8, LANES))
    empty = jnp.zeros((8, LANES), jnp.float32)
    x_terms(flags, psi, lambda k, l: empty, coefs, acc, ghost)
    for k in range(FIELDS):
        high = packed_rows([ghost[k, l] for l in range(LAYERS)])
        low = packed_rows([pltpu.roll(ghost[k, l], 2, axis=0) for l in range(LAYERS)])
        to_a[k] = jnp.where(even, high, low)
        to_b[k] = jnp.where(even, low, high)
    sub = place_in_segment()
    edges = ((sub >= 6) & (sub < 8)) | ((sub >= 23) & (sub < 25))
    values = [packed_strip([psi[k, l] for l in range(LAYERS)]) for k in range(FIELDS)]
    strip_terms(values, edges, coefs, strip)


def settle(psi, outer, inner, keep, factor, pushed, base, looped):
    @each(LAYERS, looped)
    def _(l):
        for k in range(FIELDS):
            total = inner[k, l] if outer is None else outer[k, l] + inner[k, l]
            base[k, l] = psi[k, l] * keep[l] - factor[l] * total + pushed[k, l]


def arrived_rows(flags, lower, upper):
    row = iota((8, LANES), 0)
    first = (row < 2) & jnp.logical_not(flagged(flags, INLET, (8, LANES)))
    last = (row >= 6) & jnp.logical_not(flagged(flags, OUTLET, (8, LANES)))

    def rows(k, l):
        low = jnp.where(first, pair(lower[k], l, 0), 0.0)
        high = jnp.where(last, pair(upper[k], l, 6), 0.0)
        return jnp.concatenate([low, high], axis=0)

    return rows


def facing_gradients(flags, flow, from_a, from_b, near, far, maps):
    rotor = jnp.logical_not(flagged(flags, B_EVEN, (8, LANES)))
    row = iota((8, LANES), 0)
    panel = []
    for k in range(FIELDS):
        low = packed_rows([flow[k, l, 0:8] for l in range(LAYERS)])
        high = packed_rows([pltpu.roll(flow[k, l, 8:16], 2, axis=0) for l in range(LAYERS)])
        panel.append(jnp.where(rotor, high, low))
    panel = jnp.stack(panel)
    first, second = [], []
    for k in range(FIELDS):
        left, right = left_and_right(flags, from_a[k, 16:24], from_b[k, 16:24])
        first.append(jnp.where(rotor, left, right))
        second.append(jnp.where(rotor, right, left))
    ghosts = (
        mapped(panel, jnp.stack(first), maps),
        mapped(jnp.stack(second), panel, maps),
    )
    kept = (row == 7) | (rotor & (row == 0)) | (jnp.logical_not(rotor) & (row == 6))
    out = []
    for ghost, facing in zip(ghosts, (near, far)):
        layers = []
        for l in range(LAYERS):
            u, psi = [], []
            for k in range(FIELDS):
                cells = facing[k, 0:16]
                below = pair(ghost[k], l, 6)
                above = pair(ghost[k], l, 0)
                as_rotor = jnp.where(
                    row < 4,
                    quad(cells, l, False),
                    jnp.where(row < 6, pltpu.roll(below, 6, axis=0), below),
                )
                as_stator = jnp.where(
                    row < 2,
                    above,
                    jnp.where(row < 4, pltpu.roll(above, 2, axis=0), quad(cells, l, True)),
                )
                u.append(jnp.where(rotor, as_rotor, as_stator))
                value = facing[k, 16:24]
                psi.append(
                    jnp.where(
                        rotor,
                        jnp.where(row < 2, pair(value, l, 0), 0.0),
                        jnp.where(row >= 6, pair(value, l, 6), 0.0),
                    )
                )
            p, radius, _, cells = primitives(u)
            faces = rolled_faces(u, p, radius[0], 0)
            g = rolled_transpose(psi, lambda i: faces[i], cells, 0, 0, kept)
            layers.append([jnp.where(rotor, pltpu.roll(x, 2, axis=0), x) for x in g])
        out.append(jnp.stack([packed_rows([layers[l][k] for l in range(LAYERS)]) for k in range(FIELDS)]))
    return out


def prepare_kernel(
    flags, panel_maps, flow, adjoint, later, gradient, volume,
    state_maps, grad_maps, keep, factor, pushed, own, base, cm, tf, lf, ln, shared, sems, acc, radii,
):
    of_phase = panel_maps.at[flags[PHASE]]
    copies = [
        pltpu.make_async_copy(of_phase.at[pl.ds(flags[which], 2)], to, sems.at[i])
        for i, (which, to) in enumerate(((STATE_MAPS, state_maps), (GRAD_MAPS, grad_maps)))
    ]
    for copy in copies:
        copy.start()

    def at_cell(l, radius_sum):
        vol = volume[l]
        f = courant / (radius_sum + (1.5 * courant / physical_step) * vol)
        factor[l] = f
        keep[l] = 1.0 - f * ((1.5 / physical_step) * vol)
        for k in range(FIELDS):
            source = gradient[k, l] + vol * (2.0 * later[0, k, l] - 0.5 * later[1, k, l]) / physical_step
            pushed[k, l] = f * source

    inner_coefficients(flow, cm, tf, lf, ln, shared, radii, at_cell)

    @each(FIELDS, True)
    def _(k):
        own[k] = packed_edges([flow[k, l] for l in range(LAYERS)], [adjoint[k, l] for l in range(LAYERS)])

    t_terms(adjoint, cm, tf, acc, True)
    l_terms(adjoint, cm, lf, ln, acc, True)
    settle(adjoint, None, acc, keep, factor, pushed, base, True)
    for copy in copies:
        copy.wait()


def start_kernel(
    flags, flow, adjoint, from_a, from_b, zone_a, near, far, state_maps, grad_maps, factor, own, base, cm, shared,
    psi, acc, strip, to_a, to_b, ch, cs, xf, ts, ghost,
):
    coefs = (cm, ch, cs, xf, ts)
    outer_coefficients(flags, flow, own, from_a, from_b, zone_a, near, far, state_maps, shared, ch, cs, xf, ts)
    even = flagged(flags, B_EVEN, (8, LANES))
    plane = flagged(flags, PLANE, (8, LANES))
    row = iota((8, LANES), 0)
    use_upper = (row < 2) & jnp.logical_not(flagged(flags, OUTLET, (8, LANES)))
    use_lower = (row >= 6) & jnp.logical_not(flagged(flags, INLET, (8, LANES)))

    def halo(k, l):
        a = zone_a[k, 16:24]
        b = jnp.where(plane, 0.0, near[k, 16:24])
        upper = pair(jnp.where(even, a, b), l, 0)
        lower = pair(jnp.where(even, b, a), l, 6)
        return jnp.where(use_upper, upper, jnp.where(use_lower, lower, 0.0))

    x_terms(flags, adjoint, halo, coefs, acc, None)
    sub = place_in_segment()
    edges = ((sub >= 6) & (sub < 9)) | ((sub >= 22) & (sub < 25))
    values = [widened_other(flags, own[k], from_a[k, 0:16], from_b[k, 0:16]) for k in range(FIELDS)]
    strip_terms(values, edges, coefs, strip)
    panels = facing_gradients(flags, flow, from_a, from_b, near, far, grad_maps)
    through = mapped_back(panels[0], panels[1], grad_maps)
    lower, upper = [], []
    for k in range(FIELDS):
        b = jnp.where(plane, through[k], 0.0)
        lower.append(jnp.where(even, b, 0.0))
        upper.append(jnp.where(even, 0.0, b))
    rows = arrived_rows(flags, lower, upper)
    for k in range(FIELDS):
        for l in range(LAYERS):
            total = acc[k, l] + from_strip(strip[k], l) + rows(k, l)
            psi[k, l] = base[k, l] - factor[l] * total
    outer_terms(flags, psi, coefs, acc, strip, to_a, to_b, ghost)


def inner_kernel(flags, psi, outer, keep, factor, pushed, cm, tf, lf, ln, base, acc):
    t_terms(psi, cm, tf, acc, False)
    l_terms(psi, cm, lf, ln, acc, False)
    settle(psi, outer, acc, keep, factor, pushed, base, False)


def advance(flags, base, strip, from_a, from_b, panels, maps, factor, out):
    zone_a, far, near = three(panels)
    through = mapped_back(near[...], far[...], maps)
    even = flagged(flags, B_EVEN, (8, LANES))
    plane = flagged(flags, PLANE, (8, LANES))
    sub = place_in_segment()
    whole, lower, upper = [], [], []
    for k in range(FIELDS):
        left, right = left_and_right(flags, from_a[k], from_b[k])
        right = jnp.where(sub < 8, pltpu.roll(right, LANES - 16, axis=1), 0.0)
        whole.append(strip[k] + jnp.where(sub >= 24, pltpu.roll(left, 16, axis=1), right))
        b = jnp.where(plane, through[k], near[k])
        a = zone_a[k]
        lower.append(jnp.where(even, b, a))
        upper.append(jnp.where(even, a, b))
    rows = arrived_rows(flags, lower, upper)
    for k in range(FIELDS):
        for l in range(LAYERS):
            out[k, l] = base[k, l] - factor[l] * (from_strip(whole[k], l) + rows(k, l))


def step_kernel(
    flags, base, strip, from_a, from_b, panels, maps, factor, cm, ch, cs, xf, ts,
    psi, acc, strip_out, to_a, to_b, ghost,
):
    advance(flags, base, strip, from_a, from_b, panels, maps, factor, psi)
    outer_terms(flags, psi, (cm, ch, cs, xf, ts), acc, strip_out, to_a, to_b, ghost)


def last_kernel(flags, base, strip, from_a, from_b, panels, maps, factor, out):
    advance(flags, base, strip, from_a, from_b, panels, maps, factor, out)


def f32(*shape):
    return jax.ShapeDtypeStruct(shape, jnp.float32)


STATE = (FIELDS, LAYERS, ROWS, LANES)
STRIP = (FIELDS, ROWS, LANES)
PANEL = (FIELDS, 8, LANES)
SCALAR = (LAYERS, ROWS, LANES)
FIRST = ((FIELDS, 24, LANES),) * 3
MAPS = (2, LANES, LANES)
GHOST = (FIELDS, LAYERS, 8, LANES)
TERMS = (f32(*STATE), f32(*STATE), f32(*STRIP), f32(*PANEL), f32(*PANEL))
FIXED = (f32(*SCALAR), f32(*SCALAR), f32(*STATE))
INNER = (
    f32(CELLS, *SCALAR),
    f32(FACES, *SCALAR),
    f32(12, LAYERS + 1, ROWS, LANES),
    f32(2, LAYERS + 2, ROWS, LANES),
)
SHARED = f32(2, *SCALAR)
OUTER = (
    f32(CELLS, LAYERS, 8, LANES),
    f32(CELLS, ROWS, LANES),
    f32(FACES, LAYERS, ROWS + 8, LANES),
    f32(FACES, ROWS, LANES),
)


def call(kernel, outs, args, work=(), name=None, in_place=None, away=(), copies=0):
    vmem = pl.BlockSpec(memory_space=pltpu.VMEM)
    smem = pl.BlockSpec(memory_space=pltpu.SMEM)
    there = pl.BlockSpec(memory_space=pltpu.HBM)
    return pl.pallas_call(
        kernel,
        out_shape=outs,
        in_specs=[smem] + [there if i in away else vmem for i in range(1, len(args))],
        out_specs=[vmem] * len(outs) if isinstance(outs, tuple) else vmem,
        scratch_shapes=([pltpu.SemaphoreType.DMA((copies,))] if copies else [])
        + [pltpu.VMEM(shape, jnp.float32) for shape in work],
        compiler_params=pltpu.CompilerParams(vmem_limit_bytes=32 * 1024 * 1024),
        input_output_aliases=in_place or {},
        name=name,
    )(*args)


def swaps(names, sectors, blocks, turn):
    half = blocks // 2
    assert half % 2 == 0
    where = {"sector": sectors, "block": blocks}
    minor = where[names[1]]

    def flat(b, s):
        first, second = (s, b) if names[0] == "sector" else (b, s)
        return first * minor + second

    sector_a, sector_b, block_a, near, far = [], [], [], [], []
    for b in range(blocks):
        for s in range(sectors):
            me = flat(b, s)
            sector_a.append((me, flat(b, s ^ 1)))
            sector_b.append((me, flat(b, (s + (1 if s % 2 else -1)) % sectors)))
            block_a.append((me, flat(b ^ 1, s)))
            if b == half - 1:
                near.append((me, flat(half, (s + turn) % sectors)))
                far.append((me, flat(half, (s + turn + 1) % sectors)))
            elif b == half:
                near.append((me, flat(half - 1, (s - turn) % sectors)))
                far.append((me, flat(half - 1, (s - turn - 1) % sectors)))
            else:
                other = b + 1 if b % 2 else b - 1
                near.append((me, flat(other, s) if 0 <= other < blocks else me))
                far.append((me, me))
    return sector_a, sector_b, block_a, near, far


def exchange(names, sectors, blocks, offset, strip, to_a, to_b, beside=None, args=()):
    def branch(shift):
        sector_a, sector_b, block_a, near, far = swaps(names, sectors, blocks, shift)

        def run(strip, to_a, to_b, *args):
            move = lambda x, pairs: lax.ppermute(x, names, pairs)
            moved = (
                move(strip, sector_a),
                move(strip, sector_b),
                move(to_a, block_a),
                move(to_b, near),
                move(to_b, far),
            )
            return tuple(beside(moved, *args))

        return run

    return tuple(
        lax.switch(offset, [branch(shift) for shift in range(sectors)], strip, to_a, to_b, *args)
    )


def first_beside(moved, *args):
    prepared = call(
        prepare_kernel,
        (f32(*MAPS), f32(*MAPS)) + FIXED + (f32(*STRIP), f32(*STATE)) + INNER + (SHARED,),
        args,
        (STATE, SCALAR),
        name="prepare",
        away=(1,),
        copies=2,
    )
    return (*moved, *prepared)


def next_beside(moved, *args):
    a, b, block, near, far = moved
    base = call(inner_kernel, f32(*STATE), args, (STATE,), name="inner", in_place={2: 0})
    return a, b, jnp.concatenate([block, far, near], axis=2), base


def shards(flow, adjoint, adjoint_later, objective_grad, volume, panel_maps, rotor_step, names):
    blocks = lax.axis_size("block")
    sectors = lax.axis_size("sector")
    place = lax.axis_index("block")
    half = blocks // 2
    stator = place >= half
    turn = rotor_step[0]
    offset = (turn // PHASES) % sectors
    flags = jnp.stack(
        [
            (lax.axis_index("sector") % 2 == 0).astype(jnp.int32),
            (place % 2 == 0).astype(jnp.int32),
            (place == 0).astype(jnp.int32),
            (place == blocks - 1).astype(jnp.int32),
            ((place == half) | (place == half - 1)).astype(jnp.int32),
            turn % PHASES,
            jnp.where(stator, 0, 2).astype(jnp.int32),
            jnp.where(stator, 2, 0).astype(jnp.int32),
        ]
    )
    send = partial(exchange, names, sectors, blocks, offset)
    packed = tuple(
        call(
            pack_kernel,
            tuple(f32(*shape) for shape in FIRST),
            (flags, flow, adjoint),
            name="pack",
        )
    )
    arrived = send(
        *packed,
        beside=first_beside,
        args=(
            flags,
            panel_maps,
            flow,
            adjoint,
            adjoint_later,
            objective_grad,
            volume,
        ),
    )
    (state_maps, maps, keep, factor, pushed, own, base), inner, shared = arrived[5:12], arrived[12:16], arrived[16]
    cm = inner[0]
    out = call(
        start_kernel,
        TERMS + OUTER,
        (flags, flow, adjoint) + arrived[:5] + (state_maps, maps, factor, own, base, cm, shared),
        (GHOST,),
        name="start",
    )
    terms, outer = tuple(out[:5]), tuple(out[5:])
    for sweep in range(1, ITERS):
        psi, acc, strip, to_a, to_b = terms
        arrived = send(
            strip, to_a, to_b, beside=next_beside, args=(flags, psi, acc, keep, factor, pushed) + inner
        )
        args = (flags, arrived[3], strip) + arrived[:3] + (maps, factor)
        if sweep == ITERS - 1:
            return call(last_kernel, f32(*STATE), args, name="last")
        terms = tuple(call(step_kernel, TERMS, args + (cm,) + outer, (GHOST,), name="step"))


def solution(mesh):
    placed = (
        P(None, None, "block", "sector"),
        P(None, None, "block", "sector"),
        P(None, None, None, "block", "sector"),
        P(None, None, "block", "sector"),
        P(None, "block", "sector"),
        P(),
        P(),
    )
    return jax.shard_map(
        partial(shards, names=tuple(mesh.axis_names)),
        mesh=mesh,
        in_specs=placed,
        out_specs=P(None, None, "block", "sector"),
        check_vma=False,
    )
```
